32 devices in a mesh: fsdp: 4 (over y, x), dp: 8 (over z, core).
Axes of the slice: x: 2, y: 2, z: 4, core: 2. Of those that a mesh axis runs over, the one named last changes fastest.
Arguments:
- tokens: bfloat16 [32768, 768], P(('fsdp', 'dp')), may hold values from -7.5 to 7.5
- cotangent: bfloat16 [64, 204, 768], P(('fsdp', 'dp')), may hold values from -6 to 6
- positions: int32 [64, 204], P(('fsdp', 'dp')), may hold values from 0 to 511, as said below
- counts: int32 [64], P(('fsdp', 'dp')), may hold values from 10 to 204, as said below
- qkv_weight: float32 [768, 2304], P('dp', 'fsdp'), may hold values from -0.21875 to 0.21875
- qkv_moment: float32 [768, 2304], P('dp', 'fsdp'), may hold values from -0.00024414062 to 0.00024414062
- qkv_second: float32 [768, 2304], P('dp', 'fsdp'), may hold values from 1.3852441e-10 to 5.5409766e-10
- out_weight: float32 [768, 768], P('dp', 'fsdp'), may hold values from -2.5 to 2.5
- out_moment: float32 [768, 768], P('dp', 'fsdp'), may hold values from -0.00024414062 to 0.00024414062
- out_second: float32 [768, 768], P('dp', 'fsdp'), may hold values from 1.3852442e-11 to 5.5409767e-11
- up_weight: float32 [768, 3072], P('dp', 'fsdp'), may hold values from -0.21875 to 0.21875
- up_moment: float32 [768, 3072], P('dp', 'fsdp'), may hold values from -0.00024414062 to 0.00024414062
- up_second: float32 [768, 3072], P('dp', 'fsdp'), may hold values from 1.3852441e-10 to 5.5409766e-10
- down_projection_weight: float32 [3072, 768], P('dp', 'fsdp'), may hold values from -0.15625 to 0.15625
- down_moment: float32 [3072, 768], P('dp', 'fsdp'), may hold values from -0.00024414062 to 0.00024414062
- down_second: float32 [3072, 768], P('dp', 'fsdp'), may hold values from 1.3852441e-10 to 5.5409766e-10
- proj_weight: float32 [256, 512], P('fsdp', 'dp'), may hold values from -0.25 to 0.25
- proj_moment: float32 [256, 512], P('fsdp', 'dp'), may hold values from -0.00024414062 to 0.00024414062
- proj_second: float32 [256, 512], P('fsdp', 'dp'), may hold values from 1.3852441e-10 to 5.5409766e-10
- vec_weight: float32 [9984], P(('fsdp', 'dp')), may hold values from -0.8 to 4
- vec_moment: float32 [9984], P(('fsdp', 'dp')), may hold values from -0.0007324219 to 0.0007324219
- vec_second: float32 [9984], P(('fsdp', 'dp')), may hold values from 1.2467197e-09 to 4.986879e-09
Outputs:
- output: bfloat16 [32768, 768], P(('fsdp', 'dp'))
- grad_input: bfloat16 [32768, 768], P(('fsdp', 'dp'))
- grad_norm: float32 [], replicated
- qkv_next: float32 [768, 2304], P('dp', 'fsdp')
- qkv_moment_next: float32 [768, 2304], P('dp', 'fsdp')
- qkv_second_next: float32 [768, 2304], P('dp', 'fsdp')
- qkv_copy: bfloat16 [768, 2304], P('dp', 'fsdp')
- out_next: float32 [768, 768], P('dp', 'fsdp')
- out_moment_next: float32 [768, 768], P('dp', 'fsdp')
- out_second_next: float32 [768, 768], P('dp', 'fsdp')
- out_copy: bfloat16 [768, 768], P('dp', 'fsdp')
- up_next: float32 [768, 3072], P('dp', 'fsdp')
- up_moment_next: float32 [768, 3072], P('dp', 'fsdp')
- up_second_next: float32 [768, 3072], P('dp', 'fsdp')
- up_copy: bfloat16 [768, 3072], P('dp', 'fsdp')
- down_next: float32 [3072, 768], P('dp', 'fsdp')
- down_moment_next: float32 [3072, 768], P('dp', 'fsdp')
- down_second_next: float32 [3072, 768], P('dp', 'fsdp')
- down_copy: bfloat16 [3072, 768], P('dp', 'fsdp')
- proj_next: float32 [256, 512], P('fsdp', 'dp')
- proj_moment_next: float32 [256, 512], P('fsdp', 'dp')
- proj_second_next: float32 [256, 512], P('fsdp', 'dp')
- proj_copy: bfloat16 [256, 512], P('fsdp', 'dp')
- vec_next: float32 [9984], P(('fsdp', 'dp'))
- vec_moment_next: float32 [9984], P(('fsdp', 'dp'))
- vec_second_next: float32 [9984], P(('fsdp', 'dp'))
- vec_copy: bfloat16 [9984], P(('fsdp', 'dp'))
The draws below stay inside these ranges and needn't reach their ends.
Inputs may be any that keep to these rules, and one draw needn't show every extreme that they name: `positions`: positions of one sequence are all different. `counts`: slot j of a sequence is masked exactly when j < its count; some sequence has exactly 204 in every draw.
All inputs are finite; a program needn't handle non-finite values.
Results may differ from the reference program's by a relative error of at most 0.018.
Values may be sent and summed in bfloat16 or wider, within the bound.
No kernel may reach another device: no remote copies, remote signals or barrier semaphores. Data moves between devices by JAX's collectives and lax.ppermute only.
A program may use at most 192 MiB of HBM per device.

```python
import math
import jax
import jax.numpy as jnp
from jax import lax

D = 768
HEADS = 12
FF = 3072
KP = 256
SEQLEN = 512
STEP = 10
HEAD_DIM = 64
SEQS = 64
TOTAL_TOKENS = 32768
MAXM = 204
MINM = 10
NVEC = 9984
PARAMS = 7218944


def mask_layout(key):
    perm_key, count_key, selection_key = jax.random.split(key, 3)
    seq_keys = jax.random.split(perm_key, SEQS)
    orders = jax.vmap(lambda subkey: jax.random.permutation(subkey, SEQLEN))(seq_keys)
    chosen = orders[:, :MAXM].astype(jnp.int32)
    spread = jax.random.randint(count_key, (2, SEQS), 0, MAXM - MINM + 1)
    totals = MINM + jnp.min(spread, axis=0)
    picked = jax.random.randint(selection_key, (), 0, SEQS)
    totals = jnp.where(jnp.arange(SEQS) == picked, MAXM, totals).astype(jnp.int32)
    return (chosen, totals)


def draw_positions(key, part):
    layout = mask_layout(key)
    return layout[0]


def draw_counts(key, part):
    layout = mask_layout(key)
    return layout[1]


def scaled_rows(key, start):
    ramp = jnp.arange(D, dtype=jnp.float32) / (D - 1)
    values = jnp.clip(jax.random.normal(key, (TOTAL_TOKENS, D), jnp.float32), -5.0, 5.0)
    return values * (start + ramp)


def draw_tokens(key, part):
    key = jax.random.fold_in(key, 7)
    return scaled_rows(key, 0.5).astype(jnp.bfloat16)


def vector_values(key, gain_low, gain_high):
    bias_key, gain_key, shift_key = jax.random.split(key, 3)
    ramp = jnp.arange(D, dtype=jnp.float32) / (D - 1)
    biases = jnp.clip(0.2 * jax.random.normal(bias_key, (5 * D + FF,), jnp.float32), -0.8, 0.8)
    jitter = jnp.clip(jax.random.normal(gain_key, (2, D), jnp.float32), -3.0, 3.0)
    gains = (gain_low + (gain_high - gain_low) * ramp) * (1.0 + 0.1 * jitter)
    shifts = jnp.clip(0.2 * jax.random.normal(shift_key, (2, D), jnp.float32), -0.8, 0.8)
    return jnp.concatenate([biases, gains[0], shifts[0], gains[1], shifts[1]])


def draw_vec_weight(key, part):
    key = jax.random.fold_in(key, 11)
    return vector_values(key, 0.6, 1.8)


def shard_levels(key, dims, cuts, smallest, high):
    def one(dim, blocks):
        steps = jax.random.uniform(jax.random.fold_in(jax.random.fold_in(key, 6), dim), (blocks,), jnp.float32, smallest / len(cuts), high / len(cuts))
        return jnp.repeat(jnp.exp(steps), dims[dim] // blocks).reshape((-1,) + (1,) * (len(dims) - dim - 1))

    loudness = one(*cuts[0])
    for cut in cuts[1:]:
        loudness = loudness * one(*cut)
    return loudness


def normal_values(key, extent, deviation, reach, cuts=(), held_as=jnp.bfloat16):
    array = jax.random.normal(key, extent, jnp.float32) * deviation
    if len(cuts) > 0:
        array = shard_levels(key, extent, cuts, -0.22, 0.18) * array
    return jnp.clip(array, min=-reach, max=reach).astype(held_as)


def setup_inputs(seed: int = 0) -> dict:
    key_of = jax.random.split(jax.random.key(seed), 23)
    return {
        "tokens": draw_tokens(jax.random.fold_in(key_of[22], 71), 0),
        "cotangent": normal_values(key_of[1], (SEQS, MAXM, D), 1.0, 6.0, ((0, 32),)),
        "positions": draw_positions(jax.random.fold_in(key_of[22], 71), 0),
        "counts": draw_counts(jax.random.fold_in(key_of[22], 71), 0),
        "qkv_weight": normal_values(key_of[4], (D, 3 * D), D ** -0.5, 0.21875, ((0, 8), (1, 4)), jnp.float32),
        "qkv_moment": normal_values(key_of[5], (D, 3 * D), (0.111 * PARAMS ** -0.5), 0.00024414062, ((0, 8), (1, 4)), jnp.float32),
        "qkv_second": jnp.clip(jnp.exp(math.log(5.540976566464906e-10) - 1.3862944 * jax.random.uniform(key_of[6], (D, 3 * D), jnp.float32) ** shard_levels(key_of[6], (D, 3 * D), ((0, 8), (1, 4)), -0.2, 0.2)), 1.3852441416162264e-10, 5.540976566464906e-10),
        "out_weight": normal_values(key_of[7], (D, D), (max(1, 2 * D // KP)) ** -0.5, 2.5, ((0, 8), (1, 4)), jnp.float32),
        "out_moment": normal_values(key_of[8], (D, D), (0.111 * PARAMS ** -0.5), 0.00024414062, ((0, 8), (1, 4)), jnp.float32),
        "out_second": jnp.clip(jnp.exp(math.log(5.540976705242784e-11) - 1.3862944 * jax.random.uniform(key_of[9], (D, D), jnp.float32) ** shard_levels(key_of[9], (D, D), ((0, 8), (1, 4)), -0.2, 0.2)), 1.385244176310696e-11, 5.540976705242784e-11),
        "up_weight": normal_values(key_of[10], (D, FF), D ** -0.5, 0.21875, ((0, 8), (1, 4)), jnp.float32),
        "up_moment": normal_values(key_of[11], (D, FF), (0.111 * PARAMS ** -0.5), 0.00024414062, ((0, 8), (1, 4)), jnp.float32),
        "up_second": jnp.clip(jnp.exp(math.log(5.540976566464906e-10) - 1.3862944 * jax.random.uniform(key_of[12], (D, FF), jnp.float32) ** shard_levels(key_of[12], (D, FF), ((0, 8), (1, 4)), -0.2, 0.2)), 1.3852441416162264e-10, 5.540976566464906e-10),
        "down_projection_weight": normal_values(key_of[13], (FF, D), (FF // 2) ** -0.5, 0.15625, ((0, 8), (1, 4)), jnp.float32),
        "down_moment": normal_values(key_of[14], (FF, D), (0.111 * PARAMS ** -0.5), 0.00024414062, ((0, 8), (1, 4)), jnp.float32),
        "down_second": jnp.clip(jnp.exp(math.log(5.540976566464906e-10) - 1.3862944 * jax.random.uniform(key_of[15], (FF, D), jnp.float32) ** shard_levels(key_of[15], (FF, D), ((0, 8), (1, 4)), -0.2, 0.2)), 1.3852441416162264e-10, 5.540976566464906e-10),
        "proj_weight": normal_values(key_of[16], (KP, SEQLEN), SEQLEN ** -0.5, 0.25, ((0, 4), (1, 8)), jnp.float32),
        "proj_moment": normal_values(key_of[17], (KP, SEQLEN), (0.111 * PARAMS ** -0.5), 0.00024414062, ((0, 4), (1, 8)), jnp.float32),
        "proj_second": jnp.clip(jnp.exp(math.log(5.540976566464906e-10) - 1.3862944 * jax.random.uniform(key_of[18], (KP, SEQLEN), jnp.float32) ** shard_levels(key_of[18], (KP, SEQLEN), ((0, 4), (1, 8)), -0.2, 0.2)), 1.3852441416162264e-10, 5.540976566464906e-10),
        "vec_weight": draw_vec_weight(jax.random.fold_in(key_of[22], 71), 0),
        "vec_moment": normal_values(key_of[20], (NVEC,), (0.333 * PARAMS ** -0.5), 0.0007324219, ((0, 32),), jnp.float32),
        "vec_second": jnp.clip(jnp.exp(math.log(4.986878909818415e-09) - 1.3862944 * jax.random.uniform(key_of[21], (NVEC,), jnp.float32) ** shard_levels(key_of[21], (NVEC,), ((0, 32),), -0.2, 0.2)), 1.2467197274546038e-09, 4.986878909818415e-09),
    }


@jax.custom_vjp
def low(v):
    return lax.optimization_barrier(v.astype(jnp.bfloat16)).astype(jnp.float32)

@jax.custom_vjp
def low_back(v):
    return v

def low_keep(v):
    return (low(v), None)

def low_pass(kept, grad):
    return (grad,)

def back_keep(v):
    return (v, None)

def back_low(kept, grad):
    return (low(grad),)
low.defvjp(low_keep, low_pass)
low_back.defvjp(back_keep, back_low)
HIGH = lax.Precision.HIGHEST
NORM_EPS = 1e-05
CLIP_NORM = 1.0
BETA_ONE = 0.9
BETA_TWO = 0.999
ADAM_EPS = 1e-08
DECAY_RATE = 0.01
RATE_QKV = 0.05
RATE_OUT = 0.4
RATE_UP = 0.05
RATE_DOWN = 0.05
RATE_PROJ = 0.05
RATE_VEC = 1.0

def layer_norm(summed, gains, shifts):
    average = lax.optimization_barrier(jnp.mean(summed, axis=-1, keepdims=True))
    centered = summed - average
    variance = lax.optimization_barrier(jnp.mean(centered * centered, axis=-1, keepdims=True))
    return centered * lax.rsqrt(variance + NORM_EPS) * gains + shifts

def gelu_exact(values):
    return jax.nn.gelu(values, approximate=False)

def split_vector(vec_full, model_width, hidden_width):
    mark_one = 3 * model_width
    mark_two = mark_one + model_width
    mark_three = mark_two + hidden_width
    mark_four = mark_three + model_width
    return (vec_full[:mark_one], vec_full[mark_one:mark_two], vec_full[mark_two:mark_three], vec_full[mark_three:mark_four], vec_full[mark_four:mark_four + model_width], vec_full[mark_four + model_width:mark_four + 2 * model_width], vec_full[mark_four + 2 * model_width:mark_four + 3 * model_width], vec_full[mark_four + 3 * model_width:mark_four + 4 * model_width])

def adam_update(weight, moment, second, grad, scale_clip, rate, decay):
    clipped = grad * scale_clip
    new_moment = BETA_ONE * moment + (1.0 - BETA_ONE) * clipped
    new_second = BETA_TWO * second + (1.0 - BETA_TWO) * clipped * clipped
    moment_hat = new_moment / (1.0 - BETA_ONE ** STEP)
    second_hat = new_second / (1.0 - BETA_TWO ** STEP)
    new_weight = weight - rate * (moment_hat / (jnp.sqrt(second_hat) + ADAM_EPS) + decay * weight)
    return (new_weight, new_moment, new_second, new_weight.astype(jnp.bfloat16))

def forward(inputs, qkv_weight, out_weight, up_weight, down_projection_weight, proj_weight, vec_weight):
    qkv_mat = low(qkv_weight)
    out_mat = low(out_weight)
    up_mat = low(up_weight)
    down_mat = low(down_projection_weight)
    proj_mat = low(proj_weight)
    vec_all = low(vec_weight)
    bias_qkv, bias_out, bias_up, bias_down, gain_one, shift_one, gain_two, shift_two = split_vector(vec_all, D, FF)
    group = inputs.shape[0]
    pre_qkv = jnp.einsum('gld,de->gle', inputs, qkv_mat, precision=HIGH)
    qkv_all = low(low_back(pre_qkv) + bias_qkv)
    queries = qkv_all[..., :D].reshape(group, SEQLEN, HEADS, HEAD_DIM)
    key_value_pair = qkv_all[..., D:]
    projected = low(low_back(jnp.einsum('jl,gld->gjd', proj_mat, key_value_pair, precision=HIGH)))
    key_heads = projected[..., :D].reshape(group, KP, HEADS, HEAD_DIM)
    value_heads = projected[..., D:].reshape(group, KP, HEADS, HEAD_DIM)
    raw_scores = jnp.einsum('glhe,gjhe->ghlj', queries, key_heads, precision=HIGH)
    scores = low_back(raw_scores) * HEAD_DIM ** (-0.5)
    soft_probs = low(jax.nn.softmax(scores, axis=-1))
    context = jnp.einsum('ghlj,gjhe->glhe', soft_probs, value_heads, precision=HIGH).reshape(group, SEQLEN, D)
    attended = low(low_back(context))
    branch_attn = low_back(jnp.einsum('gld,de->gle', attended, out_mat, precision=HIGH)) + bias_out
    normed_one = layer_norm(inputs + branch_attn, gain_one, shift_one)
    hidden_pre = low_back(jnp.einsum('gld,df->glf', low(normed_one), up_mat, precision=HIGH)) + bias_up
    active = low(gelu_exact(hidden_pre))
    branch_ffn = low_back(jnp.einsum('glf,fd->gld', active, down_mat, precision=HIGH)) + bias_down
    return layer_norm(normed_one + branch_ffn, gain_two, shift_two)

def reference(tokens, cotangent, positions, counts, qkv_weight, qkv_moment, qkv_second, out_weight, out_moment, out_second, up_weight, up_moment, up_second, down_projection_weight, down_moment, down_second, proj_weight, proj_moment, proj_second, vec_weight, vec_moment, vec_second):
    group = math.gcd(SEQS, max(1, 4096 // SEQLEN))
    blocks = SEQS // group
    inputs = tokens.astype(jnp.float32).reshape(blocks, group, SEQLEN, D)
    cot_blocks = cotangent.astype(jnp.float32).reshape(blocks, group, MAXM, D)
    pos_blocks = positions.reshape(blocks, group, MAXM)
    count_blocks = counts.reshape(blocks, group)
    params = (qkv_weight, out_weight, up_weight, down_projection_weight, proj_weight, vec_weight)

    def one_group(carry, pieces):
        block, cot_block, pos_block, count_block = pieces
        slot_live = jnp.arange(MAXM, dtype=jnp.int32)[None, :] < count_block[:, None]
        one_hot_rows = ((pos_block[:, :, None] == jnp.arange(SEQLEN, dtype=jnp.int32)[None, None, :]) & slot_live[:, :, None]).astype(jnp.float32)
        dense = jnp.einsum('gml,gmd->gld', one_hot_rows, cot_block, precision=HIGH)
        result, pullback = jax.vjp(forward, block, params[0], params[1], params[2], params[3], params[4], params[5])
        grads = pullback(dense)
        new_carry = tuple((total + grad for total, grad in zip(carry, grads[1:])))
        return (new_carry, (result.astype(jnp.bfloat16), grads[0].astype(jnp.bfloat16)))
    start = tuple((jnp.zeros_like(weight) for weight in params))
    totals, stacked = lax.scan(one_group, start, (inputs, cot_blocks, pos_blocks, count_blocks))
    output = stacked[0].reshape(TOTAL_TOKENS, D)
    grad_input = stacked[1].reshape(TOTAL_TOKENS, D)
    squares = jnp.float32(0.0)
    for grad in totals:
        squares = squares + jnp.sum(grad * grad)
    grad_norm = jnp.sqrt(squares)
    scale_clip = jnp.minimum(1.0, CLIP_NORM / grad_norm)
    qkv_parts = adam_update(qkv_weight, qkv_moment, qkv_second, totals[0], scale_clip, RATE_QKV, DECAY_RATE)
    out_parts = adam_update(out_weight, out_moment, out_second, totals[1], scale_clip, RATE_OUT, DECAY_RATE)
    up_parts = adam_update(up_weight, up_moment, up_second, totals[2], scale_clip, RATE_UP, DECAY_RATE)
    down_parts = adam_update(down_projection_weight, down_moment, down_second, totals[3], scale_clip, RATE_DOWN, DECAY_RATE)
    proj_parts = adam_update(proj_weight, proj_moment, proj_second, totals[4], scale_clip, RATE_PROJ, DECAY_RATE)
    vec_parts = adam_update(vec_weight, vec_moment, vec_second, totals[5], scale_clip, RATE_VEC, 0.0)
    return (output, grad_input, grad_norm, qkv_parts[0], qkv_parts[1], qkv_parts[2], qkv_parts[3], out_parts[0], out_parts[1], out_parts[2], out_parts[3], up_parts[0], up_parts[1], up_parts[2], up_parts[3], down_parts[0], down_parts[1], down_parts[2], down_parts[3], proj_parts[0], proj_parts[1], proj_parts[2], proj_parts[3], vec_parts[0], vec_parts[1], vec_parts[2], vec_parts[3])
```

```python
import functools
import math

import jax
import jax.numpy as jnp
from jax import lax
from jax.experimental import pallas as pl
from jax.experimental.pallas import tpu as pltpu
from jax.sharding import PartitionSpec as P

HEADS = 12
STEP = 10
NORM_EPS = 1e-05
CLIP_NORM = 1.0
BETA_ONE = 0.9
BETA_TWO = 0.999
ADAM_EPS = 1e-08
DECAY_RATE = 0.01
RATE_QKV = 0.05
RATE_OUT = 0.4
RATE_UP = 0.05
RATE_DOWN = 0.05
RATE_PROJ = 0.05
RATE_VEC = 1.0

BF = jnp.bfloat16
F32 = jnp.float32
LOG2E = math.log2(math.e)
MIB = 1 << 20


def nn(a, b):
    return jnp.dot(a, b, preferred_element_type=F32)


def nt(a, b):
    return lax.dot_general(a, b, (((1,), (1,)), ((), ())), preferred_element_type=F32)


def sds(shape, dtype):
    return jax.ShapeDtypeStruct(tuple(shape), dtype)


def whole(shape):
    n = len(shape)
    return pl.BlockSpec(tuple(shape), lambda *_: (0,) * n)


def nbytes(x):
    return math.prod(x.shape) * jnp.dtype(x.dtype).itemsize


def call(
    kernel,
    name,
    out_shape,
    args,
    grid=(1,),
    in_specs=None,
    out_specs=None,
    scratch=(),
    place=None,
    flops=0,
    exps=0,
    vmem=48,
):
    many = isinstance(out_shape, (list, tuple))
    outs = list(out_shape) if many else [out_shape]
    if in_specs is None:
        in_specs = [whole(a.shape) for a in args]
    if out_specs is None:
        out_specs = [whole(o.shape) for o in outs]
    moved = sum(nbytes(a) for a in args) + sum(nbytes(o) for o in outs)
    result = pl.pallas_call(
        kernel,
        name=name,
        out_shape=outs,
        grid_spec=pltpu.PrefetchScalarGridSpec(
            num_scalar_prefetch=0 if place is None else 1,
            grid=grid,
            in_specs=in_specs,
            out_specs=out_specs,
            scratch_shapes=list(scratch),
        ),
        cost_estimate=pl.CostEstimate(
            flops=int(flops), bytes_accessed=int(moved), transcendentals=int(exps)
        ),
        compiler_params=pltpu.CompilerParams(
            vmem_limit_bytes=vmem * MIB,
            dimension_semantics=("arbitrary",) * len(grid),
        ),
    )(*(() if place is None else (place,)), *args)
    return result if many else result[0]


def norm_stats(summed):
    average = jnp.mean(summed, axis=-1, keepdims=True)
    centered = summed - average
    variance = jnp.mean(centered * centered, axis=-1, keepdims=True)
    inverse = lax.rsqrt(variance + NORM_EPS)
    return centered * inverse, inverse


def norm_grad(shaped, inverse, gains, grad):
    inner = grad * gains
    first = jnp.mean(inner, axis=-1, keepdims=True)
    second = jnp.mean(inner * shaped, axis=-1, keepdims=True)
    return inverse * (inner - first - shaped * second)


def normal_parts(values):
    size = jnp.abs(values)
    base = 1.0 + (0.3275911 * math.sqrt(0.5)) * size
    t = pl.reciprocal(base, approx=True)
    t = t * (2.0 - base * t)
    bell = jnp.exp2(values * values * (-0.5 * LOG2E))
    poly = 0.5 * 1.061405429
    for c in (-1.453152027, 1.421413741, -0.284496736, 0.254829592):
        poly = poly * t + 0.5 * c
    tail = poly * t * bell
    return bell, jnp.where(values >= 0.0, 1.0 - tail, tail)


def pack_kernel(qkv, out, up, down, proj, vec, a_ref, b_ref, c_ref, small):
    rows, wide = qkv.shape
    a_ref[:rows, :wide] = qkv[...].astype(BF)
    a_ref[:rows, wide:] = out[...].astype(BF)
    small[...] = jnp.zeros_like(small)
    height, width = proj.shape
    for g in range(height // 8):
        small[0:8, g * width : (g + 1) * width] = proj[8 * g : 8 * g + 8, :]
    start = (height // 8) * width
    room = small.shape[1] - start
    small[0:1, start:] = vec[:, :room]
    left = vec.shape[1] - room
    small[1:2, start : start + left] = vec[:, room:]
    a_ref[rows:, :] = small[...].astype(BF)
    b_ref[...] = up[...].astype(BF)
    thin = down.shape[1]
    for g in range(down.shape[0] // rows):
        c_ref[:, g * thin : (g + 1) * thin] = down[rows * g : rows * (g + 1), :].astype(BF)


def pack(qkv, out, up, down, proj, vec):
    rows, wide = qkv.shape[0], qkv.shape[1] + out.shape[1]
    return call(
        pack_kernel,
        "pack_weights",
        [sds((rows + 16, wide), BF), sds((rows, wide), BF), sds((rows, wide), BF)],
        (qkv, out, up, down, proj, vec),
        scratch=[pltpu.VMEM((16, wide), F32)],
    )


def order_kernel(marked, pos, x, front, rest, frontt, xt, back):
    length = x.shape[1]
    half = front.shape[1]
    col = lax.broadcasted_iota(jnp.int32, (half, length), 1)
    row = lax.broadcasted_iota(jnp.int32, (half, length), 0)
    hot = (pos[0] == col) & (row < marked)
    listed = jnp.sum(hot.astype(F32), axis=0, keepdims=True)
    free = 1.0 - listed
    before = (
        lax.broadcasted_iota(jnp.int32, (length, length), 0)
        < lax.broadcasted_iota(jnp.int32, (length, length), 1)
    ).astype(BF)
    rank = nn(jnp.broadcast_to(free, (16, length)).astype(BF), before)[0:1, :]
    target = jnp.where(free > 0.5, rank.astype(jnp.int32) + marked, -1)
    one = hot | (target == row)
    two = target == (row + half)
    one = jnp.where(one, 1.0, 0.0)
    two = jnp.where(two, 1.0, 0.0)
    values = x[0]
    head = nn(one.astype(BF), values)
    front[0] = head.astype(BF)
    rest[0] = nn(two.astype(BF), values).astype(BF)
    frontt[...] = head.T.astype(BF)
    xt[...] = values.T
    back[0, :, :half] = one.T.astype(BF)
    back[0, :, half:] = two.T.astype(BF)


def order_rows(tokens, positions):
    seqs, length, width = tokens.shape
    marked = positions.shape[1]
    half = length // 2
    pos = jnp.pad(positions, ((0, 0), (0, half - marked)), constant_values=-1)[:, :, None]
    rows = sds((seqs, half, width), BF)
    spec = pl.BlockSpec((1, half, width), lambda s: (s, 0, 0))
    return call(
        functools.partial(order_kernel, marked),
        "order_rows",
        [
            rows,
            rows,
            sds((width, seqs * half), BF),
            sds((width, seqs * length), BF),
            sds((seqs, length, length), BF),
        ],
        (pos, tokens),
        grid=(seqs,),
        in_specs=[
            pl.BlockSpec((1, half, 1), lambda s: (s, 0, 0)),
            pl.BlockSpec((1, length, width), lambda s: (s, 0, 0)),
        ],
        out_specs=[
            spec,
            spec,
            pl.BlockSpec((width, half), lambda s: (0, s)),
            pl.BlockSpec((width, length), lambda s: (0, s)),
            pl.BlockSpec((1, length, length), lambda s: (s, 0, 0)),
        ],
        flops=2 * seqs * length * length * width,
    )


def qkv_kernel(front, rest, x, weight, vec, proj, q_front, q_rest, kv, kvp):
    width = front.shape[2]
    piece = width // 2
    for j in range(2):
        cols = slice(j * piece, (j + 1) * piece)
        w = weight[:, cols]
        bias = vec[:, cols]
        q_front[0, :, cols] = (nn(front[0], w) + bias).astype(BF)
        q_rest[0, :, cols] = (nn(rest[0], w) + bias).astype(BF)
    for j in range(4):
        cols = slice(j * piece, (j + 1) * piece)
        at = slice(width + j * piece, width + (j + 1) * piece)
        part = (nn(x[0], weight[:, at]) + vec[:, at]).astype(BF)
        kv[0, :, cols] = part
        kvp[0, :, cols] = nn(proj[...], part).astype(BF)


def make_qkv(front, rest, x, weight, vec, proj):
    seqs, half, width = front.shape
    length = x.shape[1]
    rows = proj.shape[0]

    def per(*shape):
        return pl.BlockSpec((1, *shape), lambda s: (s, 0, 0))

    return call(
        qkv_kernel,
        "make_qkv",
        [
            sds(front.shape, BF),
            sds(front.shape, BF),
            sds((seqs, length, 2 * width), BF),
            sds((seqs, rows, 2 * width), BF),
        ],
        (front, rest, x, weight, vec, proj),
        grid=(seqs,),
        in_specs=[
            per(half, width),
            per(half, width),
            per(length, width),
            whole(weight.shape),
            whole(vec.shape),
            whole(proj.shape),
        ],
        out_specs=[per(half, width), per(half, width), per(length, 2 * width), per(rows, 2 * width)],
        flops=2 * seqs * length * width * width * 3 + 2 * seqs * rows * length * 2 * width,
    )


def attend_kernel(head, q_front, q_rest, keys, values, o_front, o_rest):
    lane = lax.broadcasted_iota(jnp.int32, (1, 2 * head), 1)
    k, v = keys[0], values[0]
    zero = jnp.zeros_like(k)
    factor = LOG2E / math.sqrt(head)
    pairs = [
        (jnp.where(own, k, zero), jnp.where(own, v, zero)) for own in (lane < head, lane >= head)
    ]
    for q_ref, o_ref in ((q_front, o_front), (q_rest, o_rest)):
        total = None
        for kh, vh in pairs:
            s = nt(q_ref[0], kh)
            e = jnp.exp2((s - jnp.max(s, axis=-1, keepdims=True)) * factor)
            scale = 1.0 / jnp.sum(e, axis=-1, keepdims=True)
            part = nn(e.astype(BF), vh) * scale
            total = part if total is None else total + part
        o_ref[0] = total.astype(BF)


def attend(q_front, q_rest, kvp):
    seqs, half, width = q_front.shape
    rows = kvp.shape[1]
    head = width // HEADS
    pairs = HEADS // 2
    spec = pl.BlockSpec((1, half, 2 * head), lambda s, p: (s, 0, p))
    return call(
        functools.partial(attend_kernel, head),
        "attend",
        [sds(q_front.shape, BF)] * 2,
        (q_front, q_rest, kvp, kvp),
        grid=(seqs, pairs),
        in_specs=[
            spec,
            spec,
            pl.BlockSpec((1, rows, 2 * head), lambda s, p: (s, 0, p)),
            pl.BlockSpec((1, rows, 2 * head), lambda s, p: (s, 0, p + pairs)),
        ],
        out_specs=[spec, spec],
        flops=2 * seqs * HEADS * 2 * half * rows * 2 * head * 2,
        exps=seqs * HEADS * 2 * half * rows,
    )


def join_kernel(marks, keep, attended, x, weight, vec, normed, low, *more):
    bias, gain, shift = (vec[:, a:b] for a, b in marks)
    summed = x[...].astype(F32) + nn(attended[...], weight[...]) + bias
    shaped, _ = norm_stats(summed)
    result = shaped * gain + shift
    normed[...] = result
    low[...] = result.astype(BF)
    if keep:
        kept, lowt, attendedt = more
        kept[...] = summed
        lowt[...] = result.T.astype(BF)
        attendedt[...] = attended[...].T


def join(attended, x, weight, vec, marks, keep):
    rows, width = x.shape
    block = min(256, rows)
    spec = pl.BlockSpec((block, width), lambda i: (i, 0))
    across = pl.BlockSpec((width, block), lambda i: (0, i))
    outs = [sds((rows, width), F32), sds((rows, width), BF)]
    specs = [spec, spec]
    if keep:
        outs += [sds((rows, width), F32), sds((width, rows), BF), sds((width, rows), BF)]
        specs += [spec, across, across]
    return call(
        functools.partial(join_kernel, marks, keep),
        "join_front" if keep else "join_rest",
        outs,
        (attended, x, weight, vec),
        grid=(rows // block,),
        in_specs=[spec, spec, whole(weight.shape), whole(vec.shape)],
        out_specs=specs,
        flops=2 * rows * width * width,
    )


def lift_kernel(keep, low, weight, bias, active, *more):
    rows = low.shape[0]
    step = 128
    w = weight[0]
    for r in range(0, rows, step):
        u = nn(low[r : r + step, :], w) + bias[...]
        bell, share = normal_parts(u)
        a = u * share
        active[r : r + step, :] = a.astype(BF)
        if keep:
            slope, activet = more
            slope[r : r + step, :] = (share + u * bell * (1.0 / math.sqrt(2.0 * math.pi))).astype(BF)
            activet[:, r : r + step] = a.T.astype(BF)


def lift(low, weight, vec, mark, keep):
    rows, width = low.shape
    parts, _, piece = weight.shape
    first = mark // piece
    spec = pl.BlockSpec((rows, piece), lambda f: (0, f))
    outs, specs = [sds((rows, parts * piece), BF)], [spec]
    if keep:
        outs += [sds((rows, parts * piece), BF), sds((parts * piece, rows), BF)]
        specs += [spec, pl.BlockSpec((piece, rows), lambda f: (f, 0))]
    return call(
        functools.partial(lift_kernel, keep),
        "lift_front" if keep else "lift_rest",
        outs,
        (low, weight, vec),
        grid=(parts,),
        in_specs=[
            whole(low.shape),
            pl.BlockSpec((1, width, piece), lambda f: (f, 0, 0)),
            pl.BlockSpec((1, piece), lambda f: (0, first + f)),
        ],
        out_specs=specs,
        flops=2 * rows * width * parts * piece,
        exps=2 * rows * parts * piece,
    )


def lower_rest_kernel(marks, active, normed, weight, vec, output):
    bias, gain, shift = (vec[:, a:b] for a, b in marks)
    summed = normed[...] + nn(active[...], weight[...]) + bias
    shaped, _ = norm_stats(summed)
    output[...] = (shaped * gain + shift).astype(BF)


def lower_front_kernel(marks, active, normed, weight, vec, dy, output, d_sum, d_low, sums):
    bias, gain, shift = (vec[:, a:b] for a, b in marks)
    summed = normed[...] + nn(active[...], weight[...]) + bias
    shaped, inverse = norm_stats(summed)
    output[...] = (shaped * gain + shift).astype(BF)
    grad = dy[...].astype(F32)
    back = norm_grad(shaped, inverse, gain, grad)
    d_sum[...] = back
    d_low[...] = back.astype(BF)

    @pl.when(pl.program_id(0) == 0)
    def _():
        sums[...] = jnp.zeros_like(sums)

    sums[0:1, :] += jnp.sum(grad * shaped, axis=0, keepdims=True)
    sums[1:2, :] += jnp.sum(grad, axis=0, keepdims=True)
    sums[2:3, :] += jnp.sum(back, axis=0, keepdims=True)


def lower(active, normed, weight, vec, marks, dy=None):
    rows, width = normed.shape
    hidden = active.shape[1]
    block = min(256, rows)
    spec = pl.BlockSpec((block, width), lambda i: (i, 0))
    wide = pl.BlockSpec((block, hidden), lambda i: (i, 0))
    flops = 2 * rows * width * hidden
    if dy is None:
        return call(
            functools.partial(lower_rest_kernel, marks),
            "lower_rest",
            sds((rows, width), BF),
            (active, normed, weight, vec),
            grid=(rows // block,),
            in_specs=[wide, spec, whole(weight.shape), whole(vec.shape)],
            out_specs=[spec],
            flops=flops,
        )
    return call(
        functools.partial(lower_front_kernel, marks),
        "lower_front",
        [
            sds((rows, width), BF),
            sds((rows, width), F32),
            sds((rows, width), BF),
            sds((8, width), F32),
        ],
        (active, normed, weight, vec, dy),
        grid=(rows // block,),
        in_specs=[wide, spec, whole(weight.shape), whole(vec.shape), spec],
        out_specs=[spec, spec, spec, whole((8, width))],
        flops=flops,
    )


def hidden_back_kernel(d_low, weight, slope, d_hidden, sums):
    step = 256
    for r in range(0, d_low.shape[0], step):
        du = nt(d_low[r : r + step, :], weight[...]) * slope[r : r + step, :].astype(F32)
        d_hidden[r : r + step, :] = du.astype(BF)
        part = jnp.sum(du, axis=0, keepdims=True)
        if r == 0:
            sums[...] = part
        else:
            sums[...] += part


def hidden_back(d_low, weight, slope):
    rows, width = d_low.shape
    hidden = weight.shape[0]
    piece = width
    spec = pl.BlockSpec((rows, piece), lambda f: (0, f))
    return call(
        hidden_back_kernel,
        "hidden_back",
        [sds((rows, hidden), BF), sds((1, hidden), F32)],
        (d_low, weight, slope),
        grid=(hidden // piece,),
        in_specs=[whole(d_low.shape), pl.BlockSpec((piece, width), lambda f: (f, 0)), spec],
        out_specs=[spec, pl.BlockSpec((1, piece), lambda f: (0, f))],
        flops=2 * rows * width * hidden,
    )


def first_back_kernel(
    marks, d_hidden, up, d_sum, kept, vec, weight, d_first, d_low, d_attended, sums, total
):
    part = nt(d_hidden[...], up[0])

    @pl.when(pl.program_id(0) == 0)
    def _():
        total[...] = d_sum[...] + part

    @pl.when(pl.program_id(0) > 0)
    def _():
        total[...] += part

    @pl.when(pl.program_id(0) == pl.num_programs(0) - 1)
    def _():
        gain = vec[:, marks[0] : marks[1]]
        grad = total[...]
        shaped, inverse = norm_stats(kept[...])
        back = norm_grad(shaped, inverse, gain, grad)
        low = back.astype(BF)
        d_first[...] = back
        d_low[...] = low
        sums[...] = jnp.zeros_like(sums)
        sums[0:1, :] = jnp.sum(grad * shaped, axis=0, keepdims=True)
        sums[1:2, :] = jnp.sum(grad, axis=0, keepdims=True)
        sums[2:3, :] = jnp.sum(back, axis=0, keepdims=True)
        d_attended[...] = nt(low, weight[...]).astype(BF)


def first_back(d_hidden, up, d_sum, kept, vec, weight, marks):
    rows, width = d_sum.shape
    parts, _, piece = up.shape
    full = (rows, width)
    return call(
        functools.partial(first_back_kernel, marks),
        "first_back",
        [sds(full, F32), sds(full, BF), sds(full, BF), sds((8, width), F32)],
        (d_hidden, up, d_sum, kept, vec, weight),
        grid=(parts,),
        in_specs=[
            pl.BlockSpec((rows, piece), lambda f: (0, f)),
            pl.BlockSpec((1, width, piece), lambda f: (f, 0, 0)),
            whole(full),
            whole(full),
            whole(vec.shape),
            whole(weight.shape),
        ],
        out_specs=[whole(full), whole(full), whole(full), whole((8, width))],
        scratch=[pltpu.VMEM(full, F32)],
        flops=2 * rows * width * (parts * piece + width),
    )


def attend_back_kernel(head, queries, keys, values, grads, d_q, d_k, d_v, sums):
    lane = lax.broadcasted_iota(jnp.int32, (1, 2 * head), 1)
    line = lax.broadcasted_iota(jnp.int32, (2 * head, 1), 0)
    q, k, v, g = queries[0], keys[0], values[0], grads[0]
    zero = jnp.zeros_like(k)
    kt = k.T
    scale = 1.0 / math.sqrt(head)
    dq = dk = dv = None
    for own, ownt in ((lane < head, line < head), (lane >= head, line >= head)):
        s = nt(jnp.where(own, k, zero), q)
        e = jnp.exp2((s - jnp.max(s, axis=0, keepdims=True)) * (LOG2E * scale))
        p = e * (1.0 / jnp.sum(e, axis=0, keepdims=True))
        dv_part = nn(p.astype(BF), jnp.where(own, g, jnp.zeros_like(g)))
        dp = nt(jnp.where(own, v, zero), g)
        both = p * dp
        ds = ((both - p * jnp.sum(both, axis=0, keepdims=True)) * scale).astype(BF)
        dk_part = nn(ds, jnp.where(own, q, jnp.zeros_like(q)))
        dq_part = nn(jnp.where(ownt, kt, jnp.zeros_like(kt)), ds)
        dv = dv_part if dv is None else dv + dv_part
        dk = dk_part if dk is None else dk + dk_part
        dq = dq_part if dq is None else dq + dq_part
    dq = dq.T
    d_q[0] = dq.astype(BF)
    d_k[0] = dk.astype(BF)
    d_v[0] = dv.astype(BF)
    sums[0] = jnp.sum(dq, axis=0, keepdims=True)


def attend_back(queries, kvp, grads):
    seqs, half, width = queries.shape
    rows = kvp.shape[1]
    head = width // HEADS
    pairs = HEADS // 2
    spec = pl.BlockSpec((1, half, 2 * head), lambda s, p: (s, 0, p))
    proj = pl.BlockSpec((1, rows, 2 * head), lambda s, p: (s, 0, p))
    return call(
        functools.partial(attend_back_kernel, head),
        "attend_back",
        [
            sds(queries.shape, BF),
            sds((seqs, rows, width), BF),
            sds((seqs, rows, width), BF),
            sds((seqs, 1, width), F32),
        ],
        (queries, kvp, kvp, grads),
        grid=(seqs, pairs),
        in_specs=[
            spec,
            proj,
            pl.BlockSpec((1, rows, 2 * head), lambda s, p: (s, 0, p + pairs)),
            spec,
        ],
        out_specs=[spec, proj, proj, pl.BlockSpec((1, 1, 2 * head), lambda s, p: (s, 0, p))],
        flops=2 * seqs * HEADS * half * rows * 2 * head * 5,
        exps=seqs * HEADS * half * rows,
    )


def spread_kernel(d_k, d_v, kv, projt, d_kv, d_proj, sums):
    width = d_k.shape[2]
    grad = None
    for j, ref in enumerate((d_k, d_v)):
        cols = slice(j * width, (j + 1) * width)
        part = nn(projt[...], ref[0])
        d_kv[0, :, cols] = part.astype(BF)
        sums[0, :, cols] = jnp.sum(part, axis=0, keepdims=True)
        more = nt(ref[0], kv[0, :, cols])
        grad = more if grad is None else grad + more

    @pl.when(pl.program_id(0) == 0)
    def _():
        d_proj[...] = grad

    @pl.when(pl.program_id(0) > 0)
    def _():
        d_proj[...] += grad


def spread(d_k, d_v, kv, projt):
    seqs, rows, width = d_k.shape
    length = kv.shape[1]

    def per(*shape):
        return pl.BlockSpec((1, *shape), lambda s: (s, 0, 0))

    return call(
        spread_kernel,
        "spread_kv",
        [
            sds((seqs, length, 2 * width), BF),
            sds((rows, length), F32),
            sds((seqs, 1, 2 * width), F32),
        ],
        (d_k, d_v, kv, projt),
        grid=(seqs,),
        in_specs=[
            per(rows, width),
            per(rows, width),
            per(length, 2 * width),
            whole(projt.shape),
        ],
        out_specs=[per(length, 2 * width), whole((rows, length)), per(1, 2 * width)],
        flops=2 * seqs * rows * length * 2 * width * 2,
    )


def input_back_kernel(d_kv, d_q, d_first, weight, back, result):
    width = d_q.shape[2]
    half = d_q.shape[1]
    front = d_first[0] + nt(d_q[0], weight[:, :width])
    high = front.astype(BF)
    low = (front - high.astype(F32)).astype(BF)
    place = back[0, :, :half]
    total = nt(d_kv[0], weight[:, width:]) + nn(place, high) + nn(place, low)
    result[0] = total.astype(BF)


def input_back(d_kv, d_q, d_first, weight, back):
    seqs, length, wide = d_kv.shape
    half, width = d_q.shape[1:]

    def per(*shape):
        return pl.BlockSpec((1, *shape), lambda s: (s, 0, 0))

    return call(
        input_back_kernel,
        "input_back",
        sds((seqs, length, width), BF),
        (d_kv, d_q, d_first, weight, back),
        grid=(seqs,),
        in_specs=[
            per(length, wide),
            per(half, width),
            per(half, width),
            whole(weight.shape),
            per(length, length),
        ],
        out_specs=[per(length, width)],
        flops=2 * seqs * length * width * (wide + width // 2 + length),
    )


def restore_kernel(front, rest, back, result):
    half = front.shape[1]
    total = nn(back[0, :, :half], front[0]) + nn(back[0, :, half:], rest[0])
    result[0] = total.astype(BF)


def restore(front, rest, back):
    seqs, half, width = front.shape
    length = back.shape[1]

    def per(*shape):
        return pl.BlockSpec((1, *shape), lambda s: (s, 0, 0))

    return call(
        restore_kernel,
        "restore_order",
        sds((seqs, length, width), BF),
        (front, rest, back),
        grid=(seqs,),
        in_specs=[per(half, width), per(half, width), per(length, length)],
        out_specs=[per(length, width)],
        flops=2 * seqs * length * length * width,
    )


def grad_up_kernel(place, lowt, d_hidden, result):
    slots, _, rows, count = lowt.shape
    part = nn(lowt[...].reshape(slots * rows, count), d_hidden[...]).astype(BF)
    for z in range(slots):
        result[0, (z - place[1] + slots) % slots] = part[z * rows : (z + 1) * rows]


def grad_up(place, lowt, d_hidden, other, fsdp, slots):
    width, count = lowt.shape
    rows = width // (2 * slots)
    piece = d_hidden.shape[1] // fsdp
    lowt = lowt.reshape(slots, 2, rows, count)
    return call(
        grad_up_kernel,
        "grad_up",
        sds((fsdp, slots, rows, piece), BF),
        (lowt, d_hidden),
        grid=(fsdp,),
        in_specs=[
            pl.BlockSpec((slots, 1, rows, count), lambda f, p: (0, p[2] ^ other, 0, 0)),
            pl.BlockSpec((count, piece), lambda f, p: (0, f)),
        ],
        out_specs=[pl.BlockSpec((1, slots, rows, piece), lambda f, p: (f ^ p[0], 0, 0, 0))],
        place=place,
        flops=2 * width // 2 * count * piece * fsdp,
    )


def grad_down_kernel(place, activet, d_low, result, work):
    fsdp, _, rows, wide = result.shape
    thin = d_low.shape[1] // fsdp
    work[...] = nn(activet[0, 0], d_low[...]).astype(BF)
    for f in range(fsdp):
        for g in range(wide // thin):
            result[f ^ place[0], 0, :, g * thin : (g + 1) * thin] = work[
                g * rows : (g + 1) * rows, f * thin : (f + 1) * thin
            ]


def grad_down(place, activet, d_low, other, fsdp, slots):
    hidden, count = activet.shape
    width = d_low.shape[1]
    tall = hidden // (2 * slots)
    thin = width // fsdp
    rows = tall * thin // width
    activet = activet.reshape(slots, 2, tall, count)
    return call(
        grad_down_kernel,
        "grad_down",
        sds((fsdp, slots, rows, width), BF),
        (activet, d_low),
        grid=(slots,),
        in_specs=[
            pl.BlockSpec((1, 1, tall, count), lambda z, p: (z, p[2] ^ other, 0, 0)),
            whole(d_low.shape),
        ],
        out_specs=[
            pl.BlockSpec(
                (fsdp, 1, rows, width), lambda z, p: (0, (z - p[1] + slots) % slots, 0, 0)
            )
        ],
        scratch=[pltpu.VMEM((tall, width), BF)],
        place=place,
        flops=2 * hidden // 2 * count * width,
    )


def grad_rest_kernel(
    other,
    place,
    xt,
    frontt,
    attendedt,
    d_q,
    d_kv,
    d_low,
    d_proj,
    q_sums,
    kv_sums,
    one_sums,
    up_sums,
    two_sums,
    result,
    work_qkv,
    work_out,
    vector,
    small,
):
    fsdp, slots, tall, wide = result.shape
    rows = tall - 16
    width = d_q.shape[1]
    count = d_q.shape[0]
    work_qkv[:, :width] = nn(frontt[...].reshape(slots * rows, count), d_q[...]).astype(BF)
    left = xt[...].reshape(slots * rows, d_kv.shape[0])
    for j in range(2):
        cols = slice(j * width, (j + 1) * width)
        work_qkv[:, (j + 1) * width : (j + 2) * width] = nn(left, d_kv[:, cols]).astype(BF)
    work_out[...] = nn(attendedt[...].reshape(slots * rows, count), d_low[...]).astype(BF)
    hidden = up_sums.shape[1]
    at = 0
    for value in (
        jnp.sum(q_sums[...], axis=0),
        jnp.sum(kv_sums[...], axis=0),
        one_sums[2:3, :],
        up_sums[...],
        two_sums[2:3, :],
        one_sums[0:1, :],
        one_sums[1:2, :],
        two_sums[0:1, :],
        two_sums[1:2, :],
    ):
        size = value.shape[1]
        vector[:, at : at + size] = value
        at += size
    piece = 3 * width // fsdp
    thin = width // fsdp
    entries = vector.shape[1] // (2 * fsdp * slots)
    height = d_proj.shape[0] // fsdp
    across = d_proj.shape[1] // (2 * slots)
    start = (height // 8) * across
    room = wide - start
    first = (place[2] ^ other) == 0
    small[...] = jnp.zeros_like(small)
    for f in range(fsdp):
        for z in range(slots):
            at = (f ^ place[0], (z - place[1] + slots) % slots)
            lines = slice(z * rows, (z + 1) * rows)
            result[at[0], at[1], :rows, :piece] = work_qkv[lines, f * piece : (f + 1) * piece]
            result[at[0], at[1], :rows, piece:] = work_out[lines, f * thin : (f + 1) * thin]
            for g in range(height // 8):
                both = d_proj[
                    f * height + 8 * g : f * height + 8 * g + 8,
                    2 * z * across : 2 * (z + 1) * across,
                ]
                small[0:8, g * across : (g + 1) * across] = jnp.where(
                    first, both[:, :across], both[:, across:]
                )
            base = (f * 2 * slots + 2 * z) * entries
            own = jnp.where(
                first,
                vector[:, base : base + entries],
                vector[:, base + entries : base + 2 * entries],
            )
            small[0:1, start:] = own[:, :room]
            small[1:2, start : start + entries - room] = own[:, room:]
            result[at[0], at[1], rows:, :] = small[...].astype(BF)


def grad_rest(place, xt, frontt, attendedt, d_q, d_kv, d_low, d_proj, sums, other, fsdp, slots):
    width, tokens = xt.shape
    count = frontt.shape[1]
    rows = width // (2 * slots)
    wide = 4 * width // fsdp

    def lines(n):
        return pl.BlockSpec((slots, 1, rows, n), lambda i, p: (0, p[2] ^ other, 0, 0))

    def split(value):
        return value.reshape(slots, 2, rows, value.shape[1])

    plain = (d_q, d_kv, d_low, d_proj, *sums)
    entries = sum(math.prod(s.shape[1:]) for s in sums[:2]) + 6 * width + sums[3].shape[1]
    return call(
        functools.partial(grad_rest_kernel, other),
        "grad_rest",
        sds((fsdp, slots, rows + 16, wide), BF),
        (split(xt), split(frontt), split(attendedt), *plain),
        in_specs=[lines(tokens), lines(count), lines(count), *(whole(a.shape) for a in plain)],
        scratch=[
            pltpu.VMEM((slots * rows, 3 * width), BF),
            pltpu.VMEM((slots * rows, width), BF),
            pltpu.VMEM((1, entries), F32),
            pltpu.VMEM((16, wide), F32),
        ],
        place=place,
        flops=width * width * (2 * count + 2 * tokens),
    )


def swap_core(value):
    n = lax.axis_size("dp")
    return lax.ppermute(value, "dp", [(i, i ^ 1) for i in range(n)])


def shift_slot(value, by):
    n = lax.axis_size("dp")
    return lax.ppermute(value, "dp", [(i, (i + 2 * by) % n) for i in range(n)])


def swap_fsdp(value, bits):
    n = lax.axis_size("fsdp")
    return lax.ppermute(value, "fsdp", [(i, i ^ bits) for i in range(n)])


SOURCES = [
    (bits, steps, other)
    for other in (0, 1)
    for bits in (0, 1, 2, 3)
    for steps in ((0, 1), (2, 3))
]


def gather_piece(own):
    back = [own] + [shift_slot(own, k) for k in (1, 2, 3)]
    near = jnp.stack(back[:2])
    far = jnp.stack(back[2:])
    x_near, y_near = swap_fsdp(near, 1), swap_fsdp(near, 2)
    x_far, y_far = swap_fsdp(far, 1), swap_fsdp(far, 2)
    d_near = swap_fsdp(x_near, 2)
    d_far = swap_fsdp(y_far, 1)
    ours = [near, far, x_near, x_far, y_near, y_far, d_near, d_far]
    return ours + [swap_core(a) for a in ours]


def source_places(place, slots):
    for n, (bits, steps, other) in enumerate(SOURCES):
        for i, back in enumerate(steps):
            f = place[0] ^ bits
            z = (place[1] - back + slots) % slots
            yield n, i, f, z, place[2] ^ other


def fetch_blocks(place, refs, work, sems, slots, at):
    copies = []
    for number, (n, i, f, z, c) in enumerate(source_places(place, slots)):
        copies.append(
            pltpu.make_async_copy(refs[n].at[i], work.at[at(f, z, c)], sems.at[number])
        )
    for copy in copies:
        copy.start()
    for copy in copies:
        copy.wait()


def first_whole_kernel(slots, fsdp, height, across, place, *refs):
    blocks = refs[:16]
    qkv, out, vec, proj, projt, work, matrix, sems = refs[16:]
    fetch_blocks(place, blocks, work, sems, slots, lambda f, z, c: (c, z, f))
    wide = work.shape[4]
    rows = work.shape[3] - 16
    piece = qkv.shape[1] // fsdp
    thin = out.shape[1] // fsdp
    entries = vec.shape[1] // (2 * slots * fsdp)
    start = (height // 8) * across
    room = wide - start
    for f in range(fsdp):
        for z in range(slots):
            for c in range(2):
                d = 2 * z + c
                lines = slice(d * rows, (d + 1) * rows)
                qkv[lines, f * piece : (f + 1) * piece] = work[c, z, f, :rows, :piece]
                out[lines, f * thin : (f + 1) * thin] = work[c, z, f, :rows, piece:]
                small = work[c, z, f, rows:, :].astype(F32)
                for g in range(height // 8):
                    matrix[
                        f * height + 8 * g : f * height + 8 * g + 8, d * across : (d + 1) * across
                    ] = small[0:8, g * across : (g + 1) * across]
                base = (f * 2 * slots + d) * entries
                vec[:, base : base + room] = small[0:1, start:]
                vec[:, base + room : base + entries] = small[1:2, start : start + entries - room]
    proj[...] = matrix[...].astype(BF)
    projt[...] = matrix[...].T.astype(BF)


def first_whole(place, blocks, fsdp, slots, width, proj_shape, entries):
    tall, wide = blocks[0].shape[1:]
    height, across = proj_shape[0] // fsdp, proj_shape[1] // (2 * slots)
    return call(
        functools.partial(first_whole_kernel, slots, fsdp, height, across),
        "whole_first",
        [
            sds((width, 3 * width), BF),
            sds((width, width), BF),
            sds((1, entries), F32),
            sds(proj_shape, BF),
            sds(proj_shape[::-1], BF),
        ],
        blocks,
        in_specs=[pl.BlockSpec(memory_space=pl.ANY)] * 16,
        scratch=[
            pltpu.VMEM((2, slots, fsdp, tall, wide), BF),
            pltpu.VMEM(proj_shape, F32),
            pltpu.SemaphoreType.DMA((32,)),
        ],
        place=place,
    )


def up_whole_kernel(slots, place, *refs):
    blocks, result, sems = refs[:16], refs[16], refs[17]
    fetch_blocks(place, blocks, result, sems, slots, lambda f, z, c: (f, 2 * z + c))


def up_whole(place, blocks, fsdp, slots):
    rows, wide = blocks[0].shape[1:]
    result = call(
        functools.partial(up_whole_kernel, slots),
        "whole_up",
        sds((fsdp, 2 * slots, rows, wide), BF),
        blocks,
        in_specs=[pl.BlockSpec(memory_space=pl.ANY)] * 16,
        scratch=[pltpu.SemaphoreType.DMA((32,))],
        place=place,
    )
    return result.reshape(fsdp, 2 * slots * rows, wide)


def down_whole_kernel(slots, fsdp, place, *refs):
    blocks, result, work, sems = refs[:16], refs[16], refs[17], refs[18]
    fetch_blocks(place, blocks, work, sems, slots, lambda f, z, c: (c, z, f))
    rows, wide = work.shape[3:]
    thin = result.shape[1] // fsdp
    count = wide // thin
    for z in range(slots):
        for c in range(2):
            for g in range(count):
                top = (2 * z + c) * count * rows + g * rows
                for f in range(fsdp):
                    result[top : top + rows, f * thin : (f + 1) * thin] = work[
                        c, z, f, :, g * thin : (g + 1) * thin
                    ]


def down_whole(place, blocks, fsdp, slots, hidden, width):
    rows, wide = blocks[0].shape[1:]
    return call(
        functools.partial(down_whole_kernel, slots, fsdp),
        "whole_down",
        sds((hidden, width), BF),
        blocks,
        in_specs=[pl.BlockSpec(memory_space=pl.ANY)] * 16,
        scratch=[
            pltpu.VMEM((2, slots, fsdp, rows, wide), BF),
            pltpu.SemaphoreType.DMA((32,)),
        ],
        place=place,
    )


def added(*parts):
    total = parts[0].astype(F32)
    for p in parts[1:]:
        total = total + p.astype(F32)
    return total


def reduce_piece(mine, theirs):
    came = swap_core(theirs)

    def chip(rel, lo, hi):
        return added(mine[rel, lo:hi], came[rel, lo:hi])

    def pair(a, b, lo, hi):
        return jnp.stack([chip(a, lo, hi), chip(b, lo, hi)]).astype(BF)

    from_x = swap_fsdp(pair(1, 3, 0, 2), 1)
    from_y = swap_fsdp(pair(2, 3, 2, 4), 2)
    over_y = swap_fsdp((chip(2, 0, 2) + from_x[1].astype(F32)).astype(BF), 2)
    over_x = swap_fsdp((chip(1, 2, 4) + from_y[1].astype(F32)).astype(BF), 1)
    near = chip(0, 0, 2) + from_x[0].astype(F32) + over_y.astype(F32)
    far = chip(0, 2, 4) + from_y[0].astype(F32) + over_x.astype(F32)
    one = shift_slot(near[1].astype(BF), 1)
    two = shift_slot(far[0].astype(BF), 2)
    three = shift_slot(far[1].astype(BF), 3)
    return (near[0] + two.astype(F32)) + (one.astype(F32) + three.astype(F32))


def sum_everywhere(value):
    a, b, c = (swap_fsdp(value, k) for k in (1, 2, 3))
    value = (value + a) + (b + c)
    a, b, c = (shift_slot(value, k) for k in (1, 2, 3))
    value = (value + b) + (a + c)
    return value + swap_core(value)


def adam(weight, moment, second, grad, scale_clip, rate, decay):
    clipped = grad * scale_clip
    new_moment = BETA_ONE * moment + (1.0 - BETA_ONE) * clipped
    new_second = BETA_TWO * second + (1.0 - BETA_TWO) * clipped * clipped
    moment_hat = new_moment / (1.0 - BETA_ONE**STEP)
    second_hat = new_second / (1.0 - BETA_TWO**STEP)
    new_weight = weight - rate * (moment_hat / (jnp.sqrt(second_hat) + ADAM_EPS) + decay * weight)
    return new_weight, new_moment, new_second, new_weight.astype(BF)


def update_kernel(rates, squares, g_first, g_up, g_down, *refs):
    ins, outs = refs[:18], refs[18:-1]
    norm_ref, outs = outs[0], outs[1:]
    vector = refs[-1]
    norm = jnp.sqrt(squares[0:1, 0:1])
    norm_ref[...] = norm
    clip = jnp.minimum(1.0, CLIP_NORM / norm)

    def put(n, place, grad):
        new = adam(*(ins[3 * n + i][place] for i in range(3)), grad, clip, *rates[n])
        for i in range(4):
            outs[4 * n + i][place] = new[i]

    rows, wide = g_up.shape
    piece = ins[0].shape[1]
    every = (slice(None), slice(None))
    put(0, every, g_first[:rows, :piece])
    put(1, every, g_first[:rows, piece:])
    put(2, every, g_up[...])
    thin = ins[9].shape[1]
    for g in range(wide // thin):
        put(3, (slice(g * rows, (g + 1) * rows), slice(None)), g_down[:, g * thin : (g + 1) * thin])
    height, across = ins[12].shape
    for g in range(height // 8):
        put(
            4,
            (slice(8 * g, 8 * g + 8), slice(None)),
            g_first[rows : rows + 8, g * across : (g + 1) * across],
        )
    start = (height // 8) * across
    room = wide - start
    entries = ins[15].shape[1]
    vector[:, :room] = g_first[rows : rows + 1, start:]
    vector[:, room:] = g_first[rows + 1 : rows + 2, start : start + entries - room]
    put(5, every, vector[...])


def update(squares, g_first, g_up, g_down, states, rates):
    outs = [sds((1, 1), F32)]
    for n in range(6):
        shape = states[3 * n].shape
        outs += [sds(shape, F32)] * 3 + [sds(shape, BF)]
    return call(
        functools.partial(update_kernel, rates),
        "update",
        outs,
        (squares, g_first, g_up, g_down, *states),
        scratch=[pltpu.VMEM(states[15].shape, F32)],
    )


def on_device(
    tokens,
    cotangent,
    positions,
    counts,
    qkv_weight,
    qkv_moment,
    qkv_second,
    out_weight,
    out_moment,
    out_second,
    up_weight,
    up_moment,
    up_second,
    down_projection_weight,
    down_moment,
    down_second,
    proj_weight,
    proj_moment,
    proj_second,
    vec_weight,
    vec_moment,
    vec_second,
):
    fsdp, slots = lax.axis_size("fsdp"), lax.axis_size("dp") // 2
    place = jnp.stack(
        [lax.axis_index("fsdp"), lax.axis_index("dp") // 2, lax.axis_index("dp") % 2]
    ).astype(jnp.int32)
    seqs = counts.shape[0]
    rows, width = tokens.shape
    length = rows // seqs
    half = length // 2
    marked = positions.shape[1]
    hidden = down_projection_weight.shape[0] * slots * 2
    proj_shape = (proj_weight.shape[0] * fsdp, proj_weight.shape[1] * 2 * slots)
    entries = vec_weight.shape[0] * fsdp * 2 * slots
    rates = (
        (RATE_QKV, DECAY_RATE),
        (RATE_OUT, DECAY_RATE),
        (RATE_UP, DECAY_RATE),
        (RATE_DOWN, DECAY_RATE),
        (RATE_PROJ, DECAY_RATE),
        (RATE_VEC, 0.0),
    )

    row = tuple(v[None, :] for v in (vec_weight, vec_moment, vec_second))
    own_first, own_up, own_down = pack(
        qkv_weight, out_weight, up_weight, down_projection_weight, proj_weight, row[0]
    )
    blocks_first = gather_piece(own_first)
    blocks_up = gather_piece(own_up)
    blocks_down = gather_piece(own_down)

    x = tokens.reshape(seqs, length, width)
    front, rest, frontt, xt, back = order_rows(x, positions)
    live = jnp.arange(marked, dtype=jnp.int32)[None, :] < counts[:, None]
    dy = jnp.pad(
        jnp.where(live[:, :, None], cotangent, jnp.zeros_like(cotangent)),
        ((0, 0), (0, half - marked), (0, 0)),
    ).reshape(seqs * half, width)

    qkv_full, out_full, vec, proj, projt = first_whole(
        place, blocks_first, fsdp, slots, width, proj_shape, entries
    )
    q_front, q_rest, kv, kvp = make_qkv(front, rest, x, qkv_full, vec, proj)
    a_front, a_rest = attend(q_front, q_rest, kvp)

    m1 = 3 * width
    m2 = m1 + width
    m3 = m2 + hidden
    m4 = m3 + width
    ends = [m4 + i * width for i in range(5)]
    marks_one = ((m1, m2), (ends[0], ends[1]), (ends[1], ends[2]))
    marks_two = ((m3, m4), (ends[2], ends[3]), (ends[3], ends[4]))

    def flat(v):
        return v.reshape(seqs * half, width)

    h_front, low_front, kept, lowt, attendedt = join(
        flat(a_front), flat(front), out_full, vec, marks_one, True
    )
    h_rest, low_rest = join(flat(a_rest), flat(rest), out_full, vec, marks_one, False)
    up_full = up_whole(place, blocks_up, fsdp, slots)
    act_front, slope, activet = lift(low_front, up_full, vec, m2, True)
    act_rest = lift(low_rest, up_full, vec, m2, False)[0]
    down_full = down_whole(place, blocks_down, fsdp, slots, hidden, width)
    out_front, d_sum, d_low, two_sums = lower(act_front, h_front, down_full, vec, marks_two, dy)

    theirs = grad_down(place, activet, d_low, 1, fsdp, slots)
    mine = grad_down(place, activet, d_low, 0, fsdp, slots)
    g_down = reduce_piece(mine, theirs)
    d_hidden, up_sums = hidden_back(d_low, down_full, slope)
    theirs = grad_up(place, lowt, d_hidden, 1, fsdp, slots)
    mine = grad_up(place, lowt, d_hidden, 0, fsdp, slots)
    g_up = reduce_piece(mine, theirs)
    d_first, d_first_low, d_attended, one_sums = first_back(
        d_hidden, up_full, d_sum, kept, vec, out_full, (ends[0], ends[1])
    )
    d_q, d_k, d_v, q_sums = attend_back(q_front, kvp, d_attended.reshape(seqs, half, width))
    d_kv, d_proj, kv_sums = spread(d_k, d_v, kv, projt)
    sums = (q_sums, kv_sums, one_sums, up_sums, two_sums)
    give = (
        xt,
        frontt,
        attendedt,
        flat(d_q),
        d_kv.reshape(rows, 2 * width),
        d_first_low,
        d_proj,
        sums,
    )
    theirs = grad_rest(place, *give, 1, fsdp, slots)
    mine = grad_rest(place, *give, 0, fsdp, slots)
    g_first = reduce_piece(mine, theirs)

    out_rest = lower(act_rest, h_rest, down_full, vec, marks_two)
    output = restore(
        out_front.reshape(seqs, half, width), out_rest.reshape(seqs, half, width), back
    ).reshape(rows, width)
    grad_input = input_back(
        d_kv, d_q, d_first.reshape(seqs, half, width), qkv_full, back
    ).reshape(rows, width)

    squares = jnp.sum(g_first * g_first) + jnp.sum(g_up * g_up) + jnp.sum(g_down * g_down)
    squares = sum_everywhere(jnp.broadcast_to(squares, (8, 128)))
    states = (
        qkv_weight,
        qkv_moment,
        qkv_second,
        out_weight,
        out_moment,
        out_second,
        up_weight,
        up_moment,
        up_second,
        down_projection_weight,
        down_moment,
        down_second,
        proj_weight,
        proj_moment,
        proj_second,
        *row,
    )
    new = update(squares, g_first, g_up, g_down, states, rates)
    norm, new = new[0].reshape(()), new[1:]
    return (output, grad_input, norm, *new[:20], *(v[0] for v in new[20:]))


def split_up(value, dim, peers):
    dims = value.shape
    blocks = value.reshape(*dims[:dim], peers, dims[dim] // peers, *dims[dim + 1 :])
    return jnp.moveaxis(blocks, dim, 0)


def sum_at_owner(value, axis, dim):
    blocks = split_up(value, dim, lax.axis_size(axis))
    arrived = lax.all_to_all(blocks, axis, split_axis=0, concat_axis=0, tiled=True)
    return arrived.astype(jnp.float32).sum(axis=0)


def side_by_side(arrays, axis, dim, along):
    ends, at = ([], 0)
    for a in arrays[:-1]:
        at += a.shape[along]
        ends.append(at)
    both = jnp.concatenate(arrays, axis=along)
    return tuple(jnp.split(sum_at_owner(both, axis, dim), ends, axis=along))


def layer_norm(summed, gains, shifts):
    average = jnp.mean(summed, axis=-1, keepdims=True)
    centered = summed - average
    variance = jnp.mean(centered * centered, axis=-1, keepdims=True)
    return centered * lax.rsqrt(variance + NORM_EPS) * gains + shifts


def norm_back(summed, gains, shifts, grad_out):
    result, pullback = jax.vjp(layer_norm, summed, gains, shifts)
    return pullback(grad_out)


def gelu_exact(values):
    return jax.nn.gelu(values, approximate=False)


def split_vector(vec_full, model_width, hidden_width):
    mark_one = 3 * model_width
    mark_two = mark_one + model_width
    mark_three = mark_two + hidden_width
    mark_four = mark_three + model_width
    return (
        vec_full[:mark_one],
        vec_full[mark_one:mark_two],
        vec_full[mark_two:mark_three],
        vec_full[mark_three:mark_four],
        vec_full[mark_four : mark_four + model_width],
        vec_full[mark_four + model_width : mark_four + 2 * model_width],
        vec_full[mark_four + 2 * model_width : mark_four + 3 * model_width],
        vec_full[mark_four + 3 * model_width : mark_four + 4 * model_width],
    )


def adam_update(weight, moment, second, grad, scale_clip, rate, decay):
    clipped = grad * scale_clip
    new_moment = BETA_ONE * moment + (1.0 - BETA_ONE) * clipped
    new_second = BETA_TWO * second + (1.0 - BETA_TWO) * clipped * clipped
    moment_hat = new_moment / (1.0 - BETA_ONE**STEP)
    second_hat = new_second / (1.0 - BETA_TWO**STEP)
    new_weight = weight - rate * (moment_hat / (jnp.sqrt(second_hat) + ADAM_EPS) + decay * weight)
    return (new_weight, new_moment, new_second, new_weight.astype(jnp.bfloat16))


def fetch_whole(low_qkv, low_out, low_up, low_down, low_proj, low_vec):
    rows = (
        lax.all_gather(low_qkv, "dp", axis=0, tiled=True),
        lax.all_gather(low_out, "dp", axis=0, tiled=True),
        lax.all_gather(low_up, "dp", axis=0, tiled=True),
        lax.all_gather(low_down, "dp", axis=0, tiled=True),
        lax.all_gather(low_proj, "dp", axis=1, tiled=True),
        lax.all_gather(low_vec, "dp", axis=0, tiled=True),
    )
    return (
        lax.all_gather(rows[0], "fsdp", axis=1, tiled=True),
        lax.all_gather(rows[1], "fsdp", axis=1, tiled=True),
        lax.all_gather(rows[2], "fsdp", axis=1, tiled=True),
        lax.all_gather(rows[3], "fsdp", axis=1, tiled=True),
        lax.all_gather(rows[4], "fsdp", axis=0, tiled=True),
        lax.all_gather(rows[5], "fsdp", axis=0, tiled=True),
    )


def on_any_mesh(
    tokens,
    cotangent,
    positions,
    counts,
    qkv_weight,
    qkv_moment,
    qkv_second,
    out_weight,
    out_moment,
    out_second,
    up_weight,
    up_moment,
    up_second,
    down_projection_weight,
    down_moment,
    down_second,
    proj_weight,
    proj_moment,
    proj_second,
    vec_weight,
    vec_moment,
    vec_second,
):
    low_qkv = qkv_weight.astype(jnp.bfloat16)
    low_out = out_weight.astype(jnp.bfloat16)
    low_up = up_weight.astype(jnp.bfloat16)
    low_down = down_projection_weight.astype(jnp.bfloat16)
    low_proj = proj_weight.astype(jnp.bfloat16)
    low_vec = vec_weight.astype(jnp.bfloat16)
    qkv_full, out_full, up_full, down_full, projection_gathered, vec_full = fetch_whole(
        low_qkv, low_out, low_up, low_down, low_proj, low_vec
    )
    seq_count = counts.shape[0]
    row_count = tokens.shape[0]
    seq_length = row_count // seq_count
    model_width = tokens.shape[1]
    head_width = model_width // HEADS
    hidden_width = vec_full.shape[0] - 9 * model_width
    proj_rows = projection_gathered.shape[0]
    score_scale = head_width ** (-0.5)
    bias_qkv, bias_out, bias_up, bias_down, gain_one, shift_one, gain_two, shift_two = split_vector(
        vec_full.astype(jnp.float32), model_width, hidden_width
    )
    pre_qkv = jnp.dot(tokens, qkv_full, preferred_element_type=jnp.float32)
    qkv_low = (pre_qkv + bias_qkv).astype(jnp.bfloat16)
    queries = qkv_low[:, :model_width].reshape(seq_count, seq_length, HEADS, head_width)
    key_value_pair = qkv_low[:, model_width:].reshape(seq_count, seq_length, 2 * model_width)
    projected = jnp.einsum(
        "bu,vur->vbr", projection_gathered, key_value_pair, preferred_element_type=jnp.float32
    ).astype(jnp.bfloat16)
    key_heads = projected[:, :, :model_width].reshape(seq_count, proj_rows, HEADS, head_width)
    value_heads = projected[:, :, model_width:].reshape(seq_count, proj_rows, HEADS, head_width)
    scores = (
        jnp.einsum("slhe,sjhe->shlj", queries, key_heads, preferred_element_type=jnp.float32)
        * score_scale
    )
    peak = jnp.max(scores, axis=-1, keepdims=True)
    log_total = peak + jnp.log(jnp.sum(jnp.exp(scores - peak), axis=-1, keepdims=True))
    soft_low = jnp.exp(scores - log_total).astype(jnp.bfloat16)
    context = jnp.einsum(
        "shlj,sjhe->slhe", soft_low, value_heads, preferred_element_type=jnp.float32
    )
    attended = context.reshape(row_count, model_width).astype(jnp.bfloat16)
    first_sum = (
        tokens.astype(jnp.float32)
        + jnp.dot(attended, out_full, preferred_element_type=jnp.float32)
        + bias_out
    )
    normed_one = layer_norm(first_sum, gain_one, shift_one)
    normed_low = normed_one.astype(jnp.bfloat16)
    hidden_pre = jnp.dot(normed_low, up_full, preferred_element_type=jnp.float32) + bias_up
    active = gelu_exact(hidden_pre).astype(jnp.bfloat16)
    second_sum = (
        normed_one + jnp.dot(active, down_full, preferred_element_type=jnp.float32) + bias_down
    )
    output = layer_norm(second_sum, gain_two, shift_two).astype(jnp.bfloat16)
    slot_live = jnp.arange(positions.shape[1], dtype=jnp.int32)[None, :] < counts[:, None]
    one_hot_rows = (
        (positions[:, :, None] == jnp.arange(seq_length, dtype=jnp.int32)[None, None, :])
        & slot_live[:, :, None]
    ).astype(jnp.bfloat16)
    dense = jnp.einsum(
        "bej,bef->bjf", one_hot_rows, cotangent, preferred_element_type=jnp.float32
    ).reshape(row_count, model_width)
    qkv_full, out_full, up_full, down_full, projection_gathered, vec_full = fetch_whole(
        low_qkv, low_out, low_up, low_down, low_proj, low_vec
    )
    d_second, d_gain_two, d_shift_two = norm_back(second_sum, gain_two, shift_two, dense)
    d_bias_down = jnp.sum(d_second, axis=0)
    d_second_low = d_second.astype(jnp.bfloat16)
    grad_down = jnp.einsum("rf,rd->fd", active, d_second_low, preferred_element_type=jnp.float32)
    d_active = jnp.einsum("rd,fd->rf", d_second_low, down_full, preferred_element_type=jnp.float32)
    gelu_value, gelu_pull = jax.vjp(gelu_exact, hidden_pre)
    d_hidden = gelu_pull(d_active)[0]
    d_bias_up = jnp.sum(d_hidden, axis=0)
    d_hidden_low = d_hidden.astype(jnp.bfloat16)
    grad_up = jnp.einsum("rd,rf->df", normed_low, d_hidden_low, preferred_element_type=jnp.float32)
    d_normed = d_second + jnp.einsum(
        "rf,df->rd", d_hidden_low, up_full, preferred_element_type=jnp.float32
    )
    d_first, d_gain_one, d_shift_one = norm_back(first_sum, gain_one, shift_one, d_normed)
    d_bias_out = jnp.sum(d_first, axis=0)
    d_first_low = d_first.astype(jnp.bfloat16)
    grad_out = jnp.einsum("rd,re->de", attended, d_first_low, preferred_element_type=jnp.float32)
    d_attended = jnp.einsum("re,de->rd", d_first_low, out_full, preferred_element_type=jnp.float32)
    d_attended = d_attended.astype(jnp.bfloat16).reshape(seq_count, seq_length, HEADS, head_width)
    scores_again = (
        jnp.einsum("slhe,sjhe->shlj", queries, key_heads, preferred_element_type=jnp.float32)
        * score_scale
    )
    probs_again = jnp.exp(scores_again - log_total)
    probs_low = probs_again.astype(jnp.bfloat16)
    d_value_heads = jnp.einsum(
        "shlj,slhe->sjhe", probs_low, d_attended, preferred_element_type=jnp.float32
    )
    d_probs = jnp.einsum(
        "slhe,sjhe->shlj", d_attended, value_heads, preferred_element_type=jnp.float32
    )
    d_scores = probs_again * (d_probs - jnp.sum(probs_again * d_probs, axis=-1, keepdims=True))
    d_raw_low = (d_scores * score_scale).astype(jnp.bfloat16)
    d_queries = jnp.einsum(
        "shlj,sjhe->slhe", d_raw_low, key_heads, preferred_element_type=jnp.float32
    ).reshape(row_count, model_width)
    d_key_heads = jnp.einsum(
        "shlj,slhe->sjhe", d_raw_low, queries, preferred_element_type=jnp.float32
    )
    projected_gradient = jnp.concatenate(
        [
            d_key_heads.reshape(seq_count, proj_rows, model_width),
            d_value_heads.reshape(seq_count, proj_rows, model_width),
        ],
        axis=-1,
    ).astype(jnp.bfloat16)
    d_kv = jnp.einsum(
        "cq,uct->uqt", projection_gathered, projected_gradient, preferred_element_type=jnp.float32
    ).reshape(row_count, 2 * model_width)
    projection_gradient = jnp.einsum(
        "nhy,nxy->hx", projected_gradient, key_value_pair, preferred_element_type=jnp.float32
    )
    d_qkv = jnp.concatenate([d_queries, d_kv], axis=-1)
    d_bias_qkv = jnp.sum(d_qkv, axis=0)
    d_qkv_low = d_qkv.astype(jnp.bfloat16)
    grad_qkv = jnp.einsum("rd,re->de", tokens, d_qkv_low, preferred_element_type=jnp.float32)
    grad_input = (
        d_first + jnp.einsum("re,de->rd", d_qkv_low, qkv_full, preferred_element_type=jnp.float32)
    ).astype(jnp.bfloat16)
    grad_vec = jnp.concatenate(
        [
            d_bias_qkv,
            d_bias_out,
            d_bias_up,
            d_bias_down,
            d_gain_one,
            d_shift_one,
            d_gain_two,
            d_shift_two,
        ]
    )
    col_part = (
        lax.psum_scatter(
            grad_qkv.astype(jnp.bfloat16), "fsdp", scatter_dimension=1, tiled=True
        ).astype(jnp.float32),
        lax.psum_scatter(
            grad_out.astype(jnp.bfloat16), "fsdp", scatter_dimension=1, tiled=True
        ).astype(jnp.float32),
        lax.psum_scatter(
            grad_up.astype(jnp.bfloat16), "fsdp", scatter_dimension=1, tiled=True
        ).astype(jnp.float32),
        lax.psum_scatter(
            grad_down.astype(jnp.bfloat16), "fsdp", scatter_dimension=1, tiled=True
        ).astype(jnp.float32),
        lax.psum_scatter(
            projection_gradient.astype(jnp.bfloat16), "fsdp", scatter_dimension=0, tiled=True
        ).astype(jnp.float32),
        lax.psum_scatter(
            grad_vec.astype(jnp.bfloat16), "fsdp", scatter_dimension=0, tiled=True
        ).astype(jnp.float32),
    )
    owned = (
        *side_by_side(
            (
                col_part[0].astype(jnp.bfloat16),
                col_part[1].astype(jnp.bfloat16),
                col_part[2].astype(jnp.bfloat16),
            ),
            "dp",
            0,
            1,
        ),
        sum_at_owner(col_part[3].astype(jnp.bfloat16), "dp", 0),
        sum_at_owner(col_part[4].astype(jnp.bfloat16), "dp", 1),
        sum_at_owner(col_part[5].astype(jnp.bfloat16), "dp", 0),
    )
    owned_qkv, owned_out, owned_up, owned_down, owned_proj, owned_vec = owned
    local_squares = (
        jnp.sum(owned_qkv * owned_qkv)
        + jnp.sum(owned_out * owned_out)
        + jnp.sum(owned_up * owned_up)
        + jnp.sum(owned_down * owned_down)
        + jnp.sum(owned_proj * owned_proj)
        + jnp.sum(owned_vec * owned_vec)
    )
    all_squares = lax.psum(local_squares, ("fsdp", "dp"))
    grad_norm = jnp.sqrt(all_squares)
    scale_clip = jnp.minimum(1.0, CLIP_NORM / grad_norm)
    qkv_parts = adam_update(
        qkv_weight, qkv_moment, qkv_second, owned_qkv, scale_clip, RATE_QKV, DECAY_RATE
    )
    out_parts = adam_update(
        out_weight, out_moment, out_second, owned_out, scale_clip, RATE_OUT, DECAY_RATE
    )
    up_parts = adam_update(
        up_weight, up_moment, up_second, owned_up, scale_clip, RATE_UP, DECAY_RATE
    )
    down_parts = adam_update(
        down_projection_weight,
        down_moment,
        down_second,
        owned_down,
        scale_clip,
        RATE_DOWN,
        DECAY_RATE,
    )
    proj_parts = adam_update(
        proj_weight, proj_moment, proj_second, owned_proj, scale_clip, RATE_PROJ, DECAY_RATE
    )
    vec_parts = adam_update(
        vec_weight, vec_moment, vec_second, owned_vec, scale_clip, RATE_VEC, 0.0
    )
    return (
        output,
        grad_input,
        grad_norm,
        qkv_parts[0],
        qkv_parts[1],
        qkv_parts[2],
        qkv_parts[3],
        out_parts[0],
        out_parts[1],
        out_parts[2],
        out_parts[3],
        up_parts[0],
        up_parts[1],
        up_parts[2],
        up_parts[3],
        down_parts[0],
        down_parts[1],
        down_parts[2],
        down_parts[3],
        proj_parts[0],
        proj_parts[1],
        proj_parts[2],
        proj_parts[3],
        vec_parts[0],
        vec_parts[1],
        vec_parts[2],
        vec_parts[3],
    )


def solution(mesh):
    matrix = P("dp", "fsdp")
    tall = P("fsdp", "dp")
    every = P(("fsdp", "dp"))
    small = mesh.shape["fsdp"] == 4 and mesh.shape["dp"] == 8
    return jax.shard_map(
        on_device if small else on_any_mesh,
        mesh=mesh,
        in_specs=(every,) * 4 + (matrix,) * 12 + (tall,) * 3 + (every,) * 3,
        out_specs=(every, every, P()) + (matrix,) * 16 + (tall,) * 4 + (every,) * 4,
        check_vma=False,
    )
```

```python
import functools
import math

import jax
import jax.numpy as jnp
from jax import lax
from jax.experimental import pallas as pl
from jax.experimental.pallas import tpu as pltpu
from jax.sharding import PartitionSpec as P

HEADS = 12
STEP = 10
NORM_EPS = 1e-05
CLIP_NORM = 1.0
BETA_ONE = 0.9
BETA_TWO = 0.999
ADAM_EPS = 1e-08
DECAY_RATE = 0.01
RATE_QKV = 0.05
RATE_OUT = 0.4
RATE_UP = 0.05
RATE_DOWN = 0.05
RATE_PROJ = 0.05
RATE_VEC = 1.0

BF = jnp.bfloat16
F32 = jnp.float32
LOG2E = math.log2(math.e)
MIB = 1 << 20


def nn(a, b):
    return jnp.dot(a, b, preferred_element_type=F32)


def nt(a, b):
    return lax.dot_general(a, b, (((1,), (1,)), ((), ())), preferred_element_type=F32)


def sds(shape, dtype):
    return jax.ShapeDtypeStruct(tuple(shape), dtype)


def call(
    kernel, name, out_shape, args, scratch=(), place=None, flops=0, vmem=16, space=pltpu.VMEM, alias=()
):
    many = isinstance(out_shape, (list, tuple))
    outs = list(out_shape) if many else [out_shape]
    specs = [pl.BlockSpec(memory_space=space)] * len(args)
    if place is not None:
        args = (place, *args)
        specs = [pl.BlockSpec(memory_space=pltpu.SMEM), *specs]
    moved = sum(math.prod(a.shape) * jnp.dtype(a.dtype).itemsize for a in (*args, *outs))
    result = pl.pallas_call(
        kernel,
        name=name,
        out_shape=outs,
        in_specs=specs,
        out_specs=[pl.BlockSpec(memory_space=pltpu.VMEM)] * len(outs),
        scratch_shapes=list(scratch),
        input_output_aliases=dict(alias),
        cost_estimate=pl.CostEstimate(
            flops=int(flops) // 1000, bytes_accessed=int(moved) // 1000, transcendentals=0
        ),
        compiler_params=pltpu.CompilerParams(vmem_limit_bytes=vmem * MIB),
    )(*args)
    return result if many else result[0]


def lanes(start, size):
    return pl.ds(pl.multiple_of(start, 128), size)


def lines(start, size):
    return pl.ds(pl.multiple_of(start, 16), size)


def norm_stats(summed):
    average = jnp.mean(summed, axis=-1, keepdims=True)
    centered = summed - average
    variance = jnp.mean(centered * centered, axis=-1, keepdims=True)
    inverse = lax.rsqrt(variance + NORM_EPS)
    return centered * inverse, inverse


def norm_grad(shaped, inverse, gains, grad):
    inner = grad * gains
    first = jnp.mean(inner, axis=-1, keepdims=True)
    second = jnp.mean(inner * shaped, axis=-1, keepdims=True)
    return inverse * (inner - first - shaped * second)


def normal_parts(values):
    size = jnp.abs(values)
    base = 1.0 + (0.3275911 * math.sqrt(0.5)) * size
    t = pl.reciprocal(base, approx=True)
    t = t * (2.0 - base * t)
    bell = jnp.exp2(values * values * (-0.5 * LOG2E))
    poly = 0.5 * 1.061405429
    for c in (-1.453152027, 1.421413741, -0.284496736, 0.254829592):
        poly = poly * t + 0.5 * c
    tail = poly * t * bell
    return bell, jnp.where(values >= 0.0, 1.0 - tail, tail)


def lanes_below(width):
    return lax.broadcasted_iota(jnp.int32, (1, 2 * width), 1) < width


def swap_halves(value):
    width = value.shape[1] // 2
    return jnp.concatenate([value[:, width:], value[:, :width]], axis=1)


def pack_kernel(place, *refs):
    given, (own, a_ref, bc_ref), (small, sems), held = refs[:6], refs[6:9], refs[9:11], refs[11:]
    copies = [pltpu.make_async_copy(a, b, sems.at[i]) for i, (a, b) in enumerate(zip(given, held))]
    for copy in copies:
        copy.start()
    for copy in copies:
        copy.wait()
    qkv, out, up, down, proj, vec = held
    vec = vec[...].reshape(1, vec.shape[0])
    odd = (place[0] & 1) == 1
    rows, wide = up.shape
    tile = 128
    half = tile // 2
    full = qkv.shape[1] - half
    after = full + tile
    q, o = qkv[...], out[...]

    def pick(one, two):
        return jnp.where(odd, one, two).astype(BF)

    a_ref[:rows, :full] = pick(q[:, half:], q[:, :full])
    a_ref[:rows, full : full + half] = pick(o[:, :half], q[:, full:])
    a_ref[:rows, full + half : after] = pick(q[:, :half], o[:, tile:])
    a_ref[:rows, after:] = pick(o[:, half:], o[:, :tile])
    small[...] = jnp.zeros_like(small)
    height, width = proj.shape
    for g in range(height // 8):
        small[0:8, g * width : (g + 1) * width] = proj[8 * g : 8 * g + 8, :]
    start = (height // 8) * width
    room = wide - start
    small[0:1, start:] = vec[:, :room]
    left = vec.shape[1] - room
    small[1:2, start : start + left] = vec[:, room:]
    a_ref[rows:, :] = small[...].astype(BF)
    bc_ref[:rows, :] = up[...].astype(BF)
    across = down.shape[1]
    for h in range(down.shape[0] // rows):
        bc_ref[rows:, h * across : (h + 1) * across] = down[rows * h : rows * (h + 1), :].astype(BF)
    tall = a_ref.shape[0]
    own[:tall, :] = a_ref[...]
    own[tall:, :] = bc_ref[...]


def pack(place, *given):
    rows, wide = given[2].shape
    tall = rows + 16
    return call(
        pack_kernel,
        "pack_weights",
        [sds((tall + 2 * rows, wide), BF), sds((tall, wide), BF), sds((2 * rows, wide), BF)],
        given,
        scratch=[
            pltpu.VMEM((16, wide), F32),
            pltpu.SemaphoreType.DMA((len(given),)),
            *(pltpu.VMEM(a.shape, F32) for a in given),
        ],
        place=place,
        space=pltpu.HBM,
    )


def split_cores(place, value, rows, mine, theirs, cols):
    first = place[2] == 0
    for z in range(value.shape[0] // (2 * rows)):
        one = value[2 * z * rows : (2 * z + 1) * rows]
        two = value[(2 * z + 1) * rows : (2 * z + 2) * rows]
        mine[z * rows : (z + 1) * rows, cols] = jnp.where(first, one, two)
        theirs[z * rows : (z + 1) * rows, cols] = jnp.where(first, two, one)


def order_kernel(
    marked, rows, place, pos, x, front, rest, frontt, frontt_other, xt, xt_other, back
):
    seqs, length, _ = x.shape
    half = front.shape[1]
    col = lax.broadcasted_iota(jnp.int32, (half, length), 1)
    row = lax.broadcasted_iota(jnp.int32, (half, length), 0)
    before = (
        lax.broadcasted_iota(jnp.int32, (length, length), 0)
        < lax.broadcasted_iota(jnp.int32, (length, length), 1)
    ).astype(BF)
    for s in range(seqs):
        hot = (pos[s] == col) & (row < marked)
        free = 1.0 - jnp.sum(hot.astype(F32), axis=0, keepdims=True)
        rank = nn(jnp.broadcast_to(free, (16, length)).astype(BF), before)[0:1, :]
        target = jnp.where(free > 0.5, rank.astype(jnp.int32) + marked, -1)
        one = jnp.where(hot | (target == row), 1.0, 0.0)
        two = jnp.where(target == (row + half), 1.0, 0.0)
        values = x[s]
        head = nn(one.astype(BF), values)
        front[s] = head.astype(BF)
        rest[s] = nn(two.astype(BF), values).astype(BF)
        at = slice(s * half, (s + 1) * half)
        split_cores(place, head.T.astype(BF), rows, frontt, frontt_other, at)
        at = slice(s * length, (s + 1) * length)
        split_cores(place, values.T, rows, xt, xt_other, at)
        back[s, :, :half] = one.T.astype(BF)
        back[s, :, half:] = two.T.astype(BF)


def order_rows(place, tokens, positions, slots):
    seqs, length, width = tokens.shape
    marked = positions.shape[1]
    half = length // 2
    pos = jnp.pad(positions, ((0, 0), (0, half - marked)), constant_values=-1)[:, :, None]
    rows = sds((seqs, half, width), BF)
    front = sds((width // 2, seqs * half), BF)
    every = sds((width // 2, seqs * length), BF)
    return call(
        functools.partial(order_kernel, marked, width // (2 * slots)),
        "order_rows",
        [rows, rows, front, front, every, every, sds((seqs, length, length), BF)],
        (pos, tokens),
        place=place,
        flops=2 * seqs * length * length * width,
    )


def qkv_kernel(front, rest, x, weight, vec, proj, q_front, q_rest, kv, kvp):
    seqs, _, width = front.shape
    piece = width // 2
    for s in range(seqs):
        for j in range(2):
            cols = slice(j * piece, (j + 1) * piece)
            w = weight[:, cols]
            bias = vec[:, cols]
            q_front[s, :, cols] = (nn(front[s], w) + bias).astype(BF)
            q_rest[s, :, cols] = (nn(rest[s], w) + bias).astype(BF)
        for j in range(4):
            cols = slice(j * piece, (j + 1) * piece)
            at = slice(width + j * piece, width + (j + 1) * piece)
            part = (nn(x[s], weight[:, at]) + vec[:, at]).astype(BF)
            kv[s, :, cols] = part
            kvp[s, :, cols] = nn(proj[...], part).astype(BF)


def make_qkv(front, rest, x, weight, vec, proj):
    seqs, half, width = front.shape
    length = x.shape[1]
    rows = proj.shape[0]
    return call(
        qkv_kernel,
        "make_qkv",
        [
            sds(front.shape, BF),
            sds(front.shape, BF),
            sds((seqs, length, 2 * width), BF),
            sds((seqs, rows, 2 * width), BF),
        ],
        (front, rest, x, weight, vec, proj),
        flops=2 * seqs * length * width * width * 3 + 2 * seqs * rows * length * 2 * width,
    )


def attend_kernel(head, q_front, q_rest, kvp, o_front, o_rest):
    seqs, _, width = q_front.shape
    below = lanes_below(head)
    factor = LOG2E / math.sqrt(head)

    def pair(p, carry):
        at = lanes(p * 2 * head, 2 * head)
        for s in range(seqs):
            k, v = kvp[s, :, at], kvp[s, :, lanes(width + p * 2 * head, 2 * head)]
            zero = jnp.zeros_like(k)
            heads = [(jnp.where(own, k, zero), jnp.where(own, v, zero)) for own in (below, ~below)]
            for q_ref, o_ref in ((q_front, o_front), (q_rest, o_rest)):
                q = q_ref[s, :, at]
                total = None
                for kh, vh in heads:
                    scores = nt(q, kh)
                    e = jnp.exp2((scores - jnp.max(scores, axis=-1, keepdims=True)) * factor)
                    scale = 1.0 / jnp.sum(e, axis=-1, keepdims=True)
                    part = nn(e.astype(BF), vh) * scale
                    total = part if total is None else total + part
                o_ref[s, :, at] = total.astype(BF)
        return carry

    lax.fori_loop(0, HEADS // 2, pair, 0)


def attend(q_front, q_rest, kvp):
    seqs, half, width = q_front.shape
    rows = kvp.shape[1]
    head = width // HEADS
    return call(
        functools.partial(attend_kernel, head),
        "attend",
        [sds(q_front.shape, BF)] * 2,
        (q_front, q_rest, kvp),
        flops=2 * seqs * HEADS * 2 * half * rows * 2 * head * 2,
    )


def join_kernel(marks, keep, rows, place, attended, x, weight, vec, normed, low, *more):
    bias, gain, shift = (vec[:, a:b] for a, b in marks)
    step = 256
    for r in range(0, x.shape[0], step):
        at = slice(r, r + step)
        part = attended[at, :]
        summed = x[at, :].astype(F32) + nn(part, weight[...]) + bias
        shaped, _ = norm_stats(summed)
        result = shaped * gain + shift
        normed[at, :] = result
        low[at, :] = result.astype(BF)
        if keep:
            kept, lowt, lowt_other, attendedt, attendedt_other = more
            kept[at, :] = summed
            split_cores(place, result.T.astype(BF), rows, lowt, lowt_other, at)
            split_cores(place, part.T, rows, attendedt, attendedt_other, at)


def join(place, attended, x, weight, vec, marks, keep, slots):
    rows, width = x.shape
    outs = [sds((rows, width), F32), sds((rows, width), BF)]
    if keep:
        outs += [sds((rows, width), F32)] + [sds((width // 2, rows), BF)] * 4
    return call(
        functools.partial(join_kernel, marks, keep, width // (2 * slots)),
        "join_front" if keep else "join_rest",
        outs,
        (attended, x, weight, vec),
        place=place,
        flops=2 * rows * width * width,
    )


def lift_kernel(mark, keep, place, low, weight, vec, active, *more):
    rows = low.shape[0]
    parts, _, piece = weight.shape
    step = 128
    for f in range(parts):
        cols = slice(f * piece, (f + 1) * piece)
        bias = vec[:, mark + f * piece : mark + (f + 1) * piece]
        for r in range(0, rows, step):
            at = slice(r, r + step)
            u = nn(low[at, :], weight[f]) + bias
            bell, share = normal_parts(u)
            a = (u * share).astype(BF)
            active[at, cols] = a
            if keep:
                slope, give = more
                factor = 1.0 / math.sqrt(2.0 * math.pi)
                slope[at, cols] = (share + u * bell * factor).astype(BF)
                half = piece // 2
                give[at, f * half : (f + 1) * half] = jnp.where(
                    place[2] == 0, a[:, half:], a[:, :half]
                )


def lift(place, low, weight, vec, mark, keep):
    rows, width = low.shape
    parts, _, piece = weight.shape
    outs = [sds((rows, parts * piece), BF)]
    if keep:
        outs += [sds((rows, parts * piece), BF), sds((rows, parts * piece // 2), BF)]
    return call(
        functools.partial(lift_kernel, mark, keep),
        "lift_front" if keep else "lift_rest",
        outs,
        (low, weight, vec),
        place=place,
        flops=2 * rows * width * parts * piece,
    )


def lower_kernel(marks, active, normed, weight, vec, *refs):
    bias, gain, shift = (vec[:, a:b] for a, b in marks)
    step = 256
    for r in range(0, normed.shape[0], step):
        at = slice(r, r + step)
        summed = normed[at, :] + nt(active[at, :], weight[...]) + bias
        shaped, inverse = norm_stats(summed)
        if len(refs) == 1:
            refs[0][at, :] = (shaped * gain + shift).astype(BF)
            continue
        dy, output, d_sum, d_low, d_lowt, sums = refs
        output[at, :] = (shaped * gain + shift).astype(BF)
        grad = dy[at, :].astype(F32)
        back = norm_grad(shaped, inverse, gain, grad)
        d_sum[at, :] = back
        d_low[at, :] = back.astype(BF)
        d_lowt[:, at] = back.T.astype(BF)
        new = [jnp.sum(v, axis=0, keepdims=True) for v in (grad * shaped, grad, back)]
        for i, v in enumerate(new):
            sums[i : i + 1, :] = v if r == 0 else sums[i : i + 1, :] + v


def lower(active, normed, weight, vec, marks, dy=None):
    rows, width = normed.shape
    hidden = active.shape[1]
    full = (rows, width)
    if dy is None:
        outs, more = [sds(full, BF)], ()
    else:
        outs = [
            sds(full, BF),
            sds(full, F32),
            sds(full, BF),
            sds((width, rows), BF),
            sds((8, width), F32),
        ]
        more = (dy,)
    return call(
        functools.partial(lower_kernel, marks),
        "lower_rest" if dy is None else "lower_front",
        outs,
        (active, normed, weight, vec, *more),
        flops=2 * rows * width * hidden,
    )


def hidden_back_kernel(d_low, weight, slope, d_hidden, sums):
    rows, piece = d_low.shape
    step = 256
    for f in range(weight.shape[1] // piece):
        cols = slice(f * piece, (f + 1) * piece)
        for r in range(0, rows, step):
            at = slice(r, r + step)
            du = nn(d_low[at, :], weight[:, cols]) * slope[at, cols].astype(F32)
            d_hidden[at, cols] = du.astype(BF)
            part = jnp.sum(du, axis=0, keepdims=True)
            sums[:, cols] = part if r == 0 else sums[:, cols] + part


def hidden_back(d_low, weight, slope):
    rows, width = d_low.shape
    hidden = weight.shape[1]
    return call(
        hidden_back_kernel,
        "hidden_back",
        [sds((rows, hidden), BF), sds((1, hidden), F32)],
        (d_low, weight, slope),
        flops=2 * rows * width * hidden,
    )


def first_back_kernel(
    marks, d_hidden, up, d_sum, kept, vec, weight, d_first, d_low, d_attended, sums
):
    gain = vec[:, marks[0] : marks[1]]
    parts, _, piece = up.shape
    step = 256
    for r in range(0, d_sum.shape[0], step):
        at = slice(r, r + step)
        grad = d_sum[at, :]
        for f in range(parts):
            grad = grad + nt(d_hidden[at, f * piece : (f + 1) * piece], up[f])
        shaped, inverse = norm_stats(kept[at, :])
        back = norm_grad(shaped, inverse, gain, grad)
        low = back.astype(BF)
        d_first[at, :] = back
        d_low[at, :] = low
        d_attended[at, :] = nt(low, weight[...]).astype(BF)
        new = [jnp.sum(v, axis=0, keepdims=True) for v in (grad * shaped, grad, back)]
        for i, v in enumerate(new):
            sums[i : i + 1, :] = v if r == 0 else sums[i : i + 1, :] + v


def first_back(d_hidden, up, d_sum, kept, vec, weight, marks):
    rows, width = d_sum.shape
    parts, _, piece = up.shape
    full = (rows, width)
    return call(
        functools.partial(first_back_kernel, marks),
        "first_back",
        [sds(full, F32), sds(full, BF), sds(full, BF), sds((8, width), F32)],
        (d_hidden, up, d_sum, kept, vec, weight),
        flops=2 * rows * width * (parts * piece + width),
    )


def attend_back_kernel(head, s, queries, kvp, grads, *refs):
    d_q, d_k, d_v, sums = refs[-4:]
    width = queries.shape[2]
    below = lanes_below(head)
    line = lax.broadcasted_iota(jnp.int32, (2 * head, 1), 0) < head
    scale = 1.0 / math.sqrt(head)

    def pair(n, carry):
        at = lanes(n * 2 * head, 2 * head)
        q, k, g = queries[s, :, at], kvp[s, :, at], grads[s, :, at]
        v = kvp[s, :, lanes(width + n * 2 * head, 2 * head)]
        zero = jnp.zeros_like(k)
        none = jnp.zeros_like(q)
        kt = k.T
        dq = dk = dv = None
        for own, ownt in ((below, line), (~below, ~line)):
            scores = nt(jnp.where(own, k, zero), q)
            top = jnp.max(scores, axis=0, keepdims=True)
            e = jnp.exp2((scores - top) * (LOG2E * scale))
            p = e * (1.0 / jnp.sum(e, axis=0, keepdims=True))
            dv_part = nn(p.astype(BF), jnp.where(own, g, none))
            dp = nt(jnp.where(own, v, zero), g)
            both = p * dp
            ds = ((both - p * jnp.sum(both, axis=0, keepdims=True)) * scale).astype(BF)
            dk_part = nn(ds, jnp.where(own, q, none))
            dq_part = nn(jnp.where(ownt, kt, jnp.zeros_like(kt)), ds)
            dv = dv_part if dv is None else dv + dv_part
            dk = dk_part if dk is None else dk + dk_part
            dq = dq_part if dq is None else dq + dq_part
        dq = dq.T
        d_q[s, :, at] = dq.astype(BF)
        d_k[s, :, at] = dk.astype(BF)
        d_v[s, :, at] = dv.astype(BF)
        sums[s, :, at] = jnp.sum(dq, axis=0, keepdims=True)
        return carry

    lax.fori_loop(0, HEADS // 2, pair, 0)


def attend_back(s, queries, kvp, grads, before=()):
    seqs, half, width = queries.shape
    rows = kvp.shape[1]
    head = width // HEADS
    return call(
        functools.partial(attend_back_kernel, head, s),
        "attend_back",
        [
            sds(queries.shape, BF),
            sds((seqs, rows, width), BF),
            sds((seqs, rows, width), BF),
            sds((seqs, 1, width), F32),
        ],
        (queries, kvp, grads, *before),
        flops=2 * HEADS * half * rows * 2 * head * 5,
        alias=[(3 + i, i) for i in range(len(before))],
    )


def spread_kernel(d_k, d_v, kv, projt, q_sums, one_sums, up_sums, two_sums, d_kv, small, vector):
    width = d_k.shape[2]
    grad, k_sums = None, [None, None]
    for s in range(d_k.shape[0]):
        for j, ref in enumerate((d_k, d_v)):
            cols = slice(j * width, (j + 1) * width)
            part = nn(projt[...], ref[s])
            d_kv[s, :, cols] = part.astype(BF)
            new = jnp.sum(part, axis=0, keepdims=True)
            k_sums[j] = new if s == 0 else k_sums[j] + new
            more = nt(ref[s], kv[s, :, cols])
            grad = more if grad is None else grad + more
    rows, across = grad.shape
    small[:rows, :] = grad
    at = 0
    for value in (
        jnp.sum(q_sums[...], axis=0),
        *k_sums,
        one_sums[2:3, :],
        up_sums[...],
        two_sums[2:3, :],
        one_sums[0:1, :],
        one_sums[1:2, :],
        two_sums[0:1, :],
        two_sums[1:2, :],
    ):
        size = value.shape[1]
        vector[:, at : at + size] = value
        at += size
    vector[:, at:] = jnp.zeros((1, vector.shape[1] - at), F32)
    small[rows:, :] = jnp.zeros((small.shape[0] - rows, across), F32)
    for r in range(vector.shape[1] // across):
        small[rows + r : rows + r + 1, :] = vector[:, r * across : (r + 1) * across]


def spread(d_k, d_v, kv, projt, q_sums, one_sums, up_sums, two_sums, entries):
    seqs, rows, width = d_k.shape
    length = kv.shape[1]
    extra = -(-entries // length)
    return call(
        spread_kernel,
        "spread_kv",
        [sds((seqs, length, 2 * width), BF), sds((rows + -(-extra // 8) * 8, length), F32)],
        (d_k, d_v, kv, projt, q_sums, one_sums, up_sums, two_sums),
        scratch=[pltpu.VMEM((1, extra * length), F32)],
        flops=2 * seqs * rows * length * 2 * width * 2,
    )


def input_back_kernel(d_kv, d_q, d_first, weight, back, result):
    seqs, half, width = d_q.shape
    for s in range(seqs):
        front = d_first[s] + nt(d_q[s], weight[:, :width])
        high = front.astype(BF)
        low = (front - high.astype(F32)).astype(BF)
        place = back[s, :, :half]
        total = nt(d_kv[s], weight[:, width:]) + nn(place, high) + nn(place, low)
        result[s] = total.astype(BF)


def input_back(d_kv, d_q, d_first, weight, back):
    seqs, length, wide = d_kv.shape
    half, width = d_q.shape[1:]
    return call(
        input_back_kernel,
        "input_back",
        sds((seqs, length, width), BF),
        (d_kv, d_q, d_first, weight, back),
        flops=2 * seqs * length * width * (wide + width // 2 + length),
    )


def restore_kernel(front, rest, back, result):
    seqs, half, _ = front.shape
    for s in range(seqs):
        total = nn(back[s, :, :half], front[s]) + nn(back[s, :, half:], rest[s])
        result[s] = total.astype(BF)


def restore(front, rest, back):
    seqs, half, width = front.shape
    length = back.shape[1]
    return call(
        restore_kernel,
        "restore_order",
        sds((seqs, length, width), BF),
        (front, rest, back),
        flops=2 * seqs * length * length * width,
    )


def route(rel, slot, send_x, stay_x, send_y, stay_y):
    if slot < 2:
        return (send_x if rel & 1 else stay_x), rel >> 1, slot
    return (send_y if rel & 2 else stay_y), rel & 1, slot - 2


def grad_up_kernel(place, lowt, lowt_other, d_hidden, d_hidden_other, *refs):
    outs, work = refs[:4], refs[4]
    slots, rows, piece = work.shape
    for rel in range(4):
        cols = lanes((rel ^ place[0]) * piece, piece)
        part = nn(lowt[...], d_hidden[:, cols]) + nn(lowt_other[...], d_hidden_other[:, cols])
        work[...] = part.astype(BF).reshape(work.shape)
        for slot in range(slots):
            ref, i, j = route(rel, slot, *outs)
            ref[i, j] = work[(place[1] + slot) % slots]


def grad_up(place, lowt, lowt_other, d_hidden, d_hidden_other, fsdp, slots):
    width, count = lowt.shape
    rows = width // slots
    piece = d_hidden.shape[1] // fsdp
    return call(
        grad_up_kernel,
        "grad_up",
        [sds((2, 2, rows, piece), BF)] * 4,
        (lowt, lowt_other, d_hidden, d_hidden_other),
        scratch=[pltpu.VMEM((slots, rows, piece), BF)],
        place=place,
        flops=2 * width * 2 * count * piece * fsdp,
    )


def grad_down_kernel(place, d_lowt, d_lowt_other, active, active_other, *refs):
    outs, work = refs[:4], refs[4]
    _, _, rows, wide = outs[0].shape
    piece = work.shape[1]
    for slot in range(4):
        z = (place[1] + slot) % 4
        work[...] = (
            nn(d_lowt[...], active[:, lanes((2 * z + place[2]) * piece, piece)])
            + nn(d_lowt_other[...], active_other[:, lanes(z * piece, piece)])
        ).astype(BF)
        for rel in range(4):
            ref, i, j = route(rel, slot, *outs)
            for h in range(wide // piece):
                top = (rel ^ place[0]) * rows * (wide // piece) + h * rows
                ref[i, j, :, h * piece : (h + 1) * piece] = work[lines(top, rows), :]


def grad_down(place, d_lowt, d_lowt_other, active, active_other, rows, slots):
    width, count = d_lowt.shape
    hidden = active.shape[1]
    piece = hidden // (2 * slots)
    return call(
        grad_down_kernel,
        "grad_down",
        [sds((2, 2, rows, width), BF)] * 4,
        (d_lowt, d_lowt_other, active, active_other),
        scratch=[pltpu.VMEM((width, piece), BF)],
        place=place,
        flops=2 * hidden * 2 * count * width,
    )


def grad_rest_kernel(place, *refs):
    pairs, sums, refs = refs[:12], refs[12:14], refs[14:]
    outs, (work_qkv, work_out, vector, smalls, small, d_proj) = refs[:4], refs[4:]
    slots, rows, _ = work_qkv.shape
    _, _, tall, wide = outs[0].shape
    fsdp = smalls.shape[0]
    xt, xt_o, frontt, frontt_o, attendedt, attendedt_o = pairs[:6]
    d_q, d_q_o, d_kv, d_kv_o, d_low, d_low_o = pairs[6:]
    width = d_q.shape[1]

    def both(a, a_o, b, b_o):
        total = nn(a[...], b) + nn(a_o[...], b_o)
        return total.astype(BF).reshape(slots, rows, total.shape[1])

    work_qkv[:, :, :width] = both(frontt, frontt_o, d_q[...], d_q_o[...])
    for j in range(2):
        cols = slice(j * width, (j + 1) * width)
        work_qkv[:, :, (j + 1) * width : (j + 2) * width] = both(
            xt, xt_o, d_kv[:, cols], d_kv_o[:, cols]
        )
    work_out[...] = both(attendedt, attendedt_o, d_low[...], d_low_o[...])
    d_proj[...] = sums[0][...] + sums[1][...]
    across = d_proj.shape[1]
    height = sums[0].shape[0] - (-(-vector.shape[1] // (8 * across))) * 8
    for at in range(0, vector.shape[1], across):
        size = min(across, vector.shape[1] - at)
        line = height + at // across
        vector[:, at : at + size] = d_proj[line : line + 1, :size]
    entries = vector.shape[1] // (2 * fsdp * slots)
    height = height // fsdp
    across = across // (2 * slots)
    start = (height // 8) * across
    room = wide - start
    first = place[2] == 0
    small[...] = jnp.zeros_like(small)
    for f in range(fsdp):
        for z in range(slots):
            for g in range(height // 8):
                at = (
                    slice(f * height + 8 * g, f * height + 8 * g + 8),
                    slice(2 * z * across, 2 * (z + 1) * across),
                )
                part = d_proj[at]
                small[0:8, g * across : (g + 1) * across] = jnp.where(
                    first, part[:, :across], part[:, across:]
                )
            base = (f * 2 * slots + 2 * z) * entries
            own = jnp.where(
                first,
                vector[:, base : base + entries],
                vector[:, base + entries : base + 2 * entries],
            )
            small[0:1, start:] = own[:, :room]
            small[1:2, start : start + entries - room] = own[:, room:]
            smalls[f, z] = small[...].astype(BF)
    below = lanes_below(64)
    for rel in range(fsdp):
        f = rel ^ place[0]
        even = (f & 1) == 0
        for slot in range(slots):
            z = (place[1] + slot) % slots
            ref, i, j = route(rel, slot, *outs)
            put = ref.at[i, j]
            q_first = 9 * (f // 2) + 5 * (f & 1)
            o_pair = 3 * (f // 2)
            put[:rows, :512] = work_qkv[z, :, lanes(q_first * 128, 512)]
            shared = work_qkv[z, :, lanes((9 * (f // 2) + 4) * 128, 128)]
            out_shared = work_out[z, :, lanes((o_pair + 1) * 128, 128)]
            put[:rows, 512:640] = jnp.where(below == even, shared, swap_halves(out_shared))
            put[:rows, 640:] = work_out[z, :, lanes((o_pair + 2 * (f & 1)) * 128, 128)]
            put[rows:, :] = smalls[f, z]


def grad_rest(place, pairs, small, small_other, entries, fsdp, slots):
    width, tokens = 2 * pairs[0].shape[0], pairs[0].shape[1]
    count = pairs[2].shape[1]
    rows = width // (2 * slots)
    wide = 4 * width // fsdp
    return call(
        grad_rest_kernel,
        "grad_rest",
        [sds((2, 2, rows + 16, wide), BF)] * 4,
        (*pairs, small, small_other),
        scratch=[
            pltpu.VMEM((slots, rows, 3 * width), BF),
            pltpu.VMEM((slots, rows, width), BF),
            pltpu.VMEM((1, entries), F32),
            pltpu.VMEM((fsdp, slots, 16, wide), BF),
            pltpu.VMEM((16, wide), F32),
            pltpu.VMEM(small.shape, F32),
        ],
        place=place,
        flops=width * width * (4 * count + 4 * tokens),
    )


def swap_core(value, name="core"):
    n = lax.axis_size("dp")
    with jax.named_scope(name):
        return lax.ppermute(value, "dp", [(i, i ^ 1) for i in range(n)])


def shift_slot(value, by, name="slot"):
    n = lax.axis_size("dp")
    with jax.named_scope(f"{name}_z{by}"):
        return lax.ppermute(value, "dp", [(i, (i + 2 * by) % n) for i in range(n)])


def swap_fsdp(value, bits, name="fsdp"):
    n = lax.axis_size("fsdp")
    with jax.named_scope(f"{name}_{' xyd'[bits]}"):
        return lax.ppermute(value, "fsdp", [(i, i ^ bits) for i in range(n)])


def tie(*values):
    return lax.optimization_barrier(values)


def segments_of(array, tall, blocks, cut, diagonal, low_at, high_at):
    found = []
    for first, back, rows in blocks:
        found += [(array, n * tall + first, n, back, 0, rows) for n in range(3)]
        low = min(max(cut - first, 0), rows)
        if low:
            found.append((diagonal, low_at + first, 3, back, 0, low))
        if low < rows:
            found.append((diagonal, high_at + first + low - cut, 3, back, low, rows - low))
    return found


def block_parts(segments, place, refs, slots):
    arrays = len(refs) // 2
    for other in (0, 1):
        for n, top, bits, back, line, rows in segments:
            z = (place[1] - back + slots) % slots
            ref = refs[other * arrays + n]
            yield ref, top, place[0] ^ bits, 2 * z + (place[2] ^ other), line, rows


def first_whole_kernel(segments, slots, fsdp, height, across, place, *refs):
    count = len(refs) - 8
    blocks = refs[:count]
    qkv, out, vec, proj, projt, halves, smalls, matrix = refs[count:]
    rows = qkv.shape[0] // (2 * slots)
    wide = smalls.shape[3]
    for ref, top, f, d, line, size in block_parts(segments, place, blocks, slots):
        body = min(line + size, rows) - line
        if body > 0:
            src = slice(top, top + body)
            dst = lines(d * rows + line, body)
            qkv[dst, lanes(128 * (9 * (f // 2) + 5 * (f & 1)), 512)] = ref[src, :512]
            halves[f, dst, :] = ref[src, 512:640]
            out[dst, lanes(128 * (3 * (f // 2) + 2 * (f & 1)), 128)] = ref[src, 640:]
        else:
            body = 0
        if body < size:
            smalls[f, d] = ref[top + body : top + size, :]
    entries = vec.shape[1] // (2 * slots * fsdp)
    start = (height // 8) * across
    room = wide - start
    below = lanes_below(64)
    for f in range(fsdp):
        for d in range(2 * slots):
            small = smalls[f, d].astype(F32)
            for g in range(height // 8):
                matrix[
                    f * height + 8 * g : f * height + 8 * g + 8, d * across : (d + 1) * across
                ] = small[0:8, g * across : (g + 1) * across]
            base = (f * 2 * slots + d) * entries
            vec[:, base : base + room] = small[0:1, start:]
            vec[:, base + room : base + entries] = small[1:2, start : start + entries - room]
    for f in range(0, fsdp, 2):
        one, two = halves[f], halves[f + 1]
        at = 128 * (9 * (f // 2) + 4)
        qkv[:, at : at + 128] = jnp.where(below, one, two)
        at = 128 * (3 * (f // 2) + 1)
        out[:, at : at + 128] = swap_halves(jnp.where(below, two, one))
    proj[...] = matrix[...].astype(BF)
    projt[...] = matrix[...].T.astype(BF)


def first_whole(place, blocks, segments, fsdp, slots, width, proj_shape, entries):
    wide = blocks[0].shape[1]
    height, across = proj_shape[0] // fsdp, proj_shape[1] // (2 * slots)
    return call(
        functools.partial(first_whole_kernel, segments, slots, fsdp, height, across),
        "whole_first",
        [
            sds((width, 3 * width), BF),
            sds((width, width), BF),
            sds((1, entries), F32),
            sds(proj_shape, BF),
            sds(proj_shape[::-1], BF),
        ],
        blocks,
        scratch=[
            pltpu.VMEM((fsdp, width, 128), BF),
            pltpu.VMEM((fsdp, 2 * slots, 16, wide), BF),
            pltpu.VMEM(proj_shape, F32),
        ],
        place=place,
    )


def up_whole_kernel(segments, rows, slots, place, *refs):
    blocks, result = refs[:-1], refs[-1]
    for ref, top, f, d, line, size in block_parts(segments, place, blocks, slots):
        result[f, lines(d * rows + line, size), :] = ref[top : top + size, :]


def up_whole(place, blocks, segments, rows, fsdp, slots):
    wide = blocks[0].shape[1]
    return call(
        functools.partial(up_whole_kernel, segments, rows, slots),
        "whole_up",
        sds((fsdp, 2 * slots * rows, wide), BF),
        blocks,
        place=place,
    )


def down_whole_kernel(segments, rows, slots, place, *refs):
    blocks, result = refs[:-1], refs[-1]
    piece = result.shape[1] // (2 * slots)
    parts = blocks[0].shape[1] // piece
    for ref, top, f, d, line, size in block_parts(segments, place, blocks, slots):
        for h in range(parts):
            dst = lines((f * parts + h) * rows + line, size)
            result[dst, lanes(d * piece, piece)] = ref[
                top : top + size, h * piece : (h + 1) * piece
            ]


def down_whole(place, blocks, segments, rows, slots, hidden, width):
    return call(
        functools.partial(down_whole_kernel, segments, rows, slots),
        "whole_down",
        sds((width, hidden), BF),
        blocks,
        place=place,
    )


def stack_kernel(ranges, *refs):
    at = 0
    for (first, last), ref in zip(ranges, refs[:-1]):
        refs[-1][at : at + last - first, :] = ref[first:last, :]
        at += last - first


def stack(*parts):
    arrays, ranges = [p[0] for p in parts], [p[1:] for p in parts]
    rows = sum(b - a for a, b in ranges)
    return call(
        functools.partial(stack_kernel, ranges),
        "stack",
        sds((rows, arrays[0].shape[1]), BF),
        arrays,
    )


def second_stage_kernel(stay_x, from_x, stay_y, from_y, over_y, over_x, kept):
    for stay, came, over, at in ((stay_x, from_x, over_y, 0), (stay_y, from_y, over_x, 1)):
        over[...] = (stay[1].astype(F32) + came[1].astype(F32)).astype(BF)
        kept[at] = (stay[0].astype(F32) + came[0].astype(F32)).astype(BF)


def second_stage(stay_x, from_x, stay_y, from_y):
    shape = stay_x.shape
    return call(
        second_stage_kernel,
        "second_stage",
        [sds(shape[1:], BF), sds(shape[1:], BF), sds(shape, BF)],
        (stay_x, from_x, stay_y, from_y),
    )


def third_stage_kernel(count, *refs):
    ins, owns, sends = refs[: 3 * count], refs[3 * count : 4 * count], refs[4 * count :]
    at = 0
    for n in range(count):
        kept, over_y, over_x = ins[3 * n : 3 * n + 3]
        rows = kept.shape[2]
        put = slice(at, at + rows)
        at += rows
        owns[n][...] = kept[0, 0].astype(F32) + over_y[0].astype(F32)
        sends[0][put, :] = (kept[0, 1].astype(F32) + over_y[1].astype(F32)).astype(BF)
        sends[1][put, :] = (kept[1, 0].astype(F32) + over_x[0].astype(F32)).astype(BF)
        sends[2][put, :] = (kept[1, 1].astype(F32) + over_x[1].astype(F32)).astype(BF)


def third_stage(*pieces):
    shapes = [p[0].shape[2:] for p in pieces]
    rows = sum(a for a, _ in shapes)
    count = len(pieces)
    got = call(
        functools.partial(third_stage_kernel, count),
        "third_stage",
        [sds(a, F32) for a in shapes] + [sds((rows, shapes[0][1]), BF)] * 3,
        [a for p in pieces for a in p],
    )
    return got[:count], got[count:]


def last_stage_kernel(count, *refs):
    owns, (one, two, three) = refs[:count], refs[count : count + 3]
    results, squares = refs[count + 3 : -1], refs[-1]
    at = 0
    sums = None
    for own, result in zip(owns, results):
        put = slice(at, at + own.shape[0])
        at += own.shape[0]
        total = (own[...] + two[put, :].astype(F32)) + (
            one[put, :].astype(F32) + three[put, :].astype(F32)
        )
        result[...] = total
        part = jnp.sum(total * total, axis=0, keepdims=True)
        sums = part if sums is None else sums + part
    squares[...] = jnp.broadcast_to(jnp.sum(sums), squares.shape)


def last_stage(owns, came):
    return call(
        functools.partial(last_stage_kernel, len(owns)),
        "last_stage",
        [sds(a.shape, F32) for a in owns] + [sds((8, 128), F32)],
        (*owns, *came),
    )


def sum_everywhere(value):
    a, b, c = (swap_fsdp(value, k, "norm") for k in (1, 2, 3))
    value = (value + a) + (b + c)
    a, b, c = (shift_slot(value, k, "norm") for k in (1, 2, 3))
    value = (value + b) + (a + c)
    return value + swap_core(value)


def adam(weight, moment, second, grad, scale_clip, rate, decay):
    clipped = grad * scale_clip
    new_moment = BETA_ONE * moment + (1.0 - BETA_ONE) * clipped
    new_second = BETA_TWO * second + (1.0 - BETA_TWO) * clipped * clipped
    moment_hat = new_moment / (1.0 - BETA_ONE**STEP)
    second_hat = new_second / (1.0 - BETA_TWO**STEP)
    new_weight = weight - rate * (moment_hat / (jnp.sqrt(second_hat) + ADAM_EPS) + decay * weight)
    return new_weight, new_moment, new_second, new_weight.astype(BF)


def update_kernel(rates, place, squares, g_first, g_up, g_down, *refs):
    ins, outs = refs[:18], refs[18:-3]
    norm_ref, outs = outs[0], outs[1:]
    vector, wide_work, thin_work = refs[-3:]
    odd = (place[0] & 1) == 1
    norm = jnp.sqrt(squares[0:1, 0:1])
    norm_ref[...] = norm
    clip = jnp.minimum(1.0, CLIP_NORM / norm)

    def put(n, place, grad):
        new = adam(*(ins[3 * n + i][place] for i in range(3)), grad, clip, *rates[n])
        for i in range(4):
            outs[4 * n + i][place] = new[i]

    rows, wide = g_up.shape
    piece = ins[0].shape[1]
    every = (slice(None), slice(None))
    wide_work[:, :64] = g_first[:rows, 576:640]
    wide_work[:, 64:] = g_first[:rows, :512]
    put(0, every, jnp.where(odd, wide_work[...], g_first[:rows, :piece]))

    def thin(full, first, second):
        thin_work[0, :, :128] = full
        thin_work[0, :, 128:] = second
        thin_work[1, :, :64] = first
        thin_work[1, :, 64:] = full
        return jnp.where(odd, thin_work[1], thin_work[0])

    put(1, every, thin(g_first[:rows, 640:], g_first[:rows, 512:576], g_first[:rows, 576:640]))
    put(2, every, g_up[...])
    across = ins[9].shape[1]
    for h in range(wide // across):
        put(
            3,
            (slice(h * rows, (h + 1) * rows), slice(None)),
            g_down[:, h * across : (h + 1) * across],
        )
    height, across = ins[12].shape
    for g in range(height // 8):
        put(
            4,
            (slice(8 * g, 8 * g + 8), slice(None)),
            g_first[rows : rows + 8, g * across : (g + 1) * across],
        )
    start = (height // 8) * across
    room = wide - start
    entries = ins[15].shape[0]
    vector[:, :room] = g_first[rows : rows + 1, start:]
    vector[:, room:] = g_first[rows + 1 : rows + 2, start : start + entries - room]
    state = (ins[15 + i][...].reshape(1, entries) for i in range(3))
    new = adam(*state, vector[...], clip, *rates[5])
    for i in range(4):
        outs[20 + i][...] = new[i].reshape(entries)


def update(place, squares, g_first, g_up, g_down, states, rates):
    outs = [sds((1, 1), F32)]
    for n in range(6):
        shape = states[3 * n].shape
        outs += [sds(shape, F32)] * 3 + [sds(shape, BF)]
    return call(
        functools.partial(update_kernel, rates),
        "update",
        outs,
        (squares, g_first, g_up, g_down, *states),
        scratch=[
            pltpu.VMEM((1, *states[15].shape), F32),
            pltpu.VMEM(states[0].shape, F32),
            pltpu.VMEM((2, *states[3].shape), F32),
        ],
        place=place,
    )


def on_device(
    tokens,
    cotangent,
    positions,
    counts,
    qkv_weight,
    qkv_moment,
    qkv_second,
    out_weight,
    out_moment,
    out_second,
    up_weight,
    up_moment,
    up_second,
    down_projection_weight,
    down_moment,
    down_second,
    proj_weight,
    proj_moment,
    proj_second,
    vec_weight,
    vec_moment,
    vec_second,
):
    fsdp, slots = lax.axis_size("fsdp"), lax.axis_size("dp") // 2
    place = jnp.stack(
        [lax.axis_index("fsdp"), lax.axis_index("dp") // 2, lax.axis_index("dp") % 2]
    ).astype(jnp.int32)
    seqs = counts.shape[0]
    rows, width = tokens.shape
    length = rows // seqs
    half = length // 2
    marked = positions.shape[1]
    hidden = down_projection_weight.shape[0] * slots * 2
    proj_shape = (proj_weight.shape[0] * fsdp, proj_weight.shape[1] * 2 * slots)
    entries = vec_weight.shape[0] * fsdp * 2 * slots
    rates = (
        (RATE_QKV, DECAY_RATE),
        (RATE_OUT, DECAY_RATE),
        (RATE_UP, DECAY_RATE),
        (RATE_DOWN, DECAY_RATE),
        (RATE_PROJ, DECAY_RATE),
        (RATE_VEC, 0.0),
    )

    own, own_first, own_rest = pack(
        place,
        qkv_weight,
        out_weight,
        up_weight,
        down_projection_weight.T,
        proj_weight,
        vec_weight,
    )
    rows_first, rows_up = own_first.shape[0], own_rest.shape[0] // 2

    def across(value, name):
        return swap_fsdp(value, 1, name), swap_fsdp(value, 2, name)

    def cores(arrays, name):
        return [swap_core(a, name) for a in arrays]

    back_first = [shift_slot(own_first, k, "first") for k in (1, 2, 3)]
    own_x, own_y = across(own, "own")
    x = tokens.reshape(seqs, length, width)
    front, rest, frontt, frontt_give, xt, xt_give, back = order_rows(place, x, positions, slots)
    live = jnp.arange(marked, dtype=jnp.int32)[None, :] < counts[:, None]
    dy = jnp.pad(
        jnp.where(live[:, :, None], cotangent, jnp.zeros_like(cotangent)),
        ((0, 0), (0, half - marked), (0, 0)),
    ).reshape(seqs * half, width)
    back_first, own_x, own_y, own_rest, own, frontt_give, xt_give, dy, front = tie(
        back_first, own_x, own_y, own_rest, own, frontt_give, xt_give, dy, front
    )

    def all_of(*arrays):
        return stack(*((a, 0, a.shape[0]) for a in arrays))

    far_first = all_of(*back_first)
    first_x, first_y = across(far_first, "first")
    back_rest = [None, shift_slot(own_rest, 1, "rest"), None, shift_slot(own_rest, 3, "rest")]
    near = all_of(own, own_x, own_y)
    near_other = swap_core(near, "near_core")
    own_x, own_y, own, far_first, first_x, first_y, own_rest, near, near_other, back_rest = tie(
        own_x, own_y, own, far_first, first_x, first_y, own_rest, near, near_other, back_rest
    )

    tall, far = own.shape[0], far_first.shape[0]
    half_own = tall // 32 * 16
    half_first = (tall + far) // 32 * 16 - half_own
    low = stack((own_x, 0, half_own), (first_x, 0, half_first))
    high = stack((own_y, half_own, tall), (first_y, half_first, far))
    diagonal = [swap_fsdp(low, 2, "diag"), swap_fsdp(high, 1, "diag")]
    back_rest[2] = shift_slot(own_rest, 2, "rest")
    first = all_of(far_first, first_x, first_y)
    first_other = swap_core(first, "first_core")
    diagonal, first_other, back_rest = tie(diagonal, first_other, back_rest)
    diagonal = all_of(*diagonal)
    diagonal_other = swap_core(diagonal, "diag_core")
    diagonal, diagonal_other = tie(diagonal, diagonal_other)
    high_at = half_own + half_first

    def near_segments(first, rows):
        return segments_of(0, tall, [(first, 0, rows)], half_own, 1, 0, high_at)

    far_up = stack(*((a, 0, rows_up) for a in back_rest[1:]))
    far_down = stack(*((a, rows_up, 2 * rows_up) for a in back_rest[1:]))
    up_x, up_y = across(far_up, "up")
    blocks = [(k * rows_first, k + 1, rows_first) for k in range(3)]
    qkv_full, out_full, vec, proj, projt = first_whole(
        place,
        [near, diagonal, first, near_other, diagonal_other, first_other],
        near_segments(0, rows_first)
        + segments_of(2, far, blocks, half_first, 1, half_own, high_at + tall - half_own),
        fsdp,
        slots,
        width,
        proj_shape,
        entries,
    )
    q_front, q_rest, kv, kvp = make_qkv(front, rest, x, qkv_full, vec, proj)
    up_x, up_y, q_front, far_down = tie(up_x, up_y, q_front, far_down)

    far = far_up.shape[0]
    half_up = far // 32 * 16
    blocks = [(k * rows_up, k + 1, rows_up) for k in range(3)]

    def far_diagonal(from_x, from_y, name):
        return [swap_fsdp(from_x[:half_up], 2, name), swap_fsdp(from_y[half_up:], 1, name)]

    def rest_segments(first):
        return near_segments(first, rows_up) + segments_of(2, far, blocks, half_up, 3, 0, half_up)

    up_diagonal = far_diagonal(up_x, up_y, "updiag")
    down_x, down_y = across(far_down, "down")
    up = all_of(far_up, up_x, up_y)
    up_other = swap_core(up, "up_core")
    a_front, a_rest = attend(q_front, q_rest, kvp)

    m1 = 3 * width
    m2 = m1 + width
    m3 = m2 + hidden
    m4 = m3 + width
    ends = [m4 + i * width for i in range(5)]
    marks_one = ((m1, m2), (ends[0], ends[1]), (ends[1], ends[2]))
    marks_two = ((m3, m4), (ends[2], ends[3]), (ends[3], ends[4]))

    def flat(v):
        return v.reshape(seqs * half, width)

    h_front, low_front, kept, lowt, lowt_give, attendedt, attendedt_give = join(
        place, flat(a_front), flat(front), out_full, vec, marks_one, True, slots
    )
    up_diagonal, up_other, low_front, lowt_give, attendedt_give, a_rest = tie(
        up_diagonal, up_other, low_front, lowt_give, attendedt_give, a_rest
    )
    up_diagonal = all_of(*up_diagonal)
    up_diagonal_other = swap_core(up_diagonal, "updiag_core")
    h_rest, low_rest = join(
        place, flat(a_rest), flat(rest), out_full, vec, marks_one, False, slots
    )
    up_diagonal_other, low_rest, down_x, down_y = tie(
        up_diagonal_other, low_rest, down_x, down_y
    )
    down_diagonal = far_diagonal(down_x, down_y, "downdiag")
    down = all_of(far_down, down_x, down_y)
    down_other = swap_core(down, "down_core")
    lowt_came, attendedt_came = cores((lowt_give, attendedt_give), "given_core")
    up_full = up_whole(
        place,
        [near, diagonal, up, up_diagonal]
        + [near_other, diagonal_other, up_other, up_diagonal_other],
        rest_segments(rows_first),
        rows_up,
        fsdp,
        slots,
    )
    act_front, slope, act_give = lift(place, low_front, up_full, vec, m2, True)
    down_diagonal, down_other, act_front, act_give, lowt_came, attendedt_came = tie(
        down_diagonal, down_other, act_front, act_give, lowt_came, attendedt_came
    )
    down_diagonal = all_of(*down_diagonal)
    down_diagonal_other = swap_core(down_diagonal, "downdiag_core")
    act_came = swap_core(act_give, "given_core")
    down_full = down_whole(
        place,
        [near, diagonal, down, down_diagonal]
        + [near_other, diagonal_other, down_other, down_diagonal_other],
        rest_segments(rows_first + rows_up),
        rows_up,
        slots,
        hidden,
        width,
    )
    out_front, d_sum, d_low, d_lowt, two_sums = lower(
        act_front, h_front, down_full, vec, marks_two, dy
    )

    def send(parts, name):
        send_x, stay_x, send_y, stay_y = parts
        return swap_fsdp(send_x, 1, name), swap_fsdp(send_y, 2, name), stay_x, stay_y

    def forward(from_x, from_y, stay_x, stay_y, name):
        over_y, over_x, kept = second_stage(stay_x, from_x, stay_y, from_y)
        return kept, swap_fsdp(over_y, 2, name), swap_fsdp(over_x, 1, name)

    def along_z(pieces, name):
        owns, parts = third_stage(*pieces)
        return owns, [shift_slot(a, k + 1, name) for k, a in enumerate(parts)]

    d_lowt_came = swap_core(d_lowt, "d_low_core")
    d_hidden, up_sums = hidden_back(d_low, down_full, slope)
    d_lowt_came, d_hidden, act_came, frontt_give, xt_give = tie(
        d_lowt_came, d_hidden, act_came, frontt_give, xt_give
    )
    d_hidden_came = swap_core(d_hidden, "d_hidden_core")
    parts_down = grad_down(place, d_lowt, d_lowt_came, act_front, act_came, rows_up, slots)
    parts_down, d_hidden_came, d_hidden = tie(parts_down, d_hidden_came, d_hidden)
    sent_down = send(parts_down, "gdown")
    parts_up = grad_up(place, lowt, lowt_came, d_hidden, d_hidden_came, fsdp, slots)
    frontt_came, xt_came = cores((frontt_give, xt_give), "given_core")
    parts_up, d_hidden, frontt_came, xt_came = tie(parts_up, d_hidden, frontt_came, xt_came)
    d_first, d_first_low, d_attended, one_sums = first_back(
        d_hidden, up_full, d_sum, kept, vec, out_full, (ends[0], ends[1])
    )
    d_attended = d_attended.reshape(seqs, half, width)
    got = attend_back(0, q_front, kvp, d_attended)
    got, d_first_low, sent_down, parts_up = tie(got, d_first_low, sent_down, parts_up)
    over_down = forward(*sent_down, "gdown2")
    d_first_low_came = swap_core(d_first_low, "d_low_core")
    for s in range(1, seqs):
        got = attend_back(s, q_front, kvp, d_attended, got)
    d_q, d_k, d_v, q_sums = got
    d_kv, small = spread(d_k, d_v, kv, projt, q_sums, one_sums, up_sums, two_sums, entries)
    d_kv, small, over_down, d_first_low_came, d_q, parts_up = tie(
        d_kv, small, over_down, d_first_low_came, d_q, parts_up
    )
    sent_up = send(parts_up, "gup")
    d_kv_came, small_came, d_q_came = cores((d_kv, small, d_q), "d_kv_core")
    d_kv_came, small_came, d_q_came, over_down = tie(d_kv_came, small_came, d_q_came, over_down)
    last_down = along_z((over_down,), "gdown3")
    tall = 2 * width
    parts_first = grad_rest(
        place,
        (
            xt,
            xt_came,
            frontt,
            frontt_came,
            attendedt,
            attendedt_came,
            flat(d_q),
            flat(d_q_came),
            d_kv.reshape(rows, tall),
            d_kv_came.reshape(rows, tall),
            d_first_low,
            d_first_low_came,
        ),
        small,
        small_came,
        entries,
        fsdp,
        slots,
    )
    parts_first, low_rest, d_q, sent_up = tie(parts_first, low_rest, d_q, sent_up)
    over_up = forward(*sent_up, "gup2")
    parts_first, last_down = tie(parts_first, last_down)
    sent_first = send(parts_first, "gfirst")
    act_rest = lift(place, low_rest, up_full, vec, m2, False)[0]
    act_rest, over_up, last_down = tie(act_rest, over_up, last_down)
    last_up = along_z((over_up,), "gup3")
    out_rest = lower(act_rest, h_rest, down_full, vec, marks_two)[0]
    output = restore(
        out_front.reshape(seqs, half, width), out_rest.reshape(seqs, half, width), back
    ).reshape(rows, width)
    g_down, squares_down = last_stage(*last_down)
    sent_first, output, last_up, d_q = tie(sent_first, output, last_up, d_q)
    over_first = forward(*sent_first, "gfirst2")
    grad_input = input_back(
        d_kv, d_q, d_first.reshape(seqs, half, width), qkv_full, back
    ).reshape(rows, width)
    g_up, squares_up = last_stage(*last_up)
    over_first, grad_input = tie(over_first, grad_input)
    last_first = along_z((over_first,), "gfirst3")
    g_first, squares_first = last_stage(*last_first)
    squares_rest = squares_up + squares_down
    squares = sum_everywhere(squares_first + squares_rest)
    states = (
        qkv_weight,
        qkv_moment,
        qkv_second,
        out_weight,
        out_moment,
        out_second,
        up_weight,
        up_moment,
        up_second,
        down_projection_weight.T,
        down_moment.T,
        down_second.T,
        proj_weight,
        proj_moment,
        proj_second,
        vec_weight,
        vec_moment,
        vec_second,
    )
    new = update(place, squares, g_first, g_up, g_down, states, rates)
    norm, new = new[0].reshape(()), list(new[1:])
    new[12:16] = [v.T for v in new[12:16]]
    return (output, grad_input, norm, *new)


def split_up(value, dim, peers):
    dims = value.shape
    blocks = value.reshape(*dims[:dim], peers, dims[dim] // peers, *dims[dim + 1 :])
    return jnp.moveaxis(blocks, dim, 0)


def sum_at_owner(value, axis, dim):
    blocks = split_up(value, dim, lax.axis_size(axis))
    arrived = lax.all_to_all(blocks, axis, split_axis=0, concat_axis=0, tiled=True)
    return arrived.astype(jnp.float32).sum(axis=0)


def side_by_side(arrays, axis, dim, along):
    ends, at = ([], 0)
    for a in arrays[:-1]:
        at += a.shape[along]
        ends.append(at)
    both = jnp.concatenate(arrays, axis=along)
    return tuple(jnp.split(sum_at_owner(both, axis, dim), ends, axis=along))


def layer_norm(summed, gains, shifts):
    average = jnp.mean(summed, axis=-1, keepdims=True)
    centered = summed - average
    variance = jnp.mean(centered * centered, axis=-1, keepdims=True)
    return centered * lax.rsqrt(variance + NORM_EPS) * gains + shifts


def norm_back(summed, gains, shifts, grad_out):
    result, pullback = jax.vjp(layer_norm, summed, gains, shifts)
    return pullback(grad_out)


def gelu_exact(values):
    return jax.nn.gelu(values, approximate=False)


def split_vector(vec_full, model_width, hidden_width):
    mark_one = 3 * model_width
    mark_two = mark_one + model_width
    mark_three = mark_two + hidden_width
    mark_four = mark_three + model_width
    return (
        vec_full[:mark_one],
        vec_full[mark_one:mark_two],
        vec_full[mark_two:mark_three],
        vec_full[mark_three:mark_four],
        vec_full[mark_four : mark_four + model_width],
        vec_full[mark_four + model_width : mark_four + 2 * model_width],
        vec_full[mark_four + 2 * model_width : mark_four + 3 * model_width],
        vec_full[mark_four + 3 * model_width : mark_four + 4 * model_width],
    )


def adam_update(weight, moment, second, grad, scale_clip, rate, decay):
    clipped = grad * scale_clip
    new_moment = BETA_ONE * moment + (1.0 - BETA_ONE) * clipped
    new_second = BETA_TWO * second + (1.0 - BETA_TWO) * clipped * clipped
    moment_hat = new_moment / (1.0 - BETA_ONE**STEP)
    second_hat = new_second / (1.0 - BETA_TWO**STEP)
    new_weight = weight - rate * (moment_hat / (jnp.sqrt(second_hat) + ADAM_EPS) + decay * weight)
    return (new_weight, new_moment, new_second, new_weight.astype(jnp.bfloat16))


def fetch_whole(low_qkv, low_out, low_up, low_down, low_proj, low_vec):
    rows = (
        lax.all_gather(low_qkv, "dp", axis=0, tiled=True),
        lax.all_gather(low_out, "dp", axis=0, tiled=True),
        lax.all_gather(low_up, "dp", axis=0, tiled=True),
        lax.all_gather(low_down, "dp", axis=0, tiled=True),
        lax.all_gather(low_proj, "dp", axis=1, tiled=True),
        lax.all_gather(low_vec, "dp", axis=0, tiled=True),
    )
    return (
        lax.all_gather(rows[0], "fsdp", axis=1, tiled=True),
        lax.all_gather(rows[1], "fsdp", axis=1, tiled=True),
        lax.all_gather(rows[2], "fsdp", axis=1, tiled=True),
        lax.all_gather(rows[3], "fsdp", axis=1, tiled=True),
        lax.all_gather(rows[4], "fsdp", axis=0, tiled=True),
        lax.all_gather(rows[5], "fsdp", axis=0, tiled=True),
    )


def on_any_mesh(
    tokens,
    cotangent,
    positions,
    counts,
    qkv_weight,
    qkv_moment,
    qkv_second,
    out_weight,
    out_moment,
    out_second,
    up_weight,
    up_moment,
    up_second,
    down_projection_weight,
    down_moment,
    down_second,
    proj_weight,
    proj_moment,
    proj_second,
    vec_weight,
    vec_moment,
    vec_second,
):
    low_qkv = qkv_weight.astype(jnp.bfloat16)
    low_out = out_weight.astype(jnp.bfloat16)
    low_up = up_weight.astype(jnp.bfloat16)
    low_down = down_projection_weight.astype(jnp.bfloat16)
    low_proj = proj_weight.astype(jnp.bfloat16)
    low_vec = vec_weight.astype(jnp.bfloat16)
    qkv_full, out_full, up_full, down_full, projection_gathered, vec_full = fetch_whole(
        low_qkv, low_out, low_up, low_down, low_proj, low_vec
    )
    seq_count = counts.shape[0]
    row_count = tokens.shape[0]
    seq_length = row_count // seq_count
    model_width = tokens.shape[1]
    head_width = model_width // HEADS
    hidden_width = vec_full.shape[0] - 9 * model_width
    proj_rows = projection_gathered.shape[0]
    score_scale = head_width ** (-0.5)
    bias_qkv, bias_out, bias_up, bias_down, gain_one, shift_one, gain_two, shift_two = split_vector(
        vec_full.astype(jnp.float32), model_width, hidden_width
    )
    pre_qkv = jnp.dot(tokens, qkv_full, preferred_element_type=jnp.float32)
    qkv_low = (pre_qkv + bias_qkv).astype(jnp.bfloat16)
    queries = qkv_low[:, :model_width].reshape(seq_count, seq_length, HEADS, head_width)
    key_value_pair = qkv_low[:, model_width:].reshape(seq_count, seq_length, 2 * model_width)
    projected = jnp.einsum(
        "bu,vur->vbr", projection_gathered, key_value_pair, preferred_element_type=jnp.float32
    ).astype(jnp.bfloat16)
    key_heads = projected[:, :, :model_width].reshape(seq_count, proj_rows, HEADS, head_width)
    value_heads = projected[:, :, model_width:].reshape(seq_count, proj_rows, HEADS, head_width)
    scores = (
        jnp.einsum("slhe,sjhe->shlj", queries, key_heads, preferred_element_type=jnp.float32)
        * score_scale
    )
    peak = jnp.max(scores, axis=-1, keepdims=True)
    log_total = peak + jnp.log(jnp.sum(jnp.exp(scores - peak), axis=-1, keepdims=True))
    soft_low = jnp.exp(scores - log_total).astype(jnp.bfloat16)
    context = jnp.einsum(
        "shlj,sjhe->slhe", soft_low, value_heads, preferred_element_type=jnp.float32
    )
    attended = context.reshape(row_count, model_width).astype(jnp.bfloat16)
    first_sum = (
        tokens.astype(jnp.float32)
        + jnp.dot(attended, out_full, preferred_element_type=jnp.float32)
        + bias_out
    )
    normed_one = layer_norm(first_sum, gain_one, shift_one)
    normed_low = normed_one.astype(jnp.bfloat16)
    hidden_pre = jnp.dot(normed_low, up_full, preferred_element_type=jnp.float32) + bias_up
    active = gelu_exact(hidden_pre).astype(jnp.bfloat16)
    second_sum = (
        normed_one + jnp.dot(active, down_full, preferred_element_type=jnp.float32) + bias_down
    )
    output = layer_norm(second_sum, gain_two, shift_two).astype(jnp.bfloat16)
    slot_live = jnp.arange(positions.shape[1], dtype=jnp.int32)[None, :] < counts[:, None]
    one_hot_rows = (
        (positions[:, :, None] == jnp.arange(seq_length, dtype=jnp.int32)[None, None, :])
        & slot_live[:, :, None]
    ).astype(jnp.bfloat16)
    dense = jnp.einsum(
        "bej,bef->bjf", one_hot_rows, cotangent, preferred_element_type=jnp.float32
    ).reshape(row_count, model_width)
    qkv_full, out_full, up_full, down_full, projection_gathered, vec_full = fetch_whole(
        low_qkv, low_out, low_up, low_down, low_proj, low_vec
    )
    d_second, d_gain_two, d_shift_two = norm_back(second_sum, gain_two, shift_two, dense)
    d_bias_down = jnp.sum(d_second, axis=0)
    d_second_low = d_second.astype(jnp.bfloat16)
    grad_down = jnp.einsum("rf,rd->fd", active, d_second_low, preferred_element_type=jnp.float32)
    d_active = jnp.einsum("rd,fd->rf", d_second_low, down_full, preferred_element_type=jnp.float32)
    gelu_value, gelu_pull = jax.vjp(gelu_exact, hidden_pre)
    d_hidden = gelu_pull(d_active)[0]
    d_bias_up = jnp.sum(d_hidden, axis=0)
    d_hidden_low = d_hidden.astype(jnp.bfloat16)
    grad_up = jnp.einsum("rd,rf->df", normed_low, d_hidden_low, preferred_element_type=jnp.float32)
    d_normed = d_second + jnp.einsum(
        "rf,df->rd", d_hidden_low, up_full, preferred_element_type=jnp.float32
    )
    d_first, d_gain_one, d_shift_one = norm_back(first_sum, gain_one, shift_one, d_normed)
    d_bias_out = jnp.sum(d_first, axis=0)
    d_first_low = d_first.astype(jnp.bfloat16)
    grad_out = jnp.einsum("rd,re->de", attended, d_first_low, preferred_element_type=jnp.float32)
    d_attended = jnp.einsum("re,de->rd", d_first_low, out_full, preferred_element_type=jnp.float32)
    d_attended = d_attended.astype(jnp.bfloat16).reshape(seq_count, seq_length, HEADS, head_width)
    scores_again = (
        jnp.einsum("slhe,sjhe->shlj", queries, key_heads, preferred_element_type=jnp.float32)
        * score_scale
    )
    probs_again = jnp.exp(scores_again - log_total)
    probs_low = probs_again.astype(jnp.bfloat16)
    d_value_heads = jnp.einsum(
        "shlj,slhe->sjhe", probs_low, d_attended, preferred_element_type=jnp.float32
    )
    d_probs = jnp.einsum(
        "slhe,sjhe->shlj", d_attended, value_heads, preferred_element_type=jnp.float32
    )
    d_scores = probs_again * (d_probs - jnp.sum(probs_again * d_probs, axis=-1, keepdims=True))
    d_raw_low = (d_scores * score_scale).astype(jnp.bfloat16)
    d_queries = jnp.einsum(
        "shlj,sjhe->slhe", d_raw_low, key_heads, preferred_element_type=jnp.float32
    ).reshape(row_count, model_width)
    d_key_heads = jnp.einsum(
        "shlj,slhe->sjhe", d_raw_low, queries, preferred_element_type=jnp.float32
    )
    projected_gradient = jnp.concatenate(
        [
            d_key_heads.reshape(seq_count, proj_rows, model_width),
            d_value_heads.reshape(seq_count, proj_rows, model_width),
        ],
        axis=-1,
    ).astype(jnp.bfloat16)
    d_kv = jnp.einsum(
        "cq,uct->uqt", projection_gathered, projected_gradient, preferred_element_type=jnp.float32
    ).reshape(row_count, 2 * model_width)
    projection_gradient = jnp.einsum(
        "nhy,nxy->hx", projected_gradient, key_value_pair, preferred_element_type=jnp.float32
    )
    d_qkv = jnp.concatenate([d_queries, d_kv], axis=-1)
    d_bias_qkv = jnp.sum(d_qkv, axis=0)
    d_qkv_low = d_qkv.astype(jnp.bfloat16)
    grad_qkv = jnp.einsum("rd,re->de", tokens, d_qkv_low, preferred_element_type=jnp.float32)
    grad_input = (
        d_first + jnp.einsum("re,de->rd", d_qkv_low, qkv_full, preferred_element_type=jnp.float32)
    ).astype(jnp.bfloat16)
    grad_vec = jnp.concatenate(
        [
            d_bias_qkv,
            d_bias_out,
            d_bias_up,
            d_bias_down,
            d_gain_one,
            d_shift_one,
            d_gain_two,
            d_shift_two,
        ]
    )
    col_part = (
        lax.psum_scatter(
            grad_qkv.astype(jnp.bfloat16), "fsdp", scatter_dimension=1, tiled=True
        ).astype(jnp.float32),
        lax.psum_scatter(
            grad_out.astype(jnp.bfloat16), "fsdp", scatter_dimension=1, tiled=True
        ).astype(jnp.float32),
        lax.psum_scatter(
            grad_up.astype(jnp.bfloat16), "fsdp", scatter_dimension=1, tiled=True
        ).astype(jnp.float32),
        lax.psum_scatter(
            grad_down.astype(jnp.bfloat16), "fsdp", scatter_dimension=1, tiled=True
        ).astype(jnp.float32),
        lax.psum_scatter(
            projection_gradient.astype(jnp.bfloat16), "fsdp", scatter_dimension=0, tiled=True
        ).astype(jnp.float32),
        lax.psum_scatter(
            grad_vec.astype(jnp.bfloat16), "fsdp", scatter_dimension=0, tiled=True
        ).astype(jnp.float32),
    )
    owned = (
        *side_by_side(
            (
                col_part[0].astype(jnp.bfloat16),
                col_part[1].astype(jnp.bfloat16),
                col_part[2].astype(jnp.bfloat16),
            ),
            "dp",
            0,
            1,
        ),
        sum_at_owner(col_part[3].astype(jnp.bfloat16), "dp", 0),
        sum_at_owner(col_part[4].astype(jnp.bfloat16), "dp", 1),
        sum_at_owner(col_part[5].astype(jnp.bfloat16), "dp", 0),
    )
    owned_qkv, owned_out, owned_up, owned_down, owned_proj, owned_vec = owned
    local_squares = (
        jnp.sum(owned_qkv * owned_qkv)
        + jnp.sum(owned_out * owned_out)
        + jnp.sum(owned_up * owned_up)
        + jnp.sum(owned_down * owned_down)
        + jnp.sum(owned_proj * owned_proj)
        + jnp.sum(owned_vec * owned_vec)
    )
    all_squares = lax.psum(local_squares, ("fsdp", "dp"))
    grad_norm = jnp.sqrt(all_squares)
    scale_clip = jnp.minimum(1.0, CLIP_NORM / grad_norm)
    qkv_parts = adam_update(
        qkv_weight, qkv_moment, qkv_second, owned_qkv, scale_clip, RATE_QKV, DECAY_RATE
    )
    out_parts = adam_update(
        out_weight, out_moment, out_second, owned_out, scale_clip, RATE_OUT, DECAY_RATE
    )
    up_parts = adam_update(
        up_weight, up_moment, up_second, owned_up, scale_clip, RATE_UP, DECAY_RATE
    )
    down_parts = adam_update(
        down_projection_weight,
        down_moment,
        down_second,
        owned_down,
        scale_clip,
        RATE_DOWN,
        DECAY_RATE,
    )
    proj_parts = adam_update(
        proj_weight, proj_moment, proj_second, owned_proj, scale_clip, RATE_PROJ, DECAY_RATE
    )
    vec_parts = adam_update(
        vec_weight, vec_moment, vec_second, owned_vec, scale_clip, RATE_VEC, 0.0
    )
    return (
        output,
        grad_input,
        grad_norm,
        qkv_parts[0],
        qkv_parts[1],
        qkv_parts[2],
        qkv_parts[3],
        out_parts[0],
        out_parts[1],
        out_parts[2],
        out_parts[3],
        up_parts[0],
        up_parts[1],
        up_parts[2],
        up_parts[3],
        down_parts[0],
        down_parts[1],
        down_parts[2],
        down_parts[3],
        proj_parts[0],
        proj_parts[1],
        proj_parts[2],
        proj_parts[3],
        vec_parts[0],
        vec_parts[1],
        vec_parts[2],
        vec_parts[3],
    )


def solution(mesh):
    matrix = P("dp", "fsdp")
    tall = P("fsdp", "dp")
    every = P(("fsdp", "dp"))
    small = mesh.shape["fsdp"] == 4 and mesh.shape["dp"] == 8
    return jax.shard_map(
        on_device if small else on_any_mesh,
        mesh=mesh,
        in_specs=(every,) * 4 + (matrix,) * 12 + (tall,) * 3 + (every,) * 3,
        out_specs=(every, every, P()) + (matrix,) * 16 + (tall,) * 4 + (every,) * 4,
        check_vma=False,
    )
```

```python
import functools
import math

import jax
import jax.numpy as jnp
from jax import lax
from jax.experimental import pallas as pl
from jax.experimental.pallas import tpu as pltpu
from jax.sharding import PartitionSpec as P

HEADS = 12
STEP = 10
NORM_EPS = 1e-05
CLIP_NORM = 1.0
BETA_ONE = 0.9
BETA_TWO = 0.999
ADAM_EPS = 1e-08
DECAY_RATE = 0.01
RATE_QKV = 0.05
RATE_OUT = 0.4
RATE_UP = 0.05
RATE_DOWN = 0.05
RATE_PROJ = 0.05
RATE_VEC = 1.0

BF = jnp.bfloat16
F32 = jnp.float32
LOG2E = math.log2(math.e)
MIB = 1 << 20


def nn(a, b):
    return jnp.dot(a, b, preferred_element_type=F32)


def nt(a, b):
    return lax.dot_general(a, b, (((1,), (1,)), ((), ())), preferred_element_type=F32)


def sds(shape, dtype):
    return jax.ShapeDtypeStruct(tuple(shape), dtype)


def call(
    kernel, name, out_shape, args, scratch=(), place=None, flops=0, vmem=8, space=pltpu.VMEM
):
    many = isinstance(out_shape, (list, tuple))
    outs = list(out_shape) if many else [out_shape]
    specs = [pl.BlockSpec(memory_space=space)] * len(args)
    if place is not None:
        args = (place, *args)
        specs = [pl.BlockSpec(memory_space=pltpu.SMEM), *specs]
    moved = sum(math.prod(a.shape) * jnp.dtype(a.dtype).itemsize for a in (*args, *outs))
    result = pl.pallas_call(
        kernel,
        name=name,
        out_shape=outs,
        in_specs=specs,
        out_specs=[pl.BlockSpec(memory_space=pltpu.VMEM)] * len(outs),
        scratch_shapes=list(scratch),
        cost_estimate=pl.CostEstimate(
            flops=int(flops) // 1000, bytes_accessed=int(moved) // 1000, transcendentals=0
        ),
        compiler_params=pltpu.CompilerParams(vmem_limit_bytes=vmem * MIB),
    )(*args)
    return result if many else result[0]


def lanes(start, size):
    return pl.ds(pl.multiple_of(start, 128), size)


def lines(start, size):
    return pl.ds(pl.multiple_of(start, 16), size)


def norm_stats(summed):
    average = jnp.mean(summed, axis=-1, keepdims=True)
    centered = summed - average
    variance = jnp.mean(centered * centered, axis=-1, keepdims=True)
    inverse = lax.rsqrt(variance + NORM_EPS)
    return centered * inverse, inverse


def norm_grad(shaped, inverse, gains, grad):
    inner = grad * gains
    first = jnp.mean(inner, axis=-1, keepdims=True)
    second = jnp.mean(inner * shaped, axis=-1, keepdims=True)
    return inverse * (inner - first - shaped * second)


SHARE = (
    1.8312406690584326e-09,
    -1.3438994500794415e-07,
    3.981248882617272e-06,
    -5.530906739278176e-05,
    -3.29139111098754e-05,
    0.03633373340914607,
    0.7978847692370962,
)


def normal_share(u, square):
    x = jnp.minimum(square, 36.0)
    p = x * SHARE[0] + SHARE[1]
    for c in SHARE[2:]:
        p = p * x + c
    return jnp.tanh(p * u) * 0.5 + 0.5


def lanes_below(width):
    return lax.broadcasted_iota(jnp.int32, (1, 2 * width), 1) < width


def swap_halves(value):
    width = value.shape[1] // 2
    return jnp.concatenate([value[:, width:], value[:, :width]], axis=1)


def pack_kernel(place, *refs):
    given, (own, a_ref, b_ref, c_ref), held, (small, sems) = (
        refs[:6],
        refs[6:10],
        refs[10:16],
        refs[16:],
    )
    copies = [pltpu.make_async_copy(a, b, sems.at[i]) for i, (a, b) in enumerate(zip(given, held))]
    for copy in copies:
        copy.start()
    for copy in copies:
        copy.wait()
    qkv, out, up, down, proj, vec = held
    vec = vec[...].reshape(1, vec.shape[0])
    odd = (place[0] & 1) == 1
    rows, wide = up.shape
    tile = 128
    half = tile // 2
    full = qkv.shape[1] - half
    after = full + tile
    q, o = qkv[...], out[...]

    def pick(one, two):
        return jnp.where(odd, one, two).astype(BF)

    a_ref[:rows, :full] = pick(q[:, half:], q[:, :full])
    a_ref[:rows, full : full + half] = pick(o[:, :half], q[:, full:])
    a_ref[:rows, full + half : after] = pick(q[:, :half], o[:, tile:])
    a_ref[:rows, after:] = pick(o[:, half:], o[:, :tile])
    small[...] = jnp.zeros_like(small)
    height, width = proj.shape
    for g in range(height // 8):
        small[0:8, g * width : (g + 1) * width] = proj[8 * g : 8 * g + 8, :]
    start = (height // 8) * width
    room = wide - start
    small[0:1, start:] = vec[:, :room]
    left = vec.shape[1] - room
    small[1:2, start : start + left] = vec[:, room:]
    a_ref[rows:, :] = small[...].astype(BF)
    b_ref[...] = up[...].astype(BF)
    across = down.shape[1]
    for h in range(down.shape[0] // rows):
        c_ref[:, h * across : (h + 1) * across] = down[rows * h : rows * (h + 1), :].astype(BF)
    tall = a_ref.shape[0]
    own[:tall, :] = a_ref[...]
    own[tall : tall + rows, :] = b_ref[...]
    own[tall + rows :, :] = c_ref[...]


def pack(place, *given):
    rows, wide = given[2].shape
    tall = rows + 16
    got = call(
        pack_kernel,
        "pack_weights",
        [
            sds((tall + 2 * rows, wide), BF),
            sds((tall, wide), BF),
            sds((rows, wide), BF),
            sds((rows, wide), BF),
            *(sds(a.shape, F32) for a in given),
        ],
        given,
        scratch=[pltpu.VMEM((16, wide), F32), pltpu.SemaphoreType.DMA((len(given),))],
        place=place,
        space=pltpu.HBM,
        vmem=60,
    )
    return got[:4], got[4:]


def split_cores(place, value, rows, mine, theirs, cols):
    first = place[2] == 0
    for z in range(value.shape[0] // (2 * rows)):
        one = value[2 * z * rows : (2 * z + 1) * rows]
        two = value[(2 * z + 1) * rows : (2 * z + 2) * rows]
        mine[z * rows : (z + 1) * rows, cols] = jnp.where(first, one, two)
        theirs[z * rows : (z + 1) * rows, cols] = jnp.where(first, two, one)


def order_kernel(
    marked, rows, place, pos, x, front, rest, frontt, frontt_other, xt, xt_other, back
):
    seqs, length, _ = x.shape
    half = front.shape[1]
    col = lax.broadcasted_iota(jnp.int32, (half, length), 1)
    row = lax.broadcasted_iota(jnp.int32, (half, length), 0)
    before = (
        lax.broadcasted_iota(jnp.int32, (length, length), 0)
        < lax.broadcasted_iota(jnp.int32, (length, length), 1)
    ).astype(BF)
    for s in range(seqs):
        hot = (pos[s] == col) & (row < marked)
        free = 1.0 - jnp.sum(hot.astype(F32), axis=0, keepdims=True)
        rank = nn(jnp.broadcast_to(free, (16, length)).astype(BF), before)[0:1, :]
        target = jnp.where(free > 0.5, rank.astype(jnp.int32) + marked, -1)
        one = jnp.where(hot | (target == row), 1.0, 0.0)
        two = jnp.where(target == (row + half), 1.0, 0.0)
        values = x[s]
        head = nn(one.astype(BF), values)
        front[s] = head.astype(BF)
        rest[s] = nn(two.astype(BF), values).astype(BF)
        at = slice(s * half, (s + 1) * half)
        split_cores(place, head.T.astype(BF), rows, frontt, frontt_other, at)
        at = slice(s * length, (s + 1) * length)
        split_cores(place, values.T, rows, xt, xt_other, at)
        back[s, :, :half] = one.T.astype(BF)
        back[s, :, half:] = two.T.astype(BF)


def order_rows(place, tokens, positions, slots):
    seqs, length, width = tokens.shape
    marked = positions.shape[1]
    half = length // 2
    pos = jnp.pad(positions, ((0, 0), (0, half - marked)), constant_values=-1)[:, :, None]
    rows = sds((seqs, half, width), BF)
    front = sds((width // 2, seqs * half), BF)
    every = sds((width // 2, seqs * length), BF)
    return call(
        functools.partial(order_kernel, marked, width // (2 * slots)),
        "order_rows",
        [rows, rows, front, front, every, every, sds((seqs, length, length), BF)],
        (pos, tokens),
        place=place,
        flops=2 * seqs * length * length * width,
    )


def qkv_kernel(front, rest, x, weight, vec, proj, q_front, q_rest, kv, kvp):
    seqs, half, width = front.shape
    length = x.shape[1]
    piece = width // 2
    for j in range(4):
        cols = slice(j * piece, (j + 1) * piece)
        at = slice(width + j * piece, width + (j + 1) * piece)
        part = nn(x[...].reshape(seqs * length, width), weight[:, at]) + vec[:, at]
        part = part.astype(BF).reshape(seqs, length, piece)
        kv[:, :, cols] = part
        for s in range(seqs):
            kvp[s, :, cols] = nn(proj[...], part[s]).astype(BF)
    for j in range(2):
        cols = slice(j * piece, (j + 1) * piece)
        for given, result in ((front, q_front), (rest, q_rest)):
            part = nn(given[...].reshape(seqs * half, width), weight[:, cols]) + vec[:, cols]
            result[:, :, cols] = part.astype(BF).reshape(seqs, half, piece)


def make_qkv(front, rest, x, weight, vec, proj):
    seqs, half, width = front.shape
    length = x.shape[1]
    rows = proj.shape[0]
    return call(
        qkv_kernel,
        "make_qkv",
        [
            sds(front.shape, BF),
            sds(front.shape, BF),
            sds((seqs, length, 2 * width), BF),
            sds((seqs, rows, 2 * width), BF),
        ],
        (front, rest, x, weight, vec, proj),
        flops=2 * seqs * length * width * width * 3 + 2 * seqs * rows * length * 2 * width,
    )


def pair_of_heads(head, value):
    below = lanes_below(head)
    zero = jnp.zeros_like(value)
    return jnp.concatenate([jnp.where(below, value, zero), jnp.where(below, zero, value)], axis=0)


def attend_kernel(head, q_front, q_rest, kvp, o_front, o_rest):
    seqs, half, width = q_front.shape
    count = kvp.shape[1]
    below = lanes_below(head)
    factor = LOG2E / math.sqrt(head)
    for first in range(0, width, 2 * head):
        at = slice(first, first + 2 * head)
        for s in range(seqs):
            q = jnp.concatenate([q_front[s, :, at], q_rest[s, :, at]], axis=0)
            scores = nt(q, pair_of_heads(head, kvp[s, :, at]))
            weights, scales = [], []
            for h in range(2):
                part = scores[:, h * count : (h + 1) * count]
                e = jnp.exp2((part - jnp.max(part, axis=-1, keepdims=True)) * factor)
                scales.append(1.0 / jnp.sum(e, axis=-1, keepdims=True))
                weights.append(e.astype(BF))
            values = pair_of_heads(head, kvp[s, :, width + first : width + first + 2 * head])
            total = nn(jnp.concatenate(weights, axis=1), values)
            total = (total * jnp.where(below, scales[0], scales[1])).astype(BF)
            o_front[s, :, at] = total[:half]
            o_rest[s, :, at] = total[half:]


def attend(q_front, q_rest, kvp):
    seqs, half, width = q_front.shape
    rows = kvp.shape[1]
    head = width // HEADS
    return call(
        functools.partial(attend_kernel, head),
        "attend",
        [sds(q_front.shape, BF)] * 2,
        (q_front, q_rest, kvp),
        flops=2 * seqs * HEADS * 2 * half * rows * 2 * head * 2,
    )


def join_kernel(marks, keep, rows, place, attended, x, weight, vec, normed, low, *more):
    bias, gain, shift = (vec[:, a:b] for a, b in marks)
    step = 256
    for r in range(0, x.shape[0], step):
        at = slice(r, r + step)
        part = attended[at, :]
        summed = x[at, :].astype(F32) + nn(part, weight[...]) + bias
        shaped, _ = norm_stats(summed)
        result = shaped * gain + shift
        normed[at, :] = result
        low[at, :] = result.astype(BF)
        if keep:
            kept, lowt, lowt_other, attendedt, attendedt_other = more
            kept[at, :] = summed
            split_cores(place, result.T.astype(BF), rows, lowt, lowt_other, at)
            split_cores(place, part.T, rows, attendedt, attendedt_other, at)


def join(place, attended, x, weight, vec, marks, keep, slots):
    rows, width = x.shape
    outs = [sds((rows, width), F32), sds((rows, width), BF)]
    if keep:
        outs += [sds((rows, width), F32)] + [sds((width // 2, rows), BF)] * 4
    return call(
        functools.partial(join_kernel, marks, keep, width // (2 * slots)),
        "join_front" if keep else "join_rest",
        outs,
        (attended, x, weight, vec),
        place=place,
        flops=2 * rows * width * width,
    )


def lift_kernel(mark, keep, chosen, place, low, weight, vec, active, *more):
    rows = low.shape[0]
    piece = weight.shape[2]
    step = 128
    for n, f in enumerate(chosen):
        cols = slice(n * piece, (n + 1) * piece)
        bias = vec[:, mark + f * piece : mark + (f + 1) * piece]
        for r in range(0, rows, step):
            at = slice(r, r + step)
            u = nn(low[at, :], weight[f]) + bias
            square = u * u
            share = normal_share(u, square)
            a = (u * share).astype(BF)
            active[at, cols] = a
            if keep:
                slope, give = more
                bell = jnp.exp2(square * (-0.5 * LOG2E) - 0.5 * math.log2(2.0 * math.pi))
                slope[at, cols] = (share + u * bell).astype(BF)
                half = piece // 2
                give[at, n * half : (n + 1) * half] = jnp.where(
                    place[2] == 0, a[:, half:], a[:, :half]
                )


def lift(place, low, weight, vec, mark, keep, chosen):
    rows, width = low.shape
    piece = weight.shape[2]
    wide = len(chosen) * piece
    outs = [sds((rows, wide), BF)]
    if keep:
        outs += [sds((rows, wide), BF), sds((rows, wide // 2), BF)]
    return call(
        functools.partial(lift_kernel, mark, keep, tuple(chosen)),
        "lift_front" if keep else "lift_rest",
        outs,
        (low, weight, vec),
        place=place,
        flops=2 * rows * width * wide,
    )


def lower_kernel(marks, count, *refs):
    actives, (normed, weight, vec), refs = refs[:count], refs[count : count + 3], refs[count + 3 :]
    bias, gain, shift = (vec[:, a:b] for a, b in marks)
    total = normed[...] + bias
    first = 0
    for active in actives:
        last = first + active.shape[1]
        total = total + nt(active[...], weight[:, first:last])
        first = last
    step = 128
    for r in range(0, normed.shape[0], step):
        at = slice(r, r + step)
        summed = total[at, :]
        shaped, inverse = norm_stats(summed)
        if len(refs) == 1:
            refs[0][at, :] = (shaped * gain + shift).astype(BF)
            continue
        dy, output, d_sum, d_low, d_lowt, sums = refs
        output[at, :] = (shaped * gain + shift).astype(BF)
        grad = dy[at, :].astype(F32)
        back = norm_grad(shaped, inverse, gain, grad)
        d_sum[at, :] = back
        d_low[at, :] = back.astype(BF)
        d_lowt[:, at] = back.T.astype(BF)
        new = [jnp.sum(v, axis=0, keepdims=True) for v in (grad * shaped, grad, back)]
        for i, v in enumerate(new):
            sums[i : i + 1, :] = v if r == 0 else sums[i : i + 1, :] + v


def lower(actives, normed, weight, vec, marks, dy=None):
    rows, width = normed.shape
    full = (rows, width)
    if dy is None:
        outs, more = [sds(full, BF)], ()
    else:
        outs = [
            sds(full, BF),
            sds(full, F32),
            sds(full, BF),
            sds((width, rows), BF),
            sds((8, width), F32),
        ]
        more = (dy,)
    return call(
        functools.partial(lower_kernel, marks, len(actives)),
        "lower_rest" if dy is None else "lower_front",
        outs,
        (*actives, normed, weight, vec, *more),
        flops=2 * rows * width * weight.shape[1],
    )


def hidden_back_kernel(d_low, weight, slope, d_hidden, sums):
    piece = d_low.shape[1]
    for f in range(weight.shape[1] // piece):
        cols = slice(f * piece, (f + 1) * piece)
        du = nn(d_low[...], weight[:, cols]) * slope[:, cols].astype(F32)
        d_hidden[:, cols] = du.astype(BF)
        sums[:, cols] = jnp.sum(du, axis=0, keepdims=True)


def hidden_back(d_low, weight, slope):
    rows, width = d_low.shape
    hidden = weight.shape[1]
    return call(
        hidden_back_kernel,
        "hidden_back",
        [sds((rows, hidden), BF), sds((1, hidden), F32)],
        (d_low, weight, slope),
        flops=2 * rows * width * hidden,
    )


def first_back_kernel(
    marks, d_hidden, up, d_sum, kept, vec, weight, up_sums, two_sums, *refs
):
    d_first, d_low, d_attended, sums = refs
    gain = vec[:, marks[0] : marks[1]]
    parts, _, piece = up.shape
    total = d_sum[...]
    for f in range(parts):
        total = total + nt(d_hidden[:, f * piece : (f + 1) * piece], up[f])
    step = 128
    for r in range(0, d_sum.shape[0], step):
        at = slice(r, r + step)
        grad = total[at, :]
        shaped, inverse = norm_stats(kept[at, :])
        back = norm_grad(shaped, inverse, gain, grad)
        d_first[at, :] = back
        d_low[at, :] = back.astype(BF)
        new = [jnp.sum(v, axis=0, keepdims=True) for v in (grad * shaped, grad, back)]
        for i, v in enumerate(new):
            sums[i : i + 1, :] = v if r == 0 else sums[i : i + 1, :] + v
    d_attended[...] = nt(d_low[...], weight[...]).astype(BF)
    sums[3:6, :] = two_sums[0:3, :]
    for f in range(parts):
        sums[6 + f : 7 + f, :] = up_sums[:, f * piece : (f + 1) * piece]
    sums[6 + parts :, :] = jnp.zeros((sums.shape[0] - 6 - parts, sums.shape[1]), F32)


def first_back(d_hidden, up, d_sum, kept, vec, weight, up_sums, two_sums, marks):
    rows, width = d_sum.shape
    parts, _, piece = up.shape
    full = (rows, width)
    return call(
        functools.partial(first_back_kernel, marks),
        "first_back",
        [sds(full, F32), sds(full, BF), sds(full, BF), sds((16, width), F32)],
        (d_hidden, up, d_sum, kept, vec, weight, up_sums, two_sums),
        flops=2 * rows * width * (parts * piece + width),
    )


def attend_back_kernel(head, s, queries, kvp, grads, result):
    _, half, width = queries.shape
    count = kvp.shape[1]
    below = lanes_below(head)
    scale = 1.0 / math.sqrt(head)
    for first in range(0, width, 2 * head):
        at = slice(first, first + 2 * head)
        q, k, g = queries[s, :, at], kvp[s, :, at], grads[s, :, at]
        v = kvp[s, :, width + first : width + first + 2 * head]
        scores = nt(pair_of_heads(head, k), q)
        d_probs = nt(pair_of_heads(head, v), g)
        probs, d_scores = [], []
        for h in range(2):
            part = scores[h * count : (h + 1) * count]
            e = jnp.exp2((part - jnp.max(part, axis=0, keepdims=True)) * (LOG2E * scale))
            p = e * (1.0 / jnp.sum(e, axis=0, keepdims=True))
            both = p * d_probs[h * count : (h + 1) * count]
            ds = (both - p * jnp.sum(both, axis=0, keepdims=True)) * scale
            probs.append(p.astype(BF))
            d_scores.append(ds.astype(BF))
        dv = nn(jnp.concatenate(probs, axis=0), g)
        dk = nn(jnp.concatenate(d_scores, axis=0), q)
        kt = k.T
        dq = jnp.concatenate([nn(kt[:head], d_scores[0]), nn(kt[head:], d_scores[1])], axis=0)
        result[:half, at] = dq.T.astype(BF)
        result[half : half + count, at] = jnp.where(below, dk[:count], dk[count:]).astype(BF)
        result[half + count :, at] = jnp.where(below, dv[:count], dv[count:]).astype(BF)


def attend_back(s, queries, kvp, grads):
    _, half, width = queries.shape
    rows = kvp.shape[1]
    head = width // HEADS
    return call(
        functools.partial(attend_back_kernel, head, s),
        "attend_back",
        sds((half + 2 * rows, width), BF),
        (queries, kvp, grads),
        flops=2 * HEADS * half * rows * 2 * head * 5,
    )


def input_back_kernel(projt, d_first, weight, back, *refs):
    grads, result = refs[:-1], refs[-1]
    _, half, width = d_first.shape
    rows = projt.shape[1]
    for s, grad in enumerate(grads):
        front = d_first[s] + nt(grad[:half, :], weight[:, :width])
        high = front.astype(BF)
        low = (front - high.astype(F32)).astype(BF)
        place = back[s, :, :half]
        total = nn(place, high) + nn(place, low)
        for j in (1, 2):
            part = nn(projt[...], grad[half + (j - 1) * rows : half + j * rows, :]).astype(BF)
            total = total + nt(part, weight[:, j * width : (j + 1) * width])
        result[s] = total.astype(BF)


def input_back(projt, d_first, weight, back, grads):
    seqs, half, width = d_first.shape
    length = back.shape[1]
    return call(
        input_back_kernel,
        "input_back",
        sds((seqs, length, width), BF),
        (projt, d_first, weight, back, *grads),
        flops=2 * seqs * length * width * (3 * width + length),
    )


def restore_kernel(front, rest, back, result):
    seqs, half, _ = front.shape
    for s in range(seqs):
        total = nn(back[s, :, :half], front[s]) + nn(back[s, :, half:], rest[s])
        result[s] = total.astype(BF)


def restore(front, rest, back):
    seqs, half, width = front.shape
    length = back.shape[1]
    return call(
        restore_kernel,
        "restore_order",
        sds((seqs, length, width), BF),
        (front, rest, back),
        flops=2 * seqs * length * length * width,
    )


def route(rel, slot, send_x, stay_x, send_y, stay_y):
    if slot < 2:
        return (send_x if rel & 1 else stay_x), rel >> 1, slot
    return (send_y if rel & 2 else stay_y), rel & 1, slot - 2


def grad_up_kernel(place, lowt, lowt_other, d_hidden, d_hidden_other, *refs):
    outs, work = refs[:4], refs[4]
    slots, rows, piece = work.shape
    for rel in range(4):
        cols = lanes((rel ^ place[0]) * piece, piece)
        part = nn(lowt[...], d_hidden[:, cols]) + nn(lowt_other[...], d_hidden_other[:, cols])
        work[...] = part.astype(BF).reshape(work.shape)
        for slot in range(slots):
            ref, i, j = route(rel, slot, *outs)
            ref[i, j] = work[(place[1] + slot) % slots]


def grad_up(place, lowt, lowt_other, d_hidden, d_hidden_other, fsdp, slots):
    width, count = lowt.shape
    rows = width // slots
    piece = d_hidden.shape[1] // fsdp
    return call(
        grad_up_kernel,
        "grad_up",
        [sds((2, 2, rows, piece), BF)] * 4,
        (lowt, lowt_other, d_hidden, d_hidden_other),
        scratch=[pltpu.VMEM((slots, rows, piece), BF)],
        place=place,
        flops=2 * width * 2 * count * piece * fsdp,
    )


def grad_down_kernel(place, d_lowt, d_lowt_other, active, active_other, *refs):
    outs, work = refs[:4], refs[4]
    _, _, rows, wide = outs[0].shape
    piece = work.shape[1]
    for slot in range(4):
        z = (place[1] + slot) % 4
        work[...] = (
            nn(d_lowt[...], active[:, lanes((2 * z + place[2]) * piece, piece)])
            + nn(d_lowt_other[...], active_other[:, lanes(z * piece, piece)])
        ).astype(BF)
        for rel in range(4):
            ref, i, j = route(rel, slot, *outs)
            for h in range(wide // piece):
                top = (rel ^ place[0]) * rows * (wide // piece) + h * rows
                ref[i, j, :, h * piece : (h + 1) * piece] = work[lines(top, rows), :]


def grad_down(place, d_lowt, d_lowt_other, active, active_other, rows, slots):
    width, count = d_lowt.shape
    hidden = active.shape[1]
    piece = hidden // (2 * slots)
    return call(
        grad_down_kernel,
        "grad_down",
        [sds((2, 2, rows, width), BF)] * 4,
        (d_lowt, d_lowt_other, active, active_other),
        scratch=[pltpu.VMEM((width, piece), BF)],
        place=place,
        flops=2 * hidden * 2 * count * width,
    )


def grad_rest_kernel(seqs, place, *refs):
    (xt, xt_o, frontt, frontt_o, attendedt, attendedt_o), refs = refs[:6], refs[6:]
    grads, refs = refs[: 2 * seqs], refs[2 * seqs :]
    (d_low, d_low_o, kv, kv_o, sums, sums_o, projt), refs = refs[:7], refs[7:]
    outs, (work_qkv, work_out, work_kv, vector, smalls, small, d_proj) = refs[:4], refs[4:]
    slots, rows, _ = work_qkv.shape
    _, _, tall, wide = outs[0].shape
    fsdp = smalls.shape[0]
    length, count = projt.shape
    width = d_low.shape[1]
    half = d_low.shape[0] // seqs
    first_sums = [None] * 3
    for n, grad in enumerate(grads):
        values = kv if n < seqs else kv_o
        s = n % seqs
        new = [jnp.sum(grad[:half, :].astype(F32), axis=0, keepdims=True)]
        for j in (0, 1):
            part = nn(projt[...], grad[half + j * count : half + (j + 1) * count, :])
            work_kv[n * length : (n + 1) * length, j * width : (j + 1) * width] = part.astype(BF)
            new.append(jnp.sum(part, axis=0, keepdims=True))
        first_sums = new if n == 0 else [a + b for a, b in zip(first_sums, new)]
        both = nt(grad[half : half + count, :], values[s, :, :width]) + nt(
            grad[half + count :, :], values[s, :, width:]
        )
        d_proj[...] = both if n == 0 else d_proj[...] + both

    def both_cores(a, a_o, b, b_o):
        total = nn(a[...], b) + nn(a_o[...], b_o)
        return total.astype(BF).reshape(slots, rows, total.shape[1])

    q_part = None
    for n, grad in enumerate(grads):
        left = frontt if n < seqs else frontt_o
        s = n % seqs
        part = nn(left[:, s * half : (s + 1) * half], grad[:half, :])
        q_part = part if q_part is None else q_part + part
    work_qkv[:, :, :width] = q_part.astype(BF).reshape(slots, rows, width)
    tokens = seqs * length
    for j in range(2):
        cols = slice(j * width, (j + 1) * width)
        work_qkv[:, :, (j + 1) * width : (j + 2) * width] = both_cores(
            xt, xt_o, work_kv[:tokens, cols], work_kv[tokens:, cols]
        )
    work_out[...] = both_cores(attendedt, attendedt_o, d_low[...], d_low_o[...])
    total = sums[...] + sums_o[...]
    at = 0
    for value in (
        *first_sums,
        total[2:3, :],
        *(total[i : i + 1, :] for i in range(6, 6 + vector.shape[1] // width - 9)),
        total[5:6, :],
        *(total[i : i + 1, :] for i in (0, 1, 3, 4)),
    ):
        vector[:, at : at + width] = value
        at += width
    entries = vector.shape[1] // (2 * fsdp * slots)
    height = count // fsdp
    across = length // (2 * slots)
    start = (height // 8) * across
    room = wide - start
    first = place[2] == 0
    small[...] = jnp.zeros_like(small)
    for f in range(fsdp):
        for z in range(slots):
            for g in range(height // 8):
                part = d_proj[
                    f * height + 8 * g : f * height + 8 * g + 8,
                    2 * z * across : 2 * (z + 1) * across,
                ]
                small[0:8, g * across : (g + 1) * across] = jnp.where(
                    first, part[:, :across], part[:, across:]
                )
            base = (f * 2 * slots + 2 * z) * entries
            own = jnp.where(
                first,
                vector[:, base : base + entries],
                vector[:, base + entries : base + 2 * entries],
            )
            small[0:1, start:] = own[:, :room]
            small[1:2, start : start + entries - room] = own[:, room:]
            smalls[f, z] = small[...].astype(BF)
    below = lanes_below(64)
    for rel in range(fsdp):
        f = rel ^ place[0]
        even = (f & 1) == 0
        for slot in range(slots):
            z = (place[1] + slot) % slots
            ref, i, j = route(rel, slot, *outs)
            put = ref.at[i, j]
            q_first = 9 * (f // 2) + 5 * (f & 1)
            o_pair = 3 * (f // 2)
            put[:rows, :512] = work_qkv[z, :, lanes(q_first * 128, 512)]
            shared = work_qkv[z, :, lanes((9 * (f // 2) + 4) * 128, 128)]
            out_shared = work_out[z, :, lanes((o_pair + 1) * 128, 128)]
            put[:rows, 512:640] = jnp.where(below == even, shared, swap_halves(out_shared))
            put[:rows, 640:] = work_out[z, :, lanes((o_pair + 2 * (f & 1)) * 128, 128)]
            put[rows:, :] = smalls[f, z]


def grad_rest(place, lefts, grads, rights, projt, entries, fsdp, slots):
    width, tokens = 2 * lefts[0].shape[0], lefts[0].shape[1]
    rows = width // (2 * slots)
    wide = 4 * width // fsdp
    return call(
        functools.partial(grad_rest_kernel, len(grads) // 2),
        "grad_rest",
        [sds((2, 2, rows + 16, wide), BF)] * 4,
        (*lefts, *grads, *rights, projt),
        scratch=[
            pltpu.VMEM((slots, rows, 3 * width), BF),
            pltpu.VMEM((slots, rows, width), BF),
            pltpu.VMEM((2 * tokens, 2 * width), BF),
            pltpu.VMEM((1, entries), F32),
            pltpu.VMEM((fsdp, slots, 16, wide), BF),
            pltpu.VMEM((16, wide), F32),
            pltpu.VMEM(projt.shape[::-1], F32),
        ],
        place=place,
        flops=width * width * 8 * tokens,
        vmem=20,
    )


def swap_core(value, name="core"):
    n = lax.axis_size("dp")
    with jax.named_scope(name):
        return lax.ppermute(value, "dp", [(i, i ^ 1) for i in range(n)])


def shift_slot(value, by, name="slot"):
    n = lax.axis_size("dp")
    with jax.named_scope(f"{name}_z{by}"):
        return lax.ppermute(value, "dp", [(i, (i + 2 * by) % n) for i in range(n)])


def swap_fsdp(value, bits, name="fsdp"):
    n = lax.axis_size("fsdp")
    with jax.named_scope(f"{name}_{' xyd'[bits]}"):
        return lax.ppermute(value, "fsdp", [(i, i ^ bits) for i in range(n)])


def tie(*values):
    return lax.optimization_barrier(values)


def segments_of(array, tall, blocks, cut, diagonal, low_at, high_at):
    found = []
    for first, back, rows in blocks:
        found += [(array, n * tall + first, n, back, 0, rows) for n in range(3)]
        low = min(max(cut - first, 0), rows)
        if low:
            found.append((diagonal, low_at + first, 3, back, 0, low))
        if low < rows:
            found.append((diagonal, high_at + first + low - cut, 3, back, low, rows - low))
    return found


def block_parts(segments, place, refs, slots):
    arrays = len(refs) // 2
    for other in (0, 1):
        for n, top, bits, back, line, rows in segments:
            z = (place[1] - back + slots) % slots
            ref = refs[other * arrays + n]
            yield ref, top, place[0] ^ bits, 2 * z + (place[2] ^ other), line, rows


def first_whole_kernel(segments, slots, fsdp, height, across, place, *refs):
    count = len(refs) - 8
    blocks = refs[:count]
    qkv, out, vec, proj, projt, halves, smalls, matrix = refs[count:]
    rows = qkv.shape[0] // (2 * slots)
    wide = smalls.shape[3]
    for ref, top, f, d, line, size in block_parts(segments, place, blocks, slots):
        body = min(line + size, rows) - line
        if body > 0:
            src = slice(top, top + body)
            dst = lines(d * rows + line, body)
            qkv[dst, lanes(128 * (9 * (f // 2) + 5 * (f & 1)), 512)] = ref[src, :512]
            halves[f, dst, :] = ref[src, 512:640]
            out[dst, lanes(128 * (3 * (f // 2) + 2 * (f & 1)), 128)] = ref[src, 640:]
        else:
            body = 0
        if body < size:
            smalls[f, d] = ref[top + body : top + size, :]
    entries = vec.shape[1] // (2 * slots * fsdp)
    start = (height // 8) * across
    room = wide - start
    below = lanes_below(64)
    for f in range(fsdp):
        for d in range(2 * slots):
            small = smalls[f, d].astype(F32)
            for g in range(height // 8):
                matrix[
                    f * height + 8 * g : f * height + 8 * g + 8, d * across : (d + 1) * across
                ] = small[0:8, g * across : (g + 1) * across]
            base = (f * 2 * slots + d) * entries
            vec[:, base : base + room] = small[0:1, start:]
            vec[:, base + room : base + entries] = small[1:2, start : start + entries - room]
    for f in range(0, fsdp, 2):
        one, two = halves[f], halves[f + 1]
        at = 128 * (9 * (f // 2) + 4)
        qkv[:, at : at + 128] = jnp.where(below, one, two)
        at = 128 * (3 * (f // 2) + 1)
        out[:, at : at + 128] = swap_halves(jnp.where(below, two, one))
    proj[...] = matrix[...].astype(BF)
    projt[...] = matrix[...].T.astype(BF)


def first_whole(place, blocks, segments, fsdp, slots, width, proj_shape, entries):
    wide = blocks[0].shape[1]
    height, across = proj_shape[0] // fsdp, proj_shape[1] // (2 * slots)
    return call(
        functools.partial(first_whole_kernel, segments, slots, fsdp, height, across),
        "whole_first",
        [
            sds((width, 3 * width), BF),
            sds((width, width), BF),
            sds((1, entries), F32),
            sds(proj_shape, BF),
            sds(proj_shape[::-1], BF),
        ],
        blocks,
        scratch=[
            pltpu.VMEM((fsdp, width, 128), BF),
            pltpu.VMEM((fsdp, 2 * slots, 16, wide), BF),
            pltpu.VMEM(proj_shape, F32),
        ],
        place=place,
    )


def up_whole_kernel(segments, rows, slots, place, *refs):
    blocks, result = refs[:-1], refs[-1]
    for ref, top, f, d, line, size in block_parts(segments, place, blocks, slots):
        result[f, lines(d * rows + line, size), :] = ref[top : top + size, :]


def up_whole(place, blocks, segments, rows, fsdp, slots):
    wide = blocks[0].shape[1]
    return call(
        functools.partial(up_whole_kernel, segments, rows, slots),
        "whole_up",
        sds((fsdp, 2 * slots * rows, wide), BF),
        blocks,
        place=place,
    )


def down_whole_kernel(segments, rows, slots, place, *refs):
    blocks, result = refs[:-1], refs[-1]
    piece = result.shape[1] // (2 * slots)
    parts = blocks[0].shape[1] // piece
    for ref, top, f, d, line, size in block_parts(segments, place, blocks, slots):
        for h in range(parts):
            dst = lines((f * parts + h) * rows + line, size)
            result[dst, lanes(d * piece, piece)] = ref[
                top : top + size, h * piece : (h + 1) * piece
            ]


def down_whole(place, blocks, segments, rows, slots, hidden, width):
    return call(
        functools.partial(down_whole_kernel, segments, rows, slots),
        "whole_down",
        sds((width, hidden), BF),
        blocks,
        place=place,
    )


def stack_kernel(ranges, *refs):
    at = 0
    for (first, last), ref in zip(ranges, refs[:-1]):
        refs[-1][at : at + last - first, :] = ref[first:last, :]
        at += last - first


def stack(*parts):
    arrays, ranges = [p[0] for p in parts], [p[1:] for p in parts]
    rows = sum(b - a for a, b in ranges)
    return call(
        functools.partial(stack_kernel, ranges),
        "stack",
        sds((rows, arrays[0].shape[1]), BF),
        arrays,
    )


def second_stage_kernel(stay_x, from_x, stay_y, from_y, over_y, over_x, kept):
    for stay, came, over, at in ((stay_x, from_x, over_y, 0), (stay_y, from_y, over_x, 1)):
        over[...] = (stay[1].astype(F32) + came[1].astype(F32)).astype(BF)
        kept[at] = (stay[0].astype(F32) + came[0].astype(F32)).astype(BF)


def second_stage(stay_x, from_x, stay_y, from_y):
    shape = stay_x.shape
    return call(
        second_stage_kernel,
        "second_stage",
        [sds(shape[1:], BF), sds(shape[1:], BF), sds(shape, BF)],
        (stay_x, from_x, stay_y, from_y),
    )


def third_stage_kernel(count, *refs):
    ins, owns, sends = refs[: 3 * count], refs[3 * count : 4 * count], refs[4 * count :]
    at = 0
    for n in range(count):
        kept, over_y, over_x = ins[3 * n : 3 * n + 3]
        rows = kept.shape[2]
        put = slice(at, at + rows)
        at += rows
        owns[n][...] = kept[0, 0].astype(F32) + over_y[0].astype(F32)
        sends[0][put, :] = (kept[0, 1].astype(F32) + over_y[1].astype(F32)).astype(BF)
        sends[1][put, :] = (kept[1, 0].astype(F32) + over_x[0].astype(F32)).astype(BF)
        sends[2][put, :] = (kept[1, 1].astype(F32) + over_x[1].astype(F32)).astype(BF)


def third_stage(*pieces):
    shapes = [p[0].shape[2:] for p in pieces]
    rows = sum(a for a, _ in shapes)
    count = len(pieces)
    got = call(
        functools.partial(third_stage_kernel, count),
        "third_stage",
        [sds(a, F32) for a in shapes] + [sds((rows, shapes[0][1]), BF)] * 3,
        [a for p in pieces for a in p],
    )
    return got[:count], got[count:]


def last_stage_kernel(count, *refs):
    owns, (one, two, three) = refs[:count], refs[count : count + 3]
    results, squares = refs[count + 3 : -1], refs[-1]
    at = 0
    sums = None
    for own, result in zip(owns, results):
        put = slice(at, at + own.shape[0])
        at += own.shape[0]
        total = (own[...] + two[put, :].astype(F32)) + (
            one[put, :].astype(F32) + three[put, :].astype(F32)
        )
        result[...] = total
        part = jnp.sum(total * total, axis=0, keepdims=True)
        sums = part if sums is None else sums + part
    squares[...] = jnp.broadcast_to(jnp.sum(sums), squares.shape)


def last_stage(owns, came):
    return call(
        functools.partial(last_stage_kernel, len(owns)),
        "last_stage",
        [sds(a.shape, F32) for a in owns] + [sds((8, 128), F32)],
        (*owns, *came),
    )


def sum_everywhere(value):
    a, b, c = (swap_fsdp(value, k, "norm") for k in (1, 2, 3))
    value = (value + a) + (b + c)
    a, b, c = (shift_slot(value, k, "norm") for k in (1, 2, 3))
    value = (value + b) + (a + c)
    return value + swap_core(value)


def adam(weight, moment, second, grad, scale_clip, rate, decay):
    clipped = grad * scale_clip
    new_moment = BETA_ONE * moment + (1.0 - BETA_ONE) * clipped
    new_second = BETA_TWO * second + (1.0 - BETA_TWO) * clipped * clipped
    moment_hat = new_moment / (1.0 - BETA_ONE**STEP)
    second_hat = new_second / (1.0 - BETA_TWO**STEP)
    new_weight = weight - rate * (moment_hat / (jnp.sqrt(second_hat) + ADAM_EPS) + decay * weight)
    return new_weight, new_moment, new_second, new_weight.astype(BF)


def update_kernel(rates, place, squares, g_first, g_up, g_down, *refs):
    ins, outs = refs[:18], refs[18:-3]
    norm_ref, outs = outs[0], outs[1:]
    vector, wide_work, thin_work = refs[-3:]
    odd = (place[0] & 1) == 1
    norm = jnp.sqrt(squares[0:1, 0:1])
    norm_ref[...] = norm
    clip = jnp.minimum(1.0, CLIP_NORM / norm)

    def put(n, place, grad):
        new = adam(*(ins[3 * n + i][place] for i in range(3)), grad, clip, *rates[n])
        for i in range(4):
            outs[4 * n + i][place] = new[i]

    rows, wide = g_up.shape
    piece = ins[0].shape[1]
    every = (slice(None), slice(None))
    wide_work[:, :64] = g_first[:rows, 576:640]
    wide_work[:, 64:] = g_first[:rows, :512]
    put(0, every, jnp.where(odd, wide_work[...], g_first[:rows, :piece]))

    def thin(full, first, second):
        thin_work[0, :, :128] = full
        thin_work[0, :, 128:] = second
        thin_work[1, :, :64] = first
        thin_work[1, :, 64:] = full
        return jnp.where(odd, thin_work[1], thin_work[0])

    put(1, every, thin(g_first[:rows, 640:], g_first[:rows, 512:576], g_first[:rows, 576:640]))
    put(2, every, g_up[...])
    across = ins[9].shape[1]
    for h in range(wide // across):
        put(
            3,
            (slice(h * rows, (h + 1) * rows), slice(None)),
            g_down[:, h * across : (h + 1) * across],
        )
    height, across = ins[12].shape
    for g in range(height // 8):
        put(
            4,
            (slice(8 * g, 8 * g + 8), slice(None)),
            g_first[rows : rows + 8, g * across : (g + 1) * across],
        )
    start = (height // 8) * across
    room = wide - start
    entries = ins[15].shape[0]
    vector[:, :room] = g_first[rows : rows + 1, start:]
    vector[:, room:] = g_first[rows + 1 : rows + 2, start : start + entries - room]
    state = (ins[15 + i][...].reshape(1, entries) for i in range(3))
    new = adam(*state, vector[...], clip, *rates[5])
    for i in range(4):
        outs[20 + i][...] = new[i].reshape(entries)


def update(place, squares, g_first, g_up, g_down, states, rates):
    outs = [sds((1, 1), F32)]
    for n in range(6):
        shape = states[3 * n].shape
        outs += [sds(shape, F32)] * 3 + [sds(shape, BF)]
    return call(
        functools.partial(update_kernel, rates),
        "update",
        outs,
        (squares, g_first, g_up, g_down, *states),
        scratch=[
            pltpu.VMEM((1, *states[15].shape), F32),
            pltpu.VMEM(states[0].shape, F32),
            pltpu.VMEM((2, *states[3].shape), F32),
        ],
        place=place,
    )


def on_device(
    tokens,
    cotangent,
    positions,
    counts,
    qkv_weight,
    qkv_moment,
    qkv_second,
    out_weight,
    out_moment,
    out_second,
    up_weight,
    up_moment,
    up_second,
    down_projection_weight,
    down_moment,
    down_second,
    proj_weight,
    proj_moment,
    proj_second,
    vec_weight,
    vec_moment,
    vec_second,
):
    fsdp, slots = lax.axis_size("fsdp"), lax.axis_size("dp") // 2
    place = jnp.stack(
        [lax.axis_index("fsdp"), lax.axis_index("dp") // 2, lax.axis_index("dp") % 2]
    ).astype(jnp.int32)
    seqs = counts.shape[0]
    rows, width = tokens.shape
    length = rows // seqs
    half = length // 2
    marked = positions.shape[1]
    hidden = down_projection_weight.shape[0] * slots * 2
    proj_shape = (proj_weight.shape[0] * fsdp, proj_weight.shape[1] * 2 * slots)
    entries = vec_weight.shape[0] * fsdp * 2 * slots
    rates = (
        (RATE_QKV, DECAY_RATE),
        (RATE_OUT, DECAY_RATE),
        (RATE_UP, DECAY_RATE),
        (RATE_DOWN, DECAY_RATE),
        (RATE_PROJ, DECAY_RATE),
        (RATE_VEC, 0.0),
    )

    (own, own_first, own_up, own_down), held = pack(
        place,
        qkv_weight,
        out_weight,
        up_weight,
        down_projection_weight.T,
        proj_weight,
        vec_weight,
    )
    rows_first, rows_up = own_first.shape[0], own_up.shape[0]

    def across(value, name):
        return swap_fsdp(value, 1, name), swap_fsdp(value, 2, name)

    def cores(arrays, name):
        return [swap_core(a, name) for a in arrays]

    back_first = [shift_slot(own_first, k, "first") for k in (1, 2, 3)]
    own_x, own_y = across(own, "own")
    x = tokens.reshape(seqs, length, width)
    front, rest, frontt, frontt_give, xt, xt_give, back = order_rows(place, x, positions, slots)
    live = jnp.arange(marked, dtype=jnp.int32)[None, :] < counts[:, None]
    dy = jnp.pad(
        jnp.where(live[:, :, None], cotangent, jnp.zeros_like(cotangent)),
        ((0, 0), (0, half - marked), (0, 0)),
    ).reshape(seqs * half, width)
    back_first, own_x, own_y, own_up, own_down, own, frontt_give, xt_give, dy, front = tie(
        back_first, own_x, own_y, own_up, own_down, own, frontt_give, xt_give, dy, front
    )

    def all_of(*arrays):
        return stack(*((a, 0, a.shape[0]) for a in arrays))

    far_first = all_of(*back_first)
    first_x, first_y = across(far_first, "first")
    back_up = [shift_slot(own_up, 1, "up"), None, shift_slot(own_up, 3, "up")]
    near = all_of(own, own_x, own_y)
    near_other = swap_core(near, "near_core")
    own_x, own_y, far_first, first_x, first_y, own_up, own_down, near, near_other, back_up = tie(
        own_x, own_y, far_first, first_x, first_y, own_up, own_down, near, near_other, back_up
    )

    tall, far = own.shape[0], far_first.shape[0]
    half_own = tall // 32 * 16
    half_first = (tall + far) // 32 * 16 - half_own
    low = stack((own_x, 0, half_own), (first_x, 0, half_first))
    high = stack((own_y, half_own, tall), (first_y, half_first, far))
    diagonal = [swap_fsdp(low, 2, "diag"), swap_fsdp(high, 1, "diag")]
    back_up[1] = shift_slot(own_up, 2, "up")
    back_down = [shift_slot(own_down, 1, "down"), None, None]
    first = all_of(far_first, first_x, first_y)
    first_other = swap_core(first, "first_core")
    diagonal, first_other, back_up, back_down, own_down = tie(
        diagonal, first_other, back_up, back_down, own_down
    )
    diagonal = all_of(*diagonal)
    diagonal_other = swap_core(diagonal, "diag_core")
    high_at = half_own + half_first

    def near_segments(first, rows):
        return segments_of(0, tall, [(first, 0, rows)], half_own, 1, 0, high_at)

    far_up = all_of(*back_up)
    back_down[1:] = [shift_slot(own_down, k, "down") for k in (2, 3)]
    up_x, up_y = across(far_up, "up")
    blocks = [(k * rows_first, k + 1, rows_first) for k in range(3)]
    qkv_full, out_full, vec, proj, projt = first_whole(
        place,
        [near, diagonal, first, near_other, diagonal_other, first_other],
        near_segments(0, rows_first)
        + segments_of(2, far, blocks, half_first, 1, half_own, high_at + tall - half_own),
        fsdp,
        slots,
        width,
        proj_shape,
        entries,
    )
    q_front, q_rest, kv, kvp = make_qkv(front, rest, x, qkv_full, vec, proj)
    up_x, up_y, q_front, back_down = tie(up_x, up_y, q_front, back_down)
    far_down = all_of(*back_down)

    far = far_up.shape[0]
    half_up = far // 32 * 16
    blocks = [(k * rows_up, k + 1, rows_up) for k in range(3)]

    def far_diagonal(from_x, from_y, name):
        return [swap_fsdp(from_x[:half_up], 2, name), swap_fsdp(from_y[half_up:], 1, name)]

    def rest_segments(first):
        return near_segments(first, rows_up) + segments_of(2, far, blocks, half_up, 3, 0, half_up)

    up_diagonal = far_diagonal(up_x, up_y, "updiag")
    down_x, down_y = across(far_down, "down")
    up = all_of(far_up, up_x, up_y)
    up_other = swap_core(up, "up_core")
    a_front, a_rest = attend(q_front, q_rest, kvp)

    m1 = 3 * width
    m2 = m1 + width
    m3 = m2 + hidden
    m4 = m3 + width
    ends = [m4 + i * width for i in range(5)]
    marks_one = ((m1, m2), (ends[0], ends[1]), (ends[1], ends[2]))
    marks_two = ((m3, m4), (ends[2], ends[3]), (ends[3], ends[4]))

    def flat(v):
        return v.reshape(seqs * half, width)

    h_front, low_front, kept, lowt, lowt_give, attendedt, attendedt_give = join(
        place, flat(a_front), flat(front), out_full, vec, marks_one, True, slots
    )
    up_diagonal, up_other, low_front, lowt_give, attendedt_give, a_rest = tie(
        up_diagonal, up_other, low_front, lowt_give, attendedt_give, a_rest
    )
    up_diagonal = all_of(*up_diagonal)
    up_diagonal_other = swap_core(up_diagonal, "updiag_core")
    h_rest, low_rest = join(
        place, flat(a_rest), flat(rest), out_full, vec, marks_one, False, slots
    )
    up_diagonal_other, low_rest, down_x, down_y = tie(
        up_diagonal_other, low_rest, down_x, down_y
    )
    down_diagonal = far_diagonal(down_x, down_y, "downdiag")
    down = all_of(far_down, down_x, down_y)
    down_other = swap_core(down, "down_core")
    lowt_came, attendedt_came = cores((lowt_give, attendedt_give), "given_core")
    up_full = up_whole(
        place,
        [near, diagonal, up, up_diagonal]
        + [near_other, diagonal_other, up_other, up_diagonal_other],
        rest_segments(rows_first),
        rows_up,
        fsdp,
        slots,
    )
    act_front, slope, act_give = lift(place, low_front, up_full, vec, m2, True, range(fsdp))
    down_diagonal, down_other, act_front, act_give, lowt_came, attendedt_came = tie(
        down_diagonal, down_other, act_front, act_give, lowt_came, attendedt_came
    )
    down_diagonal = all_of(*down_diagonal)
    down_diagonal_other = swap_core(down_diagonal, "downdiag_core")
    down_diagonal, down_diagonal_other, act_give = tie(
        down_diagonal, down_diagonal_other, act_give
    )
    act_came = swap_core(act_give, "given_core")
    down_full = down_whole(
        place,
        [near, diagonal, down, down_diagonal]
        + [near_other, diagonal_other, down_other, down_diagonal_other],
        rest_segments(rows_first + rows_up),
        rows_up,
        slots,
        hidden,
        width,
    )
    out_front, d_sum, d_low, d_lowt, two_sums = lower(
        [act_front], h_front, down_full, vec, marks_two, dy
    )

    def send(parts, name):
        send_x, stay_x, send_y, stay_y = parts
        return swap_fsdp(send_x, 1, name), swap_fsdp(send_y, 2, name), stay_x, stay_y

    def add_up(from_x, from_y, stay_x, stay_y):
        return second_stage(stay_x, from_x, stay_y, from_y)

    def forward(over_y, over_x, kept, name):
        return kept, swap_fsdp(over_y, 2, name), swap_fsdp(over_x, 1, name)

    def along_z(pieces, name):
        owns, parts = third_stage(*pieces)
        return owns, [shift_slot(a, k + 1, name) for k, a in enumerate(parts)]

    d_lowt_came = swap_core(d_lowt, "d_low_core")
    d_hidden, up_sums = hidden_back(d_low, down_full, slope)
    d_lowt_came, d_hidden, act_came, frontt_give, xt_give = tie(
        d_lowt_came, d_hidden, act_came, frontt_give, xt_give
    )
    d_hidden_came = swap_core(d_hidden, "d_hidden_core")
    parts_down = grad_down(place, d_lowt, d_lowt_came, act_front, act_came, rows_up, slots)
    parts_down, d_hidden_came, d_hidden, kv = tie(parts_down, d_hidden_came, d_hidden, kv)
    sent_down = send(parts_down, "gdown")
    kv_came = swap_core(kv, "given_core")
    parts_up = grad_up(place, lowt, lowt_came, d_hidden, d_hidden_came, fsdp, slots)
    frontt_came, xt_came = cores((frontt_give, xt_give), "given_core")
    parts_up, d_hidden, frontt_came, xt_came = tie(parts_up, d_hidden, frontt_came, xt_came)
    d_first, d_first_low, d_attended, sums = first_back(
        d_hidden, up_full, d_sum, kept, vec, out_full, up_sums, two_sums, (ends[0], ends[1])
    )
    d_attended = d_attended.reshape(seqs, half, width)
    grads = [attend_back(0, q_front, kvp, d_attended)]
    grads, d_first_low, sums, sent_down, parts_up, kv_came = tie(
        grads, d_first_low, sums, sent_down, parts_up, kv_came
    )
    over_down = forward(*add_up(*sent_down), "gdown2")
    d_first_low_came, sums_came = cores((d_first_low, sums), "d_low_core")
    grads_came = cores(grads, "d_qkv_core")
    for s in range(1, seqs):
        grads.append(attend_back(s, q_front, kvp, d_attended))
    grads, over_down, d_first_low_came, sums_came, grads_came, parts_up = tie(
        grads, over_down, d_first_low_came, sums_came, grads_came, parts_up
    )
    sent_up = send(parts_up, "gup")
    grads_came = grads_came + cores(grads[1:], "d_qkv_core")
    grads_came, over_down = tie(grads_came, over_down)
    owns_down, (one, two, three) = third_stage(over_down)
    one, three = shift_slot(one, 1, "gdown3"), shift_slot(three, 3, "gdown3")
    parts_first = grad_rest(
        place,
        (xt, xt_came, frontt, frontt_came, attendedt, attendedt_came),
        grads + grads_came,
        (d_first_low, d_first_low_came, kv, kv_came, sums, sums_came),
        projt,
        entries,
        fsdp,
        slots,
    )
    parts_first, low_rest, sent_up, one, two, three = tie(
        parts_first, low_rest, sent_up, one, two, three
    )
    last_down = (owns_down, (one, shift_slot(two, 2, "gdown3"), three))
    over_up = forward(*add_up(*sent_up), "gup2")
    act_rest = lift(place, low_rest, up_full, vec, m2, False, range(fsdp // 2))
    parts_first, act_rest, over_up, last_down, grads, low_rest = tie(
        parts_first, act_rest, over_up, last_down, grads, low_rest
    )
    sent_first = send(parts_first, "gfirst")
    last_up = along_z((over_up,), "gup3")
    act_rest += lift(place, low_rest, up_full, vec, m2, False, range(fsdp // 2, fsdp))
    out_rest = lower(act_rest, h_rest, down_full, vec, marks_two)[0]
    output = restore(
        out_front.reshape(seqs, half, width), out_rest.reshape(seqs, half, width), back
    ).reshape(rows, width)
    sent_first, output, grads, last_up, last_down = tie(
        sent_first, output, grads, last_up, last_down
    )
    over_first = forward(*add_up(*sent_first), "gfirst2")
    g_down, squares_down = last_stage(*last_down)
    g_up, squares_up = last_stage(*last_up)
    over_first, squares_down, squares_up, grads = tie(over_first, squares_down, squares_up, grads)
    last_first = along_z((over_first,), "gfirst3")
    grad_input = input_back(
        projt, d_first.reshape(seqs, half, width), qkv_full, back, grads
    ).reshape(rows, width)
    last_first, grad_input = tie(last_first, grad_input)
    g_first, squares_first = last_stage(*last_first)
    squares_rest = squares_up + squares_down
    squares = sum_everywhere(squares_first + squares_rest)
    moments = (
        (qkv_moment, qkv_second),
        (out_moment, out_second),
        (up_moment, up_second),
        (down_moment.T, down_second.T),
        (proj_moment, proj_second),
        (vec_moment, vec_second),
    )
    states = [a for weight, pair in zip(held, moments) for a in (weight, *pair)]
    new = update(place, squares, g_first, g_up, g_down, states, rates)
    norm, new = new[0].reshape(()), list(new[1:])
    new[12:16] = [v.T for v in new[12:16]]
    return (output, grad_input, norm, *new)


def split_up(value, dim, peers):
    dims = value.shape
    blocks = value.reshape(*dims[:dim], peers, dims[dim] // peers, *dims[dim + 1 :])
    return jnp.moveaxis(blocks, dim, 0)


def sum_at_owner(value, axis, dim):
    blocks = split_up(value, dim, lax.axis_size(axis))
    arrived = lax.all_to_all(blocks, axis, split_axis=0, concat_axis=0, tiled=True)
    return arrived.astype(jnp.float32).sum(axis=0)


def side_by_side(arrays, axis, dim, along):
    ends, at = ([], 0)
    for a in arrays[:-1]:
        at += a.shape[along]
        ends.append(at)
    both = jnp.concatenate(arrays, axis=along)
    return tuple(jnp.split(sum_at_owner(both, axis, dim), ends, axis=along))


def layer_norm(summed, gains, shifts):
    average = jnp.mean(summed, axis=-1, keepdims=True)
    centered = summed - average
    variance = jnp.mean(centered * centered, axis=-1, keepdims=True)
    return centered * lax.rsqrt(variance + NORM_EPS) * gains + shifts


def norm_back(summed, gains, shifts, grad_out):
    result, pullback = jax.vjp(layer_norm, summed, gains, shifts)
    return pullback(grad_out)


def gelu_exact(values):
    return jax.nn.gelu(values, approximate=False)


def split_vector(vec_full, model_width, hidden_width):
    mark_one = 3 * model_width
    mark_two = mark_one + model_width
    mark_three = mark_two + hidden_width
    mark_four = mark_three + model_width
    return (
        vec_full[:mark_one],
        vec_full[mark_one:mark_two],
        vec_full[mark_two:mark_three],
        vec_full[mark_three:mark_four],
        vec_full[mark_four : mark_four + model_width],
        vec_full[mark_four + model_width : mark_four + 2 * model_width],
        vec_full[mark_four + 2 * model_width : mark_four + 3 * model_width],
        vec_full[mark_four + 3 * model_width : mark_four + 4 * model_width],
    )


def adam_update(weight, moment, second, grad, scale_clip, rate, decay):
    clipped = grad * scale_clip
    new_moment = BETA_ONE * moment + (1.0 - BETA_ONE) * clipped
    new_second = BETA_TWO * second + (1.0 - BETA_TWO) * clipped * clipped
    moment_hat = new_moment / (1.0 - BETA_ONE**STEP)
    second_hat = new_second / (1.0 - BETA_TWO**STEP)
    new_weight = weight - rate * (moment_hat / (jnp.sqrt(second_hat) + ADAM_EPS) + decay * weight)
    return (new_weight, new_moment, new_second, new_weight.astype(jnp.bfloat16))


def fetch_whole(low_qkv, low_out, low_up, low_down, low_proj, low_vec):
    rows = (
        lax.all_gather(low_qkv, "dp", axis=0, tiled=True),
        lax.all_gather(low_out, "dp", axis=0, tiled=True),
        lax.all_gather(low_up, "dp", axis=0, tiled=True),
        lax.all_gather(low_down, "dp", axis=0, tiled=True),
        lax.all_gather(low_proj, "dp", axis=1, tiled=True),
        lax.all_gather(low_vec, "dp", axis=0, tiled=True),
    )
    return (
        lax.all_gather(rows[0], "fsdp", axis=1, tiled=True),
        lax.all_gather(rows[1], "fsdp", axis=1, tiled=True),
        lax.all_gather(rows[2], "fsdp", axis=1, tiled=True),
        lax.all_gather(rows[3], "fsdp", axis=1, tiled=True),
        lax.all_gather(rows[4], "fsdp", axis=0, tiled=True),
        lax.all_gather(rows[5], "fsdp", axis=0, tiled=True),
    )


def on_any_mesh(
    tokens,
    cotangent,
    positions,
    counts,
    qkv_weight,
    qkv_moment,
    qkv_second,
    out_weight,
    out_moment,
    out_second,
    up_weight,
    up_moment,
    up_second,
    down_projection_weight,
    down_moment,
    down_second,
    proj_weight,
    proj_moment,
    proj_second,
    vec_weight,
    vec_moment,
    vec_second,
):
    low_qkv = qkv_weight.astype(jnp.bfloat16)
    low_out = out_weight.astype(jnp.bfloat16)
    low_up = up_weight.astype(jnp.bfloat16)
    low_down = down_projection_weight.astype(jnp.bfloat16)
    low_proj = proj_weight.astype(jnp.bfloat16)
    low_vec = vec_weight.astype(jnp.bfloat16)
    qkv_full, out_full, up_full, down_full, projection_gathered, vec_full = fetch_whole(
        low_qkv, low_out, low_up, low_down, low_proj, low_vec
    )
    seq_count = counts.shape[0]
    row_count = tokens.shape[0]
    seq_length = row_count // seq_count
    model_width = tokens.shape[1]
    head_width = model_width // HEADS
    hidden_width = vec_full.shape[0] - 9 * model_width
    proj_rows = projection_gathered.shape[0]
    score_scale = head_width ** (-0.5)
    bias_qkv, bias_out, bias_up, bias_down, gain_one, shift_one, gain_two, shift_two = split_vector(
        vec_full.astype(jnp.float32), model_width, hidden_width
    )
    pre_qkv = jnp.dot(tokens, qkv_full, preferred_element_type=jnp.float32)
    qkv_low = (pre_qkv + bias_qkv).astype(jnp.bfloat16)
    queries = qkv_low[:, :model_width].reshape(seq_count, seq_length, HEADS, head_width)
    key_value_pair = qkv_low[:, model_width:].reshape(seq_count, seq_length, 2 * model_width)
    projected = jnp.einsum(
        "bu,vur->vbr", projection_gathered, key_value_pair, preferred_element_type=jnp.float32
    ).astype(jnp.bfloat16)
    key_heads = projected[:, :, :model_width].reshape(seq_count, proj_rows, HEADS, head_width)
    value_heads = projected[:, :, model_width:].reshape(seq_count, proj_rows, HEADS, head_width)
    scores = (
        jnp.einsum("slhe,sjhe->shlj", queries, key_heads, preferred_element_type=jnp.float32)
        * score_scale
    )
    peak = jnp.max(scores, axis=-1, keepdims=True)
    log_total = peak + jnp.log(jnp.sum(jnp.exp(scores - peak), axis=-1, keepdims=True))
    soft_low = jnp.exp(scores - log_total).astype(jnp.bfloat16)
    context = jnp.einsum(
        "shlj,sjhe->slhe", soft_low, value_heads, preferred_element_type=jnp.float32
    )
    attended = context.reshape(row_count, model_width).astype(jnp.bfloat16)
    first_sum = (
        tokens.astype(jnp.float32)
        + jnp.dot(attended, out_full, preferred_element_type=jnp.float32)
        + bias_out
    )
    normed_one = layer_norm(first_sum, gain_one, shift_one)
    normed_low = normed_one.astype(jnp.bfloat16)
    hidden_pre = jnp.dot(normed_low, up_full, preferred_element_type=jnp.float32) + bias_up
    active = gelu_exact(hidden_pre).astype(jnp.bfloat16)
    second_sum = (
        normed_one + jnp.dot(active, down_full, preferred_element_type=jnp.float32) + bias_down
    )
    output = layer_norm(second_sum, gain_two, shift_two).astype(jnp.bfloat16)
    slot_live = jnp.arange(positions.shape[1], dtype=jnp.int32)[None, :] < counts[:, None]
    one_hot_rows = (
        (positions[:, :, None] == jnp.arange(seq_length, dtype=jnp.int32)[None, None, :])
        & slot_live[:, :, None]
    ).astype(jnp.bfloat16)
    dense = jnp.einsum(
        "bej,bef->bjf", one_hot_rows, cotangent, preferred_element_type=jnp.float32
    ).reshape(row_count, model_width)
    qkv_full, out_full, up_full, down_full, projection_gathered, vec_full = fetch_whole(
        low_qkv, low_out, low_up, low_down, low_proj, low_vec
    )
    d_second, d_gain_two, d_shift_two = norm_back(second_sum, gain_two, shift_two, dense)
    d_bias_down = jnp.sum(d_second, axis=0)
    d_second_low = d_second.astype(jnp.bfloat16)
    grad_down = jnp.einsum("rf,rd->fd", active, d_second_low, preferred_element_type=jnp.float32)
    d_active = jnp.einsum("rd,fd->rf", d_second_low, down_full, preferred_element_type=jnp.float32)
    gelu_value, gelu_pull = jax.vjp(gelu_exact, hidden_pre)
    d_hidden = gelu_pull(d_active)[0]
    d_bias_up = jnp.sum(d_hidden, axis=0)
    d_hidden_low = d_hidden.astype(jnp.bfloat16)
    grad_up = jnp.einsum("rd,rf->df", normed_low, d_hidden_low, preferred_element_type=jnp.float32)
    d_normed = d_second + jnp.einsum(
        "rf,df->rd", d_hidden_low, up_full, preferred_element_type=jnp.float32
    )
    d_first, d_gain_one, d_shift_one = norm_back(first_sum, gain_one, shift_one, d_normed)
    d_bias_out = jnp.sum(d_first, axis=0)
    d_first_low = d_first.astype(jnp.bfloat16)
    grad_out = jnp.einsum("rd,re->de", attended, d_first_low, preferred_element_type=jnp.float32)
    d_attended = jnp.einsum("re,de->rd", d_first_low, out_full, preferred_element_type=jnp.float32)
    d_attended = d_attended.astype(jnp.bfloat16).reshape(seq_count, seq_length, HEADS, head_width)
    scores_again = (
        jnp.einsum("slhe,sjhe->shlj", queries, key_heads, preferred_element_type=jnp.float32)
        * score_scale
    )
    probs_again = jnp.exp(scores_again - log_total)
    probs_low = probs_again.astype(jnp.bfloat16)
    d_value_heads = jnp.einsum(
        "shlj,slhe->sjhe", probs_low, d_attended, preferred_element_type=jnp.float32
    )
    d_probs = jnp.einsum(
        "slhe,sjhe->shlj", d_attended, value_heads, preferred_element_type=jnp.float32
    )
    d_scores = probs_again * (d_probs - jnp.sum(probs_again * d_probs, axis=-1, keepdims=True))
    d_raw_low = (d_scores * score_scale).astype(jnp.bfloat16)
    d_queries = jnp.einsum(
        "shlj,sjhe->slhe", d_raw_low, key_heads, preferred_element_type=jnp.float32
    ).reshape(row_count, model_width)
    d_key_heads = jnp.einsum(
        "shlj,slhe->sjhe", d_raw_low, queries, preferred_element_type=jnp.float32
    )
    projected_gradient = jnp.concatenate(
        [
            d_key_heads.reshape(seq_count, proj_rows, model_width),
            d_value_heads.reshape(seq_count, proj_rows, model_width),
        ],
        axis=-1,
    ).astype(jnp.bfloat16)
    d_kv = jnp.einsum(
        "cq,uct->uqt", projection_gathered, projected_gradient, preferred_element_type=jnp.float32
    ).reshape(row_count, 2 * model_width)
    projection_gradient = jnp.einsum(
        "nhy,nxy->hx", projected_gradient, key_value_pair, preferred_element_type=jnp.float32
    )
    d_qkv = jnp.concatenate([d_queries, d_kv], axis=-1)
    d_bias_qkv = jnp.sum(d_qkv, axis=0)
    d_qkv_low = d_qkv.astype(jnp.bfloat16)
    grad_qkv = jnp.einsum("rd,re->de", tokens, d_qkv_low, preferred_element_type=jnp.float32)
    grad_input = (
        d_first + jnp.einsum("re,de->rd", d_qkv_low, qkv_full, preferred_element_type=jnp.float32)
    ).astype(jnp.bfloat16)
    grad_vec = jnp.concatenate(
        [
            d_bias_qkv,
            d_bias_out,
            d_bias_up,
            d_bias_down,
            d_gain_one,
            d_shift_one,
            d_gain_two,
            d_shift_two,
        ]
    )
    col_part = (
        lax.psum_scatter(
            grad_qkv.astype(jnp.bfloat16), "fsdp", scatter_dimension=1, tiled=True
        ).astype(jnp.float32),
        lax.psum_scatter(
            grad_out.astype(jnp.bfloat16), "fsdp", scatter_dimension=1, tiled=True
        ).astype(jnp.float32),
        lax.psum_scatter(
            grad_up.astype(jnp.bfloat16), "fsdp", scatter_dimension=1, tiled=True
        ).astype(jnp.float32),
        lax.psum_scatter(
            grad_down.astype(jnp.bfloat16), "fsdp", scatter_dimension=1, tiled=True
        ).astype(jnp.float32),
        lax.psum_scatter(
            projection_gradient.astype(jnp.bfloat16), "fsdp", scatter_dimension=0, tiled=True
        ).astype(jnp.float32),
        lax.psum_scatter(
            grad_vec.astype(jnp.bfloat16), "fsdp", scatter_dimension=0, tiled=True
        ).astype(jnp.float32),
    )
    owned = (
        *side_by_side(
            (
                col_part[0].astype(jnp.bfloat16),
                col_part[1].astype(jnp.bfloat16),
                col_part[2].astype(jnp.bfloat16),
            ),
            "dp",
            0,
            1,
        ),
        sum_at_owner(col_part[3].astype(jnp.bfloat16), "dp", 0),
        sum_at_owner(col_part[4].astype(jnp.bfloat16), "dp", 1),
        sum_at_owner(col_part[5].astype(jnp.bfloat16), "dp", 0),
    )
    owned_qkv, owned_out, owned_up, owned_down, owned_proj, owned_vec = owned
    local_squares = (
        jnp.sum(owned_qkv * owned_qkv)
        + jnp.sum(owned_out * owned_out)
        + jnp.sum(owned_up * owned_up)
        + jnp.sum(owned_down * owned_down)
        + jnp.sum(owned_proj * owned_proj)
        + jnp.sum(owned_vec * owned_vec)
    )
    all_squares = lax.psum(local_squares, ("fsdp", "dp"))
    grad_norm = jnp.sqrt(all_squares)
    scale_clip = jnp.minimum(1.0, CLIP_NORM / grad_norm)
    qkv_parts = adam_update(
        qkv_weight, qkv_moment, qkv_second, owned_qkv, scale_clip, RATE_QKV, DECAY_RATE
    )
    out_parts = adam_update(
        out_weight, out_moment, out_second, owned_out, scale_clip, RATE_OUT, DECAY_RATE
    )
    up_parts = adam_update(
        up_weight, up_moment, up_second, owned_up, scale_clip, RATE_UP, DECAY_RATE
    )
    down_parts = adam_update(
        down_projection_weight,
        down_moment,
        down_second,
        owned_down,
        scale_clip,
        RATE_DOWN,
        DECAY_RATE,
    )
    proj_parts = adam_update(
        proj_weight, proj_moment, proj_second, owned_proj, scale_clip, RATE_PROJ, DECAY_RATE
    )
    vec_parts = adam_update(
        vec_weight, vec_moment, vec_second, owned_vec, scale_clip, RATE_VEC, 0.0
    )
    return (
        output,
        grad_input,
        grad_norm,
        qkv_parts[0],
        qkv_parts[1],
        qkv_parts[2],
        qkv_parts[3],
        out_parts[0],
        out_parts[1],
        out_parts[2],
        out_parts[3],
        up_parts[0],
        up_parts[1],
        up_parts[2],
        up_parts[3],
        down_parts[0],
        down_parts[1],
        down_parts[2],
        down_parts[3],
        proj_parts[0],
        proj_parts[1],
        proj_parts[2],
        proj_parts[3],
        vec_parts[0],
        vec_parts[1],
        vec_parts[2],
        vec_parts[3],
    )


def solution(mesh):
    matrix = P("dp", "fsdp")
    tall = P("fsdp", "dp")
    every = P(("fsdp", "dp"))
    small = mesh.shape["fsdp"] == 4 and mesh.shape["dp"] == 8
    return jax.shard_map(
        on_device if small else on_any_mesh,
        mesh=mesh,
        in_specs=(every,) * 4 + (matrix,) * 12 + (tall,) * 3 + (every,) * 3,
        out_specs=(every, every, P()) + (matrix,) * 16 + (tall,) * 4 + (every,) * 4,
        check_vma=False,
    )
```

```python
import functools
import math

import jax
import jax.numpy as jnp
from jax import lax
from jax.experimental import pallas as pl
from jax.experimental.pallas import tpu as pltpu
from jax.sharding import PartitionSpec as P

HEADS = 12
STEP = 10
NORM_EPS = 1e-05
CLIP_NORM = 1.0
BETA_ONE = 0.9
BETA_TWO = 0.999
ADAM_EPS = 1e-08
DECAY_RATE = 0.01
RATE_QKV = 0.05
RATE_OUT = 0.4
RATE_UP = 0.05
RATE_DOWN = 0.05
RATE_PROJ = 0.05
RATE_VEC = 1.0

BF = jnp.bfloat16
F32 = jnp.float32
LOG2E = math.log2(math.e)
MIB = 1 << 20


def nn(a, b):
    return jnp.dot(a, b, preferred_element_type=F32)


def nt(a, b):
    return lax.dot_general(a, b, (((1,), (1,)), ((), ())), preferred_element_type=F32)


def sds(shape, dtype):
    return jax.ShapeDtypeStruct(tuple(shape), dtype)


def call(
    kernel, name, out_shape, args, scratch=(), place=None, flops=0, vmem=8, space=pltpu.VMEM
):
    many = isinstance(out_shape, (list, tuple))
    outs = list(out_shape) if many else [out_shape]
    specs = [pl.BlockSpec(memory_space=space)] * len(args)
    if place is not None:
        args = (place, *args)
        specs = [pl.BlockSpec(memory_space=pltpu.SMEM), *specs]
    moved = sum(math.prod(a.shape) * jnp.dtype(a.dtype).itemsize for a in (*args, *outs))
    result = pl.pallas_call(
        kernel,
        name=name,
        out_shape=outs,
        in_specs=specs,
        out_specs=[pl.BlockSpec(memory_space=pltpu.VMEM)] * len(outs),
        scratch_shapes=list(scratch),
        cost_estimate=pl.CostEstimate(
            flops=int(flops) // 1000, bytes_accessed=int(moved) // 1000, transcendentals=0
        ),
        compiler_params=pltpu.CompilerParams(vmem_limit_bytes=vmem * MIB),
    )(*args)
    return result if many else result[0]


def lanes(start, size):
    return pl.ds(pl.multiple_of(start, 128), size)


def lines(start, size):
    return pl.ds(pl.multiple_of(start, 16), size)


def norm_stats(summed):
    average = jnp.mean(summed, axis=-1, keepdims=True)
    centered = summed - average
    variance = jnp.mean(centered * centered, axis=-1, keepdims=True)
    inverse = lax.rsqrt(variance + NORM_EPS)
    return centered * inverse, inverse


def norm_grad(shaped, inverse, gains, grad):
    inner = grad * gains
    first = jnp.mean(inner, axis=-1, keepdims=True)
    second = jnp.mean(inner * shaped, axis=-1, keepdims=True)
    return inverse * (inner - first - shaped * second)


SHARE = (
    1.8312406690584326e-09,
    -1.3438994500794415e-07,
    3.981248882617272e-06,
    -5.530906739278176e-05,
    -3.29139111098754e-05,
    0.03633373340914607,
    0.7978847692370962,
)


def normal_share(u, square):
    x = jnp.minimum(square, 36.0)
    p = x * SHARE[0] + SHARE[1]
    for c in SHARE[2:]:
        p = p * x + c
    return jnp.tanh(p * u) * 0.5 + 0.5


def lanes_below(width):
    return lax.broadcasted_iota(jnp.int32, (1, 2 * width), 1) < width


def swap_halves(value):
    width = value.shape[1] // 2
    return jnp.concatenate([value[:, width:], value[:, :width]], axis=1)


def pack_kernel(place, *refs):
    given, (own, a_ref, b_ref, c_ref), (small, sems), held = (
        refs[:6],
        refs[6:10],
        refs[10:12],
        refs[12:],
    )
    copies = [pltpu.make_async_copy(a, b, sems.at[i]) for i, (a, b) in enumerate(zip(given, held))]
    for copy in copies:
        copy.start()
    for copy in copies:
        copy.wait()
    qkv, out, up, down, proj, vec = held
    vec = vec[...].reshape(1, vec.shape[0])
    odd = (place[0] & 1) == 1
    rows, wide = up.shape
    tile = 128
    half = tile // 2
    full = qkv.shape[1] - half
    after = full + tile
    q, o = qkv[...], out[...]

    def pick(one, two):
        return jnp.where(odd, one, two).astype(BF)

    a_ref[:rows, :full] = pick(q[:, half:], q[:, :full])
    a_ref[:rows, full : full + half] = pick(o[:, :half], q[:, full:])
    a_ref[:rows, full + half : after] = pick(q[:, :half], o[:, tile:])
    a_ref[:rows, after:] = pick(o[:, half:], o[:, :tile])
    small[...] = jnp.zeros_like(small)
    height, width = proj.shape
    for g in range(height // 8):
        small[0:8, g * width : (g + 1) * width] = proj[8 * g : 8 * g + 8, :]
    start = (height // 8) * width
    room = wide - start
    small[0:1, start:] = vec[:, :room]
    left = vec.shape[1] - room
    small[1:2, start : start + left] = vec[:, room:]
    a_ref[rows:, :] = small[...].astype(BF)
    b_ref[...] = up[...].astype(BF)
    across = down.shape[1]
    for h in range(down.shape[0] // rows):
        c_ref[:, h * across : (h + 1) * across] = down[rows * h : rows * (h + 1), :].astype(BF)
    tall = a_ref.shape[0]
    own[:tall, :] = a_ref[...]
    own[tall : tall + rows, :] = b_ref[...]
    own[tall + rows :, :] = c_ref[...]


def pack(place, *given):
    rows, wide = given[2].shape
    tall = rows + 16
    return call(
        pack_kernel,
        "pack_weights",
        [
            sds((tall + 2 * rows, wide), BF),
            sds((tall, wide), BF),
            sds((rows, wide), BF),
            sds((rows, wide), BF),
        ],
        given,
        scratch=[
            pltpu.VMEM((16, wide), F32),
            pltpu.SemaphoreType.DMA((len(given),)),
            *(pltpu.VMEM(a.shape, F32) for a in given),
        ],
        place=place,
        space=pltpu.HBM,
        vmem=60,
    )


def split_cores(place, value, rows, mine, theirs, cols):
    first = place[2] == 0
    for z in range(value.shape[0] // (2 * rows)):
        one = value[2 * z * rows : (2 * z + 1) * rows]
        two = value[(2 * z + 1) * rows : (2 * z + 2) * rows]
        mine[z * rows : (z + 1) * rows, cols] = jnp.where(first, one, two)
        theirs[z * rows : (z + 1) * rows, cols] = jnp.where(first, two, one)


def order_kernel(
    marked, rows, place, pos, x, front, rest, frontt, frontt_other, xt, xt_other, back
):
    seqs, length, _ = x.shape
    half = front.shape[1]
    col = lax.broadcasted_iota(jnp.int32, (half, length), 1)
    row = lax.broadcasted_iota(jnp.int32, (half, length), 0)
    before = (
        lax.broadcasted_iota(jnp.int32, (length, length), 0)
        < lax.broadcasted_iota(jnp.int32, (length, length), 1)
    ).astype(BF)
    for s in range(seqs):
        hot = (pos[s] == col) & (row < marked)
        free = 1.0 - jnp.sum(hot.astype(F32), axis=0, keepdims=True)
        rank = nn(jnp.broadcast_to(free, (16, length)).astype(BF), before)[0:1, :]
        target = jnp.where(free > 0.5, rank.astype(jnp.int32) + marked, -1)
        one = jnp.where(hot | (target == row), 1.0, 0.0)
        two = jnp.where(target == (row + half), 1.0, 0.0)
        values = x[s]
        head = nn(one.astype(BF), values)
        front[s] = head.astype(BF)
        rest[s] = nn(two.astype(BF), values).astype(BF)
        at = slice(s * half, (s + 1) * half)
        split_cores(place, head.T.astype(BF), rows, frontt, frontt_other, at)
        at = slice(s * length, (s + 1) * length)
        split_cores(place, values.T, rows, xt, xt_other, at)
        back[s, :, :half] = one.T.astype(BF)
        back[s, :, half:] = two.T.astype(BF)


def order_rows(place, tokens, positions, slots):
    seqs, length, width = tokens.shape
    marked = positions.shape[1]
    half = length // 2
    pos = jnp.pad(positions, ((0, 0), (0, half - marked)), constant_values=-1)[:, :, None]
    rows = sds((seqs, half, width), BF)
    front = sds((width // 2, seqs * half), BF)
    every = sds((width // 2, seqs * length), BF)
    return call(
        functools.partial(order_kernel, marked, width // (2 * slots)),
        "order_rows",
        [rows, rows, front, front, every, every, sds((seqs, length, length), BF)],
        (pos, tokens),
        place=place,
        flops=2 * seqs * length * length * width,
    )


def qkv_kernel(front, rest, x, weight, vec, proj, q_front, q_rest, kv, kvp):
    seqs, half, width = front.shape
    length = x.shape[1]
    piece = width // 2
    for j in range(4):
        cols = slice(j * piece, (j + 1) * piece)
        at = slice(width + j * piece, width + (j + 1) * piece)
        part = nn(x[...].reshape(seqs * length, width), weight[:, at]) + vec[:, at]
        part = part.astype(BF).reshape(seqs, length, piece)
        kv[:, :, cols] = part
        for s in range(seqs):
            kvp[s, :, cols] = nn(proj[...], part[s]).astype(BF)
    for j in range(2):
        cols = slice(j * piece, (j + 1) * piece)
        for given, result in ((front, q_front), (rest, q_rest)):
            part = nn(given[...].reshape(seqs * half, width), weight[:, cols]) + vec[:, cols]
            result[:, :, cols] = part.astype(BF).reshape(seqs, half, piece)


def make_qkv(front, rest, x, weight, vec, proj):
    seqs, half, width = front.shape
    length = x.shape[1]
    rows = proj.shape[0]
    return call(
        qkv_kernel,
        "make_qkv",
        [
            sds(front.shape, BF),
            sds(front.shape, BF),
            sds((seqs, length, 2 * width), BF),
            sds((seqs, rows, 2 * width), BF),
        ],
        (front, rest, x, weight, vec, proj),
        flops=2 * seqs * length * width * width * 3 + 2 * seqs * rows * length * 2 * width,
    )


def pair_of_heads(head, value):
    below = lanes_below(head)
    zero = jnp.zeros_like(value)
    return jnp.concatenate([jnp.where(below, value, zero), jnp.where(below, zero, value)], axis=0)


def attend_kernel(head, q_front, q_rest, kvp, o_front, o_rest):
    seqs, half, width = q_front.shape
    count = kvp.shape[1]
    below = lanes_below(head)
    factor = LOG2E / math.sqrt(head)
    for first in range(0, width, 2 * head):
        at = slice(first, first + 2 * head)
        for s in range(seqs):
            q = jnp.concatenate([q_front[s, :, at], q_rest[s, :, at]], axis=0)
            scores = nt(q, pair_of_heads(head, kvp[s, :, at]))
            weights, scales = [], []
            for h in range(2):
                part = scores[:, h * count : (h + 1) * count]
                e = jnp.exp2((part - jnp.max(part, axis=-1, keepdims=True)) * factor)
                scales.append(1.0 / jnp.sum(e, axis=-1, keepdims=True))
                weights.append(e.astype(BF))
            values = pair_of_heads(head, kvp[s, :, width + first : width + first + 2 * head])
            total = nn(jnp.concatenate(weights, axis=1), values)
            total = (total * jnp.where(below, scales[0], scales[1])).astype(BF)
            o_front[s, :, at] = total[:half]
            o_rest[s, :, at] = total[half:]


def attend(q_front, q_rest, kvp):
    seqs, half, width = q_front.shape
    rows = kvp.shape[1]
    head = width // HEADS
    return call(
        functools.partial(attend_kernel, head),
        "attend",
        [sds(q_front.shape, BF)] * 2,
        (q_front, q_rest, kvp),
        flops=2 * seqs * HEADS * 2 * half * rows * 2 * head * 2,
    )


def join_kernel(marks, keep, rows, place, attended, x, weight, vec, normed, low, *more):
    bias, gain, shift = (vec[:, a:b] for a, b in marks)
    step = 256
    for r in range(0, x.shape[0], step):
        at = slice(r, r + step)
        part = attended[at, :]
        summed = x[at, :].astype(F32) + nn(part, weight[...]) + bias
        shaped, _ = norm_stats(summed)
        result = shaped * gain + shift
        normed[at, :] = result
        low[at, :] = result.astype(BF)
        if keep:
            kept, lowt, lowt_other, attendedt, attendedt_other = more
            kept[at, :] = summed
            split_cores(place, result.T.astype(BF), rows, lowt, lowt_other, at)
            split_cores(place, part.T, rows, attendedt, attendedt_other, at)


def join(place, attended, x, weight, vec, marks, keep, slots):
    rows, width = x.shape
    outs = [sds((rows, width), F32), sds((rows, width), BF)]
    if keep:
        outs += [sds((rows, width), F32)] + [sds((width // 2, rows), BF)] * 4
    return call(
        functools.partial(join_kernel, marks, keep, width // (2 * slots)),
        "join_front" if keep else "join_rest",
        outs,
        (attended, x, weight, vec),
        place=place,
        flops=2 * rows * width * width,
    )


def lift_kernel(mark, keep, chosen, place, low, weight, vec, active, *more):
    rows = low.shape[0]
    piece = weight.shape[2]
    step = 128
    for n, f in enumerate(chosen):
        cols = slice(n * piece, (n + 1) * piece)
        bias = vec[:, mark + f * piece : mark + (f + 1) * piece]
        for r in range(0, rows, step):
            at = slice(r, r + step)
            u = nn(low[at, :], weight[f]) + bias
            square = u * u
            share = normal_share(u, square)
            a = (u * share).astype(BF)
            active[at, cols] = a
            if keep:
                slope, give = more
                bell = jnp.exp2(square * (-0.5 * LOG2E) - 0.5 * math.log2(2.0 * math.pi))
                slope[at, cols] = (share + u * bell).astype(BF)
                half = piece // 2
                give[at, n * half : (n + 1) * half] = jnp.where(
                    place[2] == 0, a[:, half:], a[:, :half]
                )


def lift(place, low, weight, vec, mark, keep, chosen):
    rows, width = low.shape
    piece = weight.shape[2]
    wide = len(chosen) * piece
    outs = [sds((rows, wide), BF)]
    if keep:
        outs += [sds((rows, wide), BF), sds((rows, wide // 2), BF)]
    return call(
        functools.partial(lift_kernel, mark, keep, tuple(chosen)),
        "lift_front" if keep else "lift_rest",
        outs,
        (low, weight, vec),
        place=place,
        flops=2 * rows * width * wide,
    )


def lower_kernel(marks, count, *refs):
    actives, (normed, weight, vec), refs = refs[:count], refs[count : count + 3], refs[count + 3 :]
    bias, gain, shift = (vec[:, a:b] for a, b in marks)
    total = normed[...] + bias
    first = 0
    for active in actives:
        last = first + active.shape[1]
        total = total + nt(active[...], weight[:, first:last])
        first = last
    step = 128
    for r in range(0, normed.shape[0], step):
        at = slice(r, r + step)
        summed = total[at, :]
        shaped, inverse = norm_stats(summed)
        if len(refs) == 1:
            refs[0][at, :] = (shaped * gain + shift).astype(BF)
            continue
        dy, output, d_sum, d_low, d_lowt, sums = refs
        output[at, :] = (shaped * gain + shift).astype(BF)
        grad = dy[at, :].astype(F32)
        back = norm_grad(shaped, inverse, gain, grad)
        d_sum[at, :] = back
        d_low[at, :] = back.astype(BF)
        d_lowt[:, at] = back.T.astype(BF)
        new = [jnp.sum(v, axis=0, keepdims=True) for v in (grad * shaped, grad, back)]
        for i, v in enumerate(new):
            sums[i : i + 1, :] = v if r == 0 else sums[i : i + 1, :] + v


def lower(actives, normed, weight, vec, marks, dy=None):
    rows, width = normed.shape
    full = (rows, width)
    if dy is None:
        outs, more = [sds(full, BF)], ()
    else:
        outs = [
            sds(full, BF),
            sds(full, F32),
            sds(full, BF),
            sds((width, rows), BF),
            sds((8, width), F32),
        ]
        more = (dy,)
    return call(
        functools.partial(lower_kernel, marks, len(actives)),
        "lower_rest" if dy is None else "lower_front",
        outs,
        (*actives, normed, weight, vec, *more),
        flops=2 * rows * width * weight.shape[1],
    )


def hidden_back_kernel(d_low, weight, slope, d_hidden, sums):
    piece = d_low.shape[1]
    for f in range(weight.shape[1] // piece):
        cols = slice(f * piece, (f + 1) * piece)
        du = nn(d_low[...], weight[:, cols]) * slope[:, cols].astype(F32)
        d_hidden[:, cols] = du.astype(BF)
        sums[:, cols] = jnp.sum(du, axis=0, keepdims=True)


def hidden_back(d_low, weight, slope):
    rows, width = d_low.shape
    hidden = weight.shape[1]
    return call(
        hidden_back_kernel,
        "hidden_back",
        [sds((rows, hidden), BF), sds((1, hidden), F32)],
        (d_low, weight, slope),
        flops=2 * rows * width * hidden,
    )


def first_back_kernel(
    marks, d_hidden, up, d_sum, kept, vec, weight, up_sums, two_sums, *refs
):
    d_first, d_low, d_attended, sums = refs
    gain = vec[:, marks[0] : marks[1]]
    parts, _, piece = up.shape
    total = d_sum[...]
    for f in range(parts):
        total = total + nt(d_hidden[:, f * piece : (f + 1) * piece], up[f])
    step = 128
    for r in range(0, d_sum.shape[0], step):
        at = slice(r, r + step)
        grad = total[at, :]
        shaped, inverse = norm_stats(kept[at, :])
        back = norm_grad(shaped, inverse, gain, grad)
        d_first[at, :] = back
        d_low[at, :] = back.astype(BF)
        new = [jnp.sum(v, axis=0, keepdims=True) for v in (grad * shaped, grad, back)]
        for i, v in enumerate(new):
            sums[i : i + 1, :] = v if r == 0 else sums[i : i + 1, :] + v
    d_attended[...] = nt(d_low[...], weight[...]).astype(BF)
    sums[3:6, :] = two_sums[0:3, :]
    for f in range(parts):
        sums[6 + f : 7 + f, :] = up_sums[:, f * piece : (f + 1) * piece]
    sums[6 + parts :, :] = jnp.zeros((sums.shape[0] - 6 - parts, sums.shape[1]), F32)


def first_back(d_hidden, up, d_sum, kept, vec, weight, up_sums, two_sums, marks):
    rows, width = d_sum.shape
    parts, _, piece = up.shape
    full = (rows, width)
    return call(
        functools.partial(first_back_kernel, marks),
        "first_back",
        [sds(full, F32), sds(full, BF), sds(full, BF), sds((16, width), F32)],
        (d_hidden, up, d_sum, kept, vec, weight, up_sums, two_sums),
        flops=2 * rows * width * (parts * piece + width),
    )


def attend_back_kernel(head, s, queries, kvp, grads, result):
    _, half, width = queries.shape
    count = kvp.shape[1]
    below = lanes_below(head)
    scale = 1.0 / math.sqrt(head)
    for first in range(0, width, 2 * head):
        at = slice(first, first + 2 * head)
        q, k, g = queries[s, :, at], kvp[s, :, at], grads[s, :, at]
        v = kvp[s, :, width + first : width + first + 2 * head]
        scores = nt(pair_of_heads(head, k), q)
        d_probs = nt(pair_of_heads(head, v), g)
        probs, d_scores = [], []
        for h in range(2):
            part = scores[h * count : (h + 1) * count]
            e = jnp.exp2((part - jnp.max(part, axis=0, keepdims=True)) * (LOG2E * scale))
            p = e * (1.0 / jnp.sum(e, axis=0, keepdims=True))
            both = p * d_probs[h * count : (h + 1) * count]
            ds = (both - p * jnp.sum(both, axis=0, keepdims=True)) * scale
            probs.append(p.astype(BF))
            d_scores.append(ds.astype(BF))
        dv = nn(jnp.concatenate(probs, axis=0), g)
        dk = nn(jnp.concatenate(d_scores, axis=0), q)
        kt = k.T
        dq = jnp.concatenate([nn(kt[:head], d_scores[0]), nn(kt[head:], d_scores[1])], axis=0)
        result[:half, at] = dq.T.astype(BF)
        result[half : half + count, at] = jnp.where(below, dk[:count], dk[count:]).astype(BF)
        result[half + count :, at] = jnp.where(below, dv[:count], dv[count:]).astype(BF)


def attend_back(s, queries, kvp, grads):
    _, half, width = queries.shape
    rows = kvp.shape[1]
    head = width // HEADS
    return call(
        functools.partial(attend_back_kernel, head, s),
        "attend_back",
        sds((half + 2 * rows, width), BF),
        (queries, kvp, grads),
        flops=2 * HEADS * half * rows * 2 * head * 5,
    )


def input_back_kernel(projt, d_first, weight, back, *refs):
    grads, result = refs[:-1], refs[-1]
    _, half, width = d_first.shape
    rows = projt.shape[1]
    for s, grad in enumerate(grads):
        front = d_first[s] + nt(grad[:half, :], weight[:, :width])
        high = front.astype(BF)
        low = (front - high.astype(F32)).astype(BF)
        place = back[s, :, :half]
        total = nn(place, high) + nn(place, low)
        for j in (1, 2):
            part = nn(projt[...], grad[half + (j - 1) * rows : half + j * rows, :]).astype(BF)
            total = total + nt(part, weight[:, j * width : (j + 1) * width])
        result[s] = total.astype(BF)


def input_back(projt, d_first, weight, back, grads):
    seqs, half, width = d_first.shape
    length = back.shape[1]
    return call(
        input_back_kernel,
        "input_back",
        sds((seqs, length, width), BF),
        (projt, d_first, weight, back, *grads),
        flops=2 * seqs * length * width * (3 * width + length),
    )


def restore_kernel(front, rest, back, result):
    seqs, half, _ = front.shape
    for s in range(seqs):
        total = nn(back[s, :, :half], front[s]) + nn(back[s, :, half:], rest[s])
        result[s] = total.astype(BF)


def restore(front, rest, back):
    seqs, half, width = front.shape
    length = back.shape[1]
    return call(
        restore_kernel,
        "restore_order",
        sds((seqs, length, width), BF),
        (front, rest, back),
        flops=2 * seqs * length * length * width,
    )


def route(rel, slot, send_x, stay_x, send_y, stay_y):
    if slot < 2:
        return (send_x if rel & 1 else stay_x), rel >> 1, slot
    return (send_y if rel & 2 else stay_y), rel & 1, slot - 2


def grad_up_kernel(place, lowt, lowt_other, d_hidden, d_hidden_other, *refs):
    outs, work = refs[:4], refs[4]
    slots, rows, piece = work.shape
    for rel in range(4):
        cols = lanes((rel ^ place[0]) * piece, piece)
        part = nn(lowt[...], d_hidden[:, cols]) + nn(lowt_other[...], d_hidden_other[:, cols])
        work[...] = part.astype(BF).reshape(work.shape)
        for slot in range(slots):
            ref, i, j = route(rel, slot, *outs)
            ref[i, j] = work[(place[1] + slot) % slots]


def grad_up(place, lowt, lowt_other, d_hidden, d_hidden_other, fsdp, slots):
    width, count = lowt.shape
    rows = width // slots
    piece = d_hidden.shape[1] // fsdp
    return call(
        grad_up_kernel,
        "grad_up",
        [sds((2, 2, rows, piece), BF)] * 4,
        (lowt, lowt_other, d_hidden, d_hidden_other),
        scratch=[pltpu.VMEM((slots, rows, piece), BF)],
        place=place,
        flops=2 * width * 2 * count * piece * fsdp,
    )


def grad_down_kernel(place, d_lowt, d_lowt_other, active, active_other, *refs):
    outs, work = refs[:4], refs[4]
    _, _, rows, wide = outs[0].shape
    piece = work.shape[1]
    for slot in range(4):
        z = (place[1] + slot) % 4
        work[...] = (
            nn(d_lowt[...], active[:, lanes((2 * z + place[2]) * piece, piece)])
            + nn(d_lowt_other[...], active_other[:, lanes(z * piece, piece)])
        ).astype(BF)
        for rel in range(4):
            ref, i, j = route(rel, slot, *outs)
            for h in range(wide // piece):
                top = (rel ^ place[0]) * rows * (wide // piece) + h * rows
                ref[i, j, :, h * piece : (h + 1) * piece] = work[lines(top, rows), :]


def grad_down(place, d_lowt, d_lowt_other, active, active_other, rows, slots):
    width, count = d_lowt.shape
    hidden = active.shape[1]
    piece = hidden // (2 * slots)
    return call(
        grad_down_kernel,
        "grad_down",
        [sds((2, 2, rows, width), BF)] * 4,
        (d_lowt, d_lowt_other, active, active_other),
        scratch=[pltpu.VMEM((width, piece), BF)],
        place=place,
        flops=2 * hidden * 2 * count * width,
    )


def grad_rest_kernel(seqs, place, *refs):
    (xt, xt_o, frontt, frontt_o, attendedt, attendedt_o), refs = refs[:6], refs[6:]
    grads, refs = refs[: 2 * seqs], refs[2 * seqs :]
    (d_low, d_low_o, kv, kv_o, sums, sums_o, projt), refs = refs[:7], refs[7:]
    outs, (work_qkv, work_out, work_kv, vector, smalls, small, d_proj) = refs[:4], refs[4:]
    slots, rows, _ = work_qkv.shape
    _, _, tall, wide = outs[0].shape
    fsdp = smalls.shape[0]
    length, count = projt.shape
    width = d_low.shape[1]
    half = d_low.shape[0] // seqs
    first_sums = [None] * 3
    for n, grad in enumerate(grads):
        values = kv if n < seqs else kv_o
        s = n % seqs
        new = [jnp.sum(grad[:half, :].astype(F32), axis=0, keepdims=True)]
        for j in (0, 1):
            part = nn(projt[...], grad[half + j * count : half + (j + 1) * count, :])
            work_kv[n * length : (n + 1) * length, j * width : (j + 1) * width] = part.astype(BF)
            new.append(jnp.sum(part, axis=0, keepdims=True))
        first_sums = new if n == 0 else [a + b for a, b in zip(first_sums, new)]
        both = nt(grad[half : half + count, :], values[s, :, :width]) + nt(
            grad[half + count :, :], values[s, :, width:]
        )
        d_proj[...] = both if n == 0 else d_proj[...] + both

    def both_cores(a, a_o, b, b_o):
        total = nn(a[...], b) + nn(a_o[...], b_o)
        return total.astype(BF).reshape(slots, rows, total.shape[1])

    q_part = None
    for n, grad in enumerate(grads):
        left = frontt if n < seqs else frontt_o
        s = n % seqs
        part = nn(left[:, s * half : (s + 1) * half], grad[:half, :])
        q_part = part if q_part is None else q_part + part
    work_qkv[:, :, :width] = q_part.astype(BF).reshape(slots, rows, width)
    tokens = seqs * length
    for j in range(2):
        cols = slice(j * width, (j + 1) * width)
        work_qkv[:, :, (j + 1) * width : (j + 2) * width] = both_cores(
            xt, xt_o, work_kv[:tokens, cols], work_kv[tokens:, cols]
        )
    work_out[...] = both_cores(attendedt, attendedt_o, d_low[...], d_low_o[...])
    total = sums[...] + sums_o[...]
    at = 0
    for value in (
        *first_sums,
        total[2:3, :],
        *(total[i : i + 1, :] for i in range(6, 6 + vector.shape[1] // width - 9)),
        total[5:6, :],
        *(total[i : i + 1, :] for i in (0, 1, 3, 4)),
    ):
        vector[:, at : at + width] = value
        at += width
    entries = vector.shape[1] // (2 * fsdp * slots)
    height = count // fsdp
    across = length // (2 * slots)
    start = (height // 8) * across
    room = wide - start
    first = place[2] == 0
    small[...] = jnp.zeros_like(small)
    for f in range(fsdp):
        for z in range(slots):
            for g in range(height // 8):
                part = d_proj[
                    f * height + 8 * g : f * height + 8 * g + 8,
                    2 * z * across : 2 * (z + 1) * across,
                ]
                small[0:8, g * across : (g + 1) * across] = jnp.where(
                    first, part[:, :across], part[:, across:]
                )
            base = (f * 2 * slots + 2 * z) * entries
            own = jnp.where(
                first,
                vector[:, base : base + entries],
                vector[:, base + entries : base + 2 * entries],
            )
            small[0:1, start:] = own[:, :room]
            small[1:2, start : start + entries - room] = own[:, room:]
            smalls[f, z] = small[...].astype(BF)
    below = lanes_below(64)
    for rel in range(fsdp):
        f = rel ^ place[0]
        even = (f & 1) == 0
        for slot in range(slots):
            z = (place[1] + slot) % slots
            ref, i, j = route(rel, slot, *outs)
            put = ref.at[i, j]
            q_first = 9 * (f // 2) + 5 * (f & 1)
            o_pair = 3 * (f // 2)
            put[:rows, :512] = work_qkv[z, :, lanes(q_first * 128, 512)]
            shared = work_qkv[z, :, lanes((9 * (f // 2) + 4) * 128, 128)]
            out_shared = work_out[z, :, lanes((o_pair + 1) * 128, 128)]
            put[:rows, 512:640] = jnp.where(below == even, shared, swap_halves(out_shared))
            put[:rows, 640:] = work_out[z, :, lanes((o_pair + 2 * (f & 1)) * 128, 128)]
            put[rows:, :] = smalls[f, z]


def grad_rest(place, lefts, grads, rights, projt, entries, fsdp, slots):
    width, tokens = 2 * lefts[0].shape[0], lefts[0].shape[1]
    rows = width // (2 * slots)
    wide = 4 * width // fsdp
    return call(
        functools.partial(grad_rest_kernel, len(grads) // 2),
        "grad_rest",
        [sds((2, 2, rows + 16, wide), BF)] * 4,
        (*lefts, *grads, *rights, projt),
        scratch=[
            pltpu.VMEM((slots, rows, 3 * width), BF),
            pltpu.VMEM((slots, rows, width), BF),
            pltpu.VMEM((2 * tokens, 2 * width), BF),
            pltpu.VMEM((1, entries), F32),
            pltpu.VMEM((fsdp, slots, 16, wide), BF),
            pltpu.VMEM((16, wide), F32),
            pltpu.VMEM(projt.shape[::-1], F32),
        ],
        place=place,
        flops=width * width * 8 * tokens,
        vmem=20,
    )


def swap_core(value, name="core"):
    n = lax.axis_size("dp")
    with jax.named_scope(name):
        return lax.ppermute(value, "dp", [(i, i ^ 1) for i in range(n)])


def shift_slot(value, by, name="slot"):
    n = lax.axis_size("dp")
    with jax.named_scope(f"{name}_z{by}"):
        return lax.ppermute(value, "dp", [(i, (i + 2 * by) % n) for i in range(n)])


def swap_fsdp(value, bits, name="fsdp"):
    n = lax.axis_size("fsdp")
    with jax.named_scope(f"{name}_{' xyd'[bits]}"):
        return lax.ppermute(value, "fsdp", [(i, i ^ bits) for i in range(n)])


def tie(*values):
    return lax.optimization_barrier(values)


def segments_of(array, tall, blocks, cut, diagonal, low_at, high_at):
    found = []
    for first, back, rows in blocks:
        found += [(array, n * tall + first, n, back, 0, rows) for n in range(3)]
        low = min(max(cut - first, 0), rows)
        if low:
            found.append((diagonal, low_at + first, 3, back, 0, low))
        if low < rows:
            found.append((diagonal, high_at + first + low - cut, 3, back, low, rows - low))
    return found


def block_parts(segments, place, refs, slots):
    arrays = len(refs) // 2
    for other in (0, 1):
        for n, top, bits, back, line, rows in segments:
            z = (place[1] - back + slots) % slots
            ref = refs[other * arrays + n]
            yield ref, top, place[0] ^ bits, 2 * z + (place[2] ^ other), line, rows


def first_whole_kernel(segments, slots, fsdp, height, across, place, *refs):
    count = len(refs) - 8
    blocks = refs[:count]
    qkv, out, vec, proj, projt, halves, smalls, matrix = refs[count:]
    rows = qkv.shape[0] // (2 * slots)
    wide = smalls.shape[3]
    for ref, top, f, d, line, size in block_parts(segments, place, blocks, slots):
        body = min(line + size, rows) - line
        if body > 0:
            src = slice(top, top + body)
            dst = lines(d * rows + line, body)
            qkv[dst, lanes(128 * (9 * (f // 2) + 5 * (f & 1)), 512)] = ref[src, :512]
            halves[f, dst, :] = ref[src, 512:640]
            out[dst, lanes(128 * (3 * (f // 2) + 2 * (f & 1)), 128)] = ref[src, 640:]
        else:
            body = 0
        if body < size:
            smalls[f, d] = ref[top + body : top + size, :]
    entries = vec.shape[1] // (2 * slots * fsdp)
    start = (height // 8) * across
    room = wide - start
    below = lanes_below(64)
    for f in range(fsdp):
        for d in range(2 * slots):
            small = smalls[f, d].astype(F32)
            for g in range(height // 8):
                matrix[
                    f * height + 8 * g : f * height + 8 * g + 8, d * across : (d + 1) * across
                ] = small[0:8, g * across : (g + 1) * across]
            base = (f * 2 * slots + d) * entries
            vec[:, base : base + room] = small[0:1, start:]
            vec[:, base + room : base + entries] = small[1:2, start : start + entries - room]
    for f in range(0, fsdp, 2):
        one, two = halves[f], halves[f + 1]
        at = 128 * (9 * (f // 2) + 4)
        qkv[:, at : at + 128] = jnp.where(below, one, two)
        at = 128 * (3 * (f // 2) + 1)
        out[:, at : at + 128] = swap_halves(jnp.where(below, two, one))
    proj[...] = matrix[...].astype(BF)
    projt[...] = matrix[...].T.astype(BF)


def first_whole(place, blocks, segments, fsdp, slots, width, proj_shape, entries):
    wide = blocks[0].shape[1]
    height, across = proj_shape[0] // fsdp, proj_shape[1] // (2 * slots)
    return call(
        functools.partial(first_whole_kernel, segments, slots, fsdp, height, across),
        "whole_first",
        [
            sds((width, 3 * width), BF),
            sds((width, width), BF),
            sds((1, entries), F32),
            sds(proj_shape, BF),
            sds(proj_shape[::-1], BF),
        ],
        blocks,
        scratch=[
            pltpu.VMEM((fsdp, width, 128), BF),
            pltpu.VMEM((fsdp, 2 * slots, 16, wide), BF),
            pltpu.VMEM(proj_shape, F32),
        ],
        place=place,
    )


def up_whole_kernel(segments, rows, slots, place, *refs):
    blocks, result = refs[:-1], refs[-1]
    for ref, top, f, d, line, size in block_parts(segments, place, blocks, slots):
        result[f, lines(d * rows + line, size), :] = ref[top : top + size, :]


def up_whole(place, blocks, segments, rows, fsdp, slots):
    wide = blocks[0].shape[1]
    return call(
        functools.partial(up_whole_kernel, segments, rows, slots),
        "whole_up",
        sds((fsdp, 2 * slots * rows, wide), BF),
        blocks,
        place=place,
    )


def down_whole_kernel(segments, rows, slots, place, *refs):
    blocks, result = refs[:-1], refs[-1]
    piece = result.shape[1] // (2 * slots)
    parts = blocks[0].shape[1] // piece
    for ref, top, f, d, line, size in block_parts(segments, place, blocks, slots):
        for h in range(parts):
            dst = lines((f * parts + h) * rows + line, size)
            result[dst, lanes(d * piece, piece)] = ref[
                top : top + size, h * piece : (h + 1) * piece
            ]


def down_whole(place, blocks, segments, rows, slots, hidden, width):
    return call(
        functools.partial(down_whole_kernel, segments, rows, slots),
        "whole_down",
        sds((width, hidden), BF),
        blocks,
        place=place,
    )


def stack_kernel(ranges, *refs):
    at = 0
    for (first, last), ref in zip(ranges, refs[:-1]):
        refs[-1][at : at + last - first, :] = ref[first:last, :]
        at += last - first


def stack(*parts):
    arrays, ranges = [p[0] for p in parts], [p[1:] for p in parts]
    rows = sum(b - a for a, b in ranges)
    return call(
        functools.partial(stack_kernel, ranges),
        "stack",
        sds((rows, arrays[0].shape[1]), BF),
        arrays,
    )


def second_stage_kernel(stay_x, from_x, stay_y, from_y, over_y, over_x, kept):
    for stay, came, over, at in ((stay_x, from_x, over_y, 0), (stay_y, from_y, over_x, 1)):
        over[...] = (stay[1].astype(F32) + came[1].astype(F32)).astype(BF)
        kept[at] = (stay[0].astype(F32) + came[0].astype(F32)).astype(BF)


def second_stage(stay_x, from_x, stay_y, from_y):
    shape = stay_x.shape
    return call(
        second_stage_kernel,
        "second_stage",
        [sds(shape[1:], BF), sds(shape[1:], BF), sds(shape, BF)],
        (stay_x, from_x, stay_y, from_y),
    )


def third_stage_kernel(count, *refs):
    ins, owns, sends = refs[: 3 * count], refs[3 * count : 4 * count], refs[4 * count :]
    at = 0
    for n in range(count):
        kept, over_y, over_x = ins[3 * n : 3 * n + 3]
        rows = kept.shape[2]
        put = slice(at, at + rows)
        at += rows
        owns[n][...] = kept[0, 0].astype(F32) + over_y[0].astype(F32)
        sends[0][put, :] = (kept[0, 1].astype(F32) + over_y[1].astype(F32)).astype(BF)
        sends[1][put, :] = (kept[1, 0].astype(F32) + over_x[0].astype(F32)).astype(BF)
        sends[2][put, :] = (kept[1, 1].astype(F32) + over_x[1].astype(F32)).astype(BF)


def third_stage(*pieces):
    shapes = [p[0].shape[2:] for p in pieces]
    rows = sum(a for a, _ in shapes)
    count = len(pieces)
    got = call(
        functools.partial(third_stage_kernel, count),
        "third_stage",
        [sds(a, F32) for a in shapes] + [sds((rows, shapes[0][1]), BF)] * 3,
        [a for p in pieces for a in p],
    )
    return got[:count], got[count:]


def last_stage_kernel(count, *refs):
    owns, (one, two, three) = refs[:count], refs[count : count + 3]
    results, squares = refs[count + 3 : -1], refs[-1]
    at = 0
    sums = None
    for own, result in zip(owns, results):
        put = slice(at, at + own.shape[0])
        at += own.shape[0]
        total = (own[...] + two[put, :].astype(F32)) + (
            one[put, :].astype(F32) + three[put, :].astype(F32)
        )
        result[...] = total
        part = jnp.sum(total * total, axis=0, keepdims=True)
        sums = part if sums is None else sums + part
    squares[...] = jnp.broadcast_to(jnp.sum(sums), squares.shape)


def last_stage(owns, came):
    return call(
        functools.partial(last_stage_kernel, len(owns)),
        "last_stage",
        [sds(a.shape, F32) for a in owns] + [sds((8, 128), F32)],
        (*owns, *came),
    )


def sum_everywhere(value):
    a, b, c = (shift_slot(value, k, "norm") for k in (1, 2, 3))
    value = (value + b) + (a + c)
    value = value + swap_core(value)
    a, b, c = (swap_fsdp(value, k, "norm") for k in (1, 2, 3))
    return (value + a) + (b + c)


def adam(weight, moment, second, grad, scale_clip, rate, decay):
    clipped = grad * scale_clip
    new_moment = BETA_ONE * moment + (1.0 - BETA_ONE) * clipped
    new_second = BETA_TWO * second + (1.0 - BETA_TWO) * clipped * clipped
    moment_hat = new_moment / (1.0 - BETA_ONE**STEP)
    second_hat = new_second / (1.0 - BETA_TWO**STEP)
    new_weight = weight - rate * (moment_hat / (jnp.sqrt(second_hat) + ADAM_EPS) + decay * weight)
    return new_weight, new_moment, new_second, new_weight.astype(BF)


def update_kernel(rates, place, squares, g_first, g_up, g_down, *refs):
    ins, outs = refs[:18], refs[18:-3]
    norm_ref, outs = outs[0], outs[1:]
    vector, wide_work, thin_work = refs[-3:]
    odd = (place[0] & 1) == 1
    norm = jnp.sqrt(squares[0:1, 0:1])
    norm_ref[...] = norm
    clip = jnp.minimum(1.0, CLIP_NORM / norm)

    def put(n, place, grad):
        new = adam(*(ins[3 * n + i][place] for i in range(3)), grad, clip, *rates[n])
        for i in range(4):
            outs[4 * n + i][place] = new[i]

    rows, wide = g_up.shape
    piece = ins[0].shape[1]
    every = (slice(None), slice(None))
    wide_work[:, :64] = g_first[:rows, 576:640]
    wide_work[:, 64:] = g_first[:rows, :512]
    put(0, every, jnp.where(odd, wide_work[...], g_first[:rows, :piece]))

    def thin(full, first, second):
        thin_work[0, :, :128] = full
        thin_work[0, :, 128:] = second
        thin_work[1, :, :64] = first
        thin_work[1, :, 64:] = full
        return jnp.where(odd, thin_work[1], thin_work[0])

    put(1, every, thin(g_first[:rows, 640:], g_first[:rows, 512:576], g_first[:rows, 576:640]))
    put(2, every, g_up[...])
    across = ins[9].shape[1]
    for h in range(wide // across):
        put(
            3,
            (slice(h * rows, (h + 1) * rows), slice(None)),
            g_down[:, h * across : (h + 1) * across],
        )
    height, across = ins[12].shape
    for g in range(height // 8):
        put(
            4,
            (slice(8 * g, 8 * g + 8), slice(None)),
            g_first[rows : rows + 8, g * across : (g + 1) * across],
        )
    start = (height // 8) * across
    room = wide - start
    entries = ins[15].shape[0]
    vector[:, :room] = g_first[rows : rows + 1, start:]
    vector[:, room:] = g_first[rows + 1 : rows + 2, start : start + entries - room]
    state = (ins[15 + i][...].reshape(1, entries) for i in range(3))
    new = adam(*state, vector[...], clip, *rates[5])
    for i in range(4):
        outs[20 + i][...] = new[i].reshape(entries)


def update(place, squares, g_first, g_up, g_down, states, rates):
    outs = [sds((1, 1), F32)]
    for n in range(6):
        shape = states[3 * n].shape
        outs += [sds(shape, F32)] * 3 + [sds(shape, BF)]
    return call(
        functools.partial(update_kernel, rates),
        "update",
        outs,
        (squares, g_first, g_up, g_down, *states),
        scratch=[
            pltpu.VMEM((1, *states[15].shape), F32),
            pltpu.VMEM(states[0].shape, F32),
            pltpu.VMEM((2, *states[3].shape), F32),
        ],
        place=place,
    )


def on_device(
    tokens,
    cotangent,
    positions,
    counts,
    qkv_weight,
    qkv_moment,
    qkv_second,
    out_weight,
    out_moment,
    out_second,
    up_weight,
    up_moment,
    up_second,
    down_projection_weight,
    down_moment,
    down_second,
    proj_weight,
    proj_moment,
    proj_second,
    vec_weight,
    vec_moment,
    vec_second,
):
    fsdp, slots = lax.axis_size("fsdp"), lax.axis_size("dp") // 2
    place = jnp.stack(
        [lax.axis_index("fsdp"), lax.axis_index("dp") // 2, lax.axis_index("dp") % 2]
    ).astype(jnp.int32)
    seqs = counts.shape[0]
    rows, width = tokens.shape
    length = rows // seqs
    half = length // 2
    marked = positions.shape[1]
    hidden = down_projection_weight.shape[0] * slots * 2
    proj_shape = (proj_weight.shape[0] * fsdp, proj_weight.shape[1] * 2 * slots)
    entries = vec_weight.shape[0] * fsdp * 2 * slots
    rates = (
        (RATE_QKV, DECAY_RATE),
        (RATE_OUT, DECAY_RATE),
        (RATE_UP, DECAY_RATE),
        (RATE_DOWN, DECAY_RATE),
        (RATE_PROJ, DECAY_RATE),
        (RATE_VEC, 0.0),
    )

    own, own_first, own_up, own_down = pack(
        place,
        qkv_weight,
        out_weight,
        up_weight,
        down_projection_weight.T,
        proj_weight,
        vec_weight,
    )
    rows_first, rows_up = own_first.shape[0], own_up.shape[0]

    def across(value, name):
        return swap_fsdp(value, 1, name), swap_fsdp(value, 2, name)

    def cores(arrays, name):
        return [swap_core(a, name) for a in arrays]

    back_first = [shift_slot(own_first, k, "first") for k in (1, 2, 3)]
    own_x, own_y = across(own, "own")
    x = tokens.reshape(seqs, length, width)
    front, rest, frontt, frontt_give, xt, xt_give, back = order_rows(place, x, positions, slots)
    live = jnp.arange(marked, dtype=jnp.int32)[None, :] < counts[:, None]
    dy = jnp.pad(
        jnp.where(live[:, :, None], cotangent, jnp.zeros_like(cotangent)),
        ((0, 0), (0, half - marked), (0, 0)),
    ).reshape(seqs * half, width)
    back_first, own_x, own_y, own_up, own_down, own, frontt_give, xt_give, dy, front = tie(
        back_first, own_x, own_y, own_up, own_down, own, frontt_give, xt_give, dy, front
    )

    def all_of(*arrays):
        return stack(*((a, 0, a.shape[0]) for a in arrays))

    far_first = all_of(*back_first)
    first_x, first_y = across(far_first, "first")
    back_up = [shift_slot(own_up, k, "up") for k in (1, 2, 3)]
    near = all_of(own, own_x, own_y)
    own_x, own_y, far_first, first_x, first_y, own_down, near, back_up = tie(
        own_x, own_y, far_first, first_x, first_y, own_down, near, back_up
    )

    tall, far = own.shape[0], far_first.shape[0]
    half_own = tall // 32 * 16
    half_first = (tall + far) // 32 * 16 - half_own
    low = stack((own_x, 0, half_own), (first_x, 0, half_first))
    high = stack((own_y, half_own, tall), (first_y, half_first, far))
    diagonal = [swap_fsdp(low, 2, "diag"), swap_fsdp(high, 1, "diag")]
    back_down = [shift_slot(own_down, 1, "down"), None, shift_slot(own_down, 3, "down")]
    near_other = swap_core(near, "near_core")
    first = all_of(far_first, first_x, first_y)
    first_other = swap_core(first, "first_core")
    diagonal, first_other, near_other, back_down, own_down = tie(
        diagonal, first_other, near_other, back_down, own_down
    )
    diagonal = all_of(*diagonal)
    diagonal_other = swap_core(diagonal, "diag_core")
    high_at = half_own + half_first

    def near_segments(first, rows):
        return segments_of(0, tall, [(first, 0, rows)], half_own, 1, 0, high_at)

    far_up = all_of(*back_up)
    back_down[1] = shift_slot(own_down, 2, "down")
    up_x, up_y = across(far_up, "up")
    blocks = [(k * rows_first, k + 1, rows_first) for k in range(3)]
    qkv_full, out_full, vec, proj, projt = first_whole(
        place,
        [near, diagonal, first, near_other, diagonal_other, first_other],
        near_segments(0, rows_first)
        + segments_of(2, far, blocks, half_first, 1, half_own, high_at + tall - half_own),
        fsdp,
        slots,
        width,
        proj_shape,
        entries,
    )
    q_front, q_rest, kv, kvp = make_qkv(front, rest, x, qkv_full, vec, proj)
    up_x, up_y, q_front, back_down = tie(up_x, up_y, q_front, back_down)
    far_down = all_of(*back_down)

    far = far_up.shape[0]
    half_up = far // 32 * 16
    blocks = [(k * rows_up, k + 1, rows_up) for k in range(3)]

    def far_diagonal(from_x, from_y, name):
        return [swap_fsdp(from_x[:half_up], 2, name), swap_fsdp(from_y[half_up:], 1, name)]

    def rest_segments(first):
        return near_segments(first, rows_up) + segments_of(2, far, blocks, half_up, 3, 0, half_up)

    up_diagonal = far_diagonal(up_x, up_y, "updiag")
    down_x, down_y = across(far_down, "down")
    up = all_of(far_up, up_x, up_y)
    up_other = swap_core(up, "up_core")
    a_front, a_rest = attend(q_front, q_rest, kvp)

    m1 = 3 * width
    m2 = m1 + width
    m3 = m2 + hidden
    m4 = m3 + width
    ends = [m4 + i * width for i in range(5)]
    marks_one = ((m1, m2), (ends[0], ends[1]), (ends[1], ends[2]))
    marks_two = ((m3, m4), (ends[2], ends[3]), (ends[3], ends[4]))

    def flat(v):
        return v.reshape(seqs * half, width)

    h_front, low_front, kept, lowt, lowt_give, attendedt, attendedt_give = join(
        place, flat(a_front), flat(front), out_full, vec, marks_one, True, slots
    )
    up_diagonal, up_other, low_front, lowt_give, attendedt_give, a_rest = tie(
        up_diagonal, up_other, low_front, lowt_give, attendedt_give, a_rest
    )
    up_diagonal = all_of(*up_diagonal)
    up_diagonal_other = swap_core(up_diagonal, "updiag_core")
    up_diagonal_other, down_x, down_y = tie(up_diagonal_other, down_x, down_y)
    down_diagonal = far_diagonal(down_x, down_y, "downdiag")
    down = all_of(far_down, down_x, down_y)
    down_other = swap_core(down, "down_core")
    lowt_came, attendedt_came = cores((lowt_give, attendedt_give), "given_core")
    up_full = up_whole(
        place,
        [near, diagonal, up, up_diagonal]
        + [near_other, diagonal_other, up_other, up_diagonal_other],
        rest_segments(rows_first),
        rows_up,
        fsdp,
        slots,
    )
    act_front, slope, act_give = lift(place, low_front, up_full, vec, m2, True, range(fsdp))
    down_diagonal, down_other, act_front, act_give, lowt_came, attendedt_came = tie(
        down_diagonal, down_other, act_front, act_give, lowt_came, attendedt_came
    )
    down_diagonal = all_of(*down_diagonal)
    down_diagonal_other = swap_core(down_diagonal, "downdiag_core")
    down_diagonal, down_diagonal_other, act_give = tie(
        down_diagonal, down_diagonal_other, act_give
    )
    act_came = swap_core(act_give, "given_core")
    down_full = down_whole(
        place,
        [near, diagonal, down, down_diagonal]
        + [near_other, diagonal_other, down_other, down_diagonal_other],
        rest_segments(rows_first + rows_up),
        rows_up,
        slots,
        hidden,
        width,
    )
    out_front, d_sum, d_low, d_lowt, two_sums = lower(
        [act_front], h_front, down_full, vec, marks_two, dy
    )

    def send(parts, name):
        send_x, stay_x, send_y, stay_y = parts
        return swap_fsdp(send_x, 1, name), swap_fsdp(send_y, 2, name), stay_x, stay_y

    def add_up(from_x, from_y, stay_x, stay_y):
        return second_stage(stay_x, from_x, stay_y, from_y)

    def forward(over_y, over_x, kept, name):
        return kept, swap_fsdp(over_y, 2, name), swap_fsdp(over_x, 1, name)

    def along_z(pieces, name):
        owns, parts = third_stage(*pieces)
        return owns, [shift_slot(a, k + 1, name) for k, a in enumerate(parts)]

    d_lowt_came = swap_core(d_lowt, "d_low_core")
    h_rest, low_rest = join(
        place, flat(a_rest), flat(rest), out_full, vec, marks_one, False, slots
    )
    d_lowt_came, act_came, low_rest, frontt_give, xt_give = tie(
        d_lowt_came, act_came, low_rest, frontt_give, xt_give
    )
    parts_down = grad_down(place, d_lowt, d_lowt_came, act_front, act_came, rows_up, slots)
    parts_down, d_low = tie(parts_down, d_low)
    sent_down = send(parts_down, "gdown")
    frontt_came, xt_came = cores((frontt_give, xt_give), "given_core")
    d_hidden, up_sums = hidden_back(d_low, down_full, slope)
    d_hidden_came = swap_core(d_hidden, "d_hidden_core")
    d_first, d_first_low, d_attended, sums = first_back(
        d_hidden, up_full, d_sum, kept, vec, out_full, up_sums, two_sums, (ends[0], ends[1])
    )
    d_attended = d_attended.reshape(seqs, half, width)
    grads = [attend_back(0, q_front, kvp, d_attended)]
    grads, d_first_low, sums, sent_down, kv, frontt_came, xt_came = tie(
        grads, d_first_low, sums, sent_down, kv, frontt_came, xt_came
    )
    over_down = forward(*add_up(*sent_down), "gdown2")
    d_first_low_came = swap_core(d_first_low, "d_low_core")
    grads_came = cores(grads, "d_qkv_core")
    kv_came = swap_core(kv, "given_core")
    for s in range(1, seqs):
        grads.append(attend_back(s, q_front, kvp, d_attended))
    parts_up = grad_up(place, lowt, lowt_came, d_hidden, d_hidden_came, fsdp, slots)
    grads, d_first_low_came, sums, grads_came, kv_came, parts_up, over_down = tie(
        grads, d_first_low_came, sums, grads_came, kv_came, parts_up, over_down
    )
    sent_up = send(parts_up, "gup")
    sums_came = swap_core(sums, "d_low_core")
    grads_came = grads_came + cores(grads[1:], "d_qkv_core")
    grads_came, sums_came = tie(grads_came, sums_came)
    owns_down, (one, two, three) = third_stage(over_down)
    two = shift_slot(two, 2, "gdown3")
    parts_first = grad_rest(
        place,
        (xt, xt_came, frontt, frontt_came, attendedt, attendedt_came),
        grads + grads_came,
        (d_first_low, d_first_low_came, kv, kv_came, sums, sums_came),
        projt,
        entries,
        fsdp,
        slots,
    )
    parts_first, low_rest, sent_up, one, two, three = tie(
        parts_first, low_rest, sent_up, one, two, three
    )
    three = shift_slot(three, 3, "gdown3")
    over_up = forward(*add_up(*sent_up), "gup2")
    act_rest = lift(place, low_rest, up_full, vec, m2, False, range(fsdp // 2))
    parts_first, act_rest, over_up, one, three, grads, low_rest = tie(
        parts_first, act_rest, over_up, one, three, grads, low_rest
    )
    sent_first = send(parts_first, "gfirst")
    last_down = (owns_down, (shift_slot(one, 1, "gdown3"), two, three))
    owns_up, (one, two, three) = third_stage(over_up)
    two, three = shift_slot(two, 2, "gup3"), shift_slot(three, 3, "gup3")
    act_rest += lift(place, low_rest, up_full, vec, m2, False, range(fsdp // 2, fsdp))
    out_rest = lower(act_rest, h_rest, down_full, vec, marks_two)[0]
    output = restore(
        out_front.reshape(seqs, half, width), out_rest.reshape(seqs, half, width), back
    ).reshape(rows, width)
    sent_first, output, grads, one, two, three, last_down = tie(
        sent_first, output, grads, one, two, three, last_down
    )
    over_first = forward(*add_up(*sent_first), "gfirst2")
    last_up = (owns_up, (shift_slot(one, 1, "gup3"), two, three))
    g_down, squares_down = last_stage(*last_down)
    over_first, squares_down, last_up, grads = tie(over_first, squares_down, last_up, grads)
    last_first = along_z((over_first,), "gfirst3")
    g_up, squares_up = last_stage(*last_up)
    grad_input = input_back(
        projt, d_first.reshape(seqs, half, width), qkv_full, back, grads
    ).reshape(rows, width)
    last_first, grad_input, squares_up = tie(last_first, grad_input, squares_up)
    g_first, squares_first = last_stage(*last_first)
    squares_rest = squares_up + squares_down
    squares = sum_everywhere(squares_first + squares_rest)
    states = (
        qkv_weight,
        qkv_moment,
        qkv_second,
        out_weight,
        out_moment,
        out_second,
        up_weight,
        up_moment,
        up_second,
        down_projection_weight.T,
        down_moment.T,
        down_second.T,
        proj_weight,
        proj_moment,
        proj_second,
        vec_weight,
        vec_moment,
        vec_second,
    )
    new = update(place, squares, g_first, g_up, g_down, states, rates)
    norm, new = new[0].reshape(()), list(new[1:])
    new[12:16] = [v.T for v in new[12:16]]
    return (output, grad_input, norm, *new)


def split_up(value, dim, peers):
    dims = value.shape
    blocks = value.reshape(*dims[:dim], peers, dims[dim] // peers, *dims[dim + 1 :])
    return jnp.moveaxis(blocks, dim, 0)


def sum_at_owner(value, axis, dim):
    blocks = split_up(value, dim, lax.axis_size(axis))
    arrived = lax.all_to_all(blocks, axis, split_axis=0, concat_axis=0, tiled=True)
    return arrived.astype(jnp.float32).sum(axis=0)


def side_by_side(arrays, axis, dim, along):
    ends, at = ([], 0)
    for a in arrays[:-1]:
        at += a.shape[along]
        ends.append(at)
    both = jnp.concatenate(arrays, axis=along)
    return tuple(jnp.split(sum_at_owner(both, axis, dim), ends, axis=along))


def layer_norm(summed, gains, shifts):
    average = jnp.mean(summed, axis=-1, keepdims=True)
    centered = summed - average
    variance = jnp.mean(centered * centered, axis=-1, keepdims=True)
    return centered * lax.rsqrt(variance + NORM_EPS) * gains + shifts


def norm_back(summed, gains, shifts, grad_out):
    result, pullback = jax.vjp(layer_norm, summed, gains, shifts)
    return pullback(grad_out)


def gelu_exact(values):
    return jax.nn.gelu(values, approximate=False)


def split_vector(vec_full, model_width, hidden_width):
    mark_one = 3 * model_width
    mark_two = mark_one + model_width
    mark_three = mark_two + hidden_width
    mark_four = mark_three + model_width
    return (
        vec_full[:mark_one],
        vec_full[mark_one:mark_two],
        vec_full[mark_two:mark_three],
        vec_full[mark_three:mark_four],
        vec_full[mark_four : mark_four + model_width],
        vec_full[mark_four + model_width : mark_four + 2 * model_width],
        vec_full[mark_four + 2 * model_width : mark_four + 3 * model_width],
        vec_full[mark_four + 3 * model_width : mark_four + 4 * model_width],
    )


def adam_update(weight, moment, second, grad, scale_clip, rate, decay):
    clipped = grad * scale_clip
    new_moment = BETA_ONE * moment + (1.0 - BETA_ONE) * clipped
    new_second = BETA_TWO * second + (1.0 - BETA_TWO) * clipped * clipped
    moment_hat = new_moment / (1.0 - BETA_ONE**STEP)
    second_hat = new_second / (1.0 - BETA_TWO**STEP)
    new_weight = weight - rate * (moment_hat / (jnp.sqrt(second_hat) + ADAM_EPS) + decay * weight)
    return (new_weight, new_moment, new_second, new_weight.astype(jnp.bfloat16))


def fetch_whole(low_qkv, low_out, low_up, low_down, low_proj, low_vec):
    rows = (
        lax.all_gather(low_qkv, "dp", axis=0, tiled=True),
        lax.all_gather(low_out, "dp", axis=0, tiled=True),
        lax.all_gather(low_up, "dp", axis=0, tiled=True),
        lax.all_gather(low_down, "dp", axis=0, tiled=True),
        lax.all_gather(low_proj, "dp", axis=1, tiled=True),
        lax.all_gather(low_vec, "dp", axis=0, tiled=True),
    )
    return (
        lax.all_gather(rows[0], "fsdp", axis=1, tiled=True),
        lax.all_gather(rows[1], "fsdp", axis=1, tiled=True),
        lax.all_gather(rows[2], "fsdp", axis=1, tiled=True),
        lax.all_gather(rows[3], "fsdp", axis=1, tiled=True),
        lax.all_gather(rows[4], "fsdp", axis=0, tiled=True),
        lax.all_gather(rows[5], "fsdp", axis=0, tiled=True),
    )


def on_any_mesh(
    tokens,
    cotangent,
    positions,
    counts,
    qkv_weight,
    qkv_moment,
    qkv_second,
    out_weight,
    out_moment,
    out_second,
    up_weight,
    up_moment,
    up_second,
    down_projection_weight,
    down_moment,
    down_second,
    proj_weight,
    proj_moment,
    proj_second,
    vec_weight,
    vec_moment,
    vec_second,
):
    low_qkv = qkv_weight.astype(jnp.bfloat16)
    low_out = out_weight.astype(jnp.bfloat16)
    low_up = up_weight.astype(jnp.bfloat16)
    low_down = down_projection_weight.astype(jnp.bfloat16)
    low_proj = proj_weight.astype(jnp.bfloat16)
    low_vec = vec_weight.astype(jnp.bfloat16)
    qkv_full, out_full, up_full, down_full, projection_gathered, vec_full = fetch_whole(
        low_qkv, low_out, low_up, low_down, low_proj, low_vec
    )
    seq_count = counts.shape[0]
    row_count = tokens.shape[0]
    seq_length = row_count // seq_count
    model_width = tokens.shape[1]
    head_width = model_width // HEADS
    hidden_width = vec_full.shape[0] - 9 * model_width
    proj_rows = projection_gathered.shape[0]
    score_scale = head_width ** (-0.5)
    bias_qkv, bias_out, bias_up, bias_down, gain_one, shift_one, gain_two, shift_two = split_vector(
        vec_full.astype(jnp.float32), model_width, hidden_width
    )
    pre_qkv = jnp.dot(tokens, qkv_full, preferred_element_type=jnp.float32)
    qkv_low = (pre_qkv + bias_qkv).astype(jnp.bfloat16)
    queries = qkv_low[:, :model_width].reshape(seq_count, seq_length, HEADS, head_width)
    key_value_pair = qkv_low[:, model_width:].reshape(seq_count, seq_length, 2 * model_width)
    projected = jnp.einsum(
        "bu,vur->vbr", projection_gathered, key_value_pair, preferred_element_type=jnp.float32
    ).astype(jnp.bfloat16)
    key_heads = projected[:, :, :model_width].reshape(seq_count, proj_rows, HEADS, head_width)
    value_heads = projected[:, :, model_width:].reshape(seq_count, proj_rows, HEADS, head_width)
    scores = (
        jnp.einsum("slhe,sjhe->shlj", queries, key_heads, preferred_element_type=jnp.float32)
        * score_scale
    )
    peak = jnp.max(scores, axis=-1, keepdims=True)
    log_total = peak + jnp.log(jnp.sum(jnp.exp(scores - peak), axis=-1, keepdims=True))
    soft_low = jnp.exp(scores - log_total).astype(jnp.bfloat16)
    context = jnp.einsum(
        "shlj,sjhe->slhe", soft_low, value_heads, preferred_element_type=jnp.float32
    )
    attended = context.reshape(row_count, model_width).astype(jnp.bfloat16)
    first_sum = (
        tokens.astype(jnp.float32)
        + jnp.dot(attended, out_full, preferred_element_type=jnp.float32)
        + bias_out
    )
    normed_one = layer_norm(first_sum, gain_one, shift_one)
    normed_low = normed_one.astype(jnp.bfloat16)
    hidden_pre = jnp.dot(normed_low, up_full, preferred_element_type=jnp.float32) + bias_up
    active = gelu_exact(hidden_pre).astype(jnp.bfloat16)
    second_sum = (
        normed_one + jnp.dot(active, down_full, preferred_element_type=jnp.float32) + bias_down
    )
    output = layer_norm(second_sum, gain_two, shift_two).astype(jnp.bfloat16)
    slot_live = jnp.arange(positions.shape[1], dtype=jnp.int32)[None, :] < counts[:, None]
    one_hot_rows = (
        (positions[:, :, None] == jnp.arange(seq_length, dtype=jnp.int32)[None, None, :])
        & slot_live[:, :, None]
    ).astype(jnp.bfloat16)
    dense = jnp.einsum(
        "bej,bef->bjf", one_hot_rows, cotangent, preferred_element_type=jnp.float32
    ).reshape(row_count, model_width)
    qkv_full, out_full, up_full, down_full, projection_gathered, vec_full = fetch_whole(
        low_qkv, low_out, low_up, low_down, low_proj, low_vec
    )
    d_second, d_gain_two, d_shift_two = norm_back(second_sum, gain_two, shift_two, dense)
    d_bias_down = jnp.sum(d_second, axis=0)
    d_second_low = d_second.astype(jnp.bfloat16)
    grad_down = jnp.einsum("rf,rd->fd", active, d_second_low, preferred_element_type=jnp.float32)
    d_active = jnp.einsum("rd,fd->rf", d_second_low, down_full, preferred_element_type=jnp.float32)
    gelu_value, gelu_pull = jax.vjp(gelu_exact, hidden_pre)
    d_hidden = gelu_pull(d_active)[0]
    d_bias_up = jnp.sum(d_hidden, axis=0)
    d_hidden_low = d_hidden.astype(jnp.bfloat16)
    grad_up = jnp.einsum("rd,rf->df", normed_low, d_hidden_low, preferred_element_type=jnp.float32)
    d_normed = d_second + jnp.einsum(
        "rf,df->rd", d_hidden_low, up_full, preferred_element_type=jnp.float32
    )
    d_first, d_gain_one, d_shift_one = norm_back(first_sum, gain_one, shift_one, d_normed)
    d_bias_out = jnp.sum(d_first, axis=0)
    d_first_low = d_first.astype(jnp.bfloat16)
    grad_out = jnp.einsum("rd,re->de", attended, d_first_low, preferred_element_type=jnp.float32)
    d_attended = jnp.einsum("re,de->rd", d_first_low, out_full, preferred_element_type=jnp.float32)
    d_attended = d_attended.astype(jnp.bfloat16).reshape(seq_count, seq_length, HEADS, head_width)
    scores_again = (
        jnp.einsum("slhe,sjhe->shlj", queries, key_heads, preferred_element_type=jnp.float32)
        * score_scale
    )
    probs_again = jnp.exp(scores_again - log_total)
    probs_low = probs_again.astype(jnp.bfloat16)
    d_value_heads = jnp.einsum(
        "shlj,slhe->sjhe", probs_low, d_attended, preferred_element_type=jnp.float32
    )
    d_probs = jnp.einsum(
        "slhe,sjhe->shlj", d_attended, value_heads, preferred_element_type=jnp.float32
    )
    d_scores = probs_again * (d_probs - jnp.sum(probs_again * d_probs, axis=-1, keepdims=True))
    d_raw_low = (d_scores * score_scale).astype(jnp.bfloat16)
    d_queries = jnp.einsum(
        "shlj,sjhe->slhe", d_raw_low, key_heads, preferred_element_type=jnp.float32
    ).reshape(row_count, model_width)
    d_key_heads = jnp.einsum(
        "shlj,slhe->sjhe", d_raw_low, queries, preferred_element_type=jnp.float32
    )
    projected_gradient = jnp.concatenate(
        [
            d_key_heads.reshape(seq_count, proj_rows, model_width),
            d_value_heads.reshape(seq_count, proj_rows, model_width),
        ],
        axis=-1,
    ).astype(jnp.bfloat16)
    d_kv = jnp.einsum(
        "cq,uct->uqt", projection_gathered, projected_gradient, preferred_element_type=jnp.float32
    ).reshape(row_count, 2 * model_width)
    projection_gradient = jnp.einsum(
        "nhy,nxy->hx", projected_gradient, key_value_pair, preferred_element_type=jnp.float32
    )
    d_qkv = jnp.concatenate([d_queries, d_kv], axis=-1)
    d_bias_qkv = jnp.sum(d_qkv, axis=0)
    d_qkv_low = d_qkv.astype(jnp.bfloat16)
    grad_qkv = jnp.einsum("rd,re->de", tokens, d_qkv_low, preferred_element_type=jnp.float32)
    grad_input = (
        d_first + jnp.einsum("re,de->rd", d_qkv_low, qkv_full, preferred_element_type=jnp.float32)
    ).astype(jnp.bfloat16)
    grad_vec = jnp.concatenate(
        [
            d_bias_qkv,
            d_bias_out,
            d_bias_up,
            d_bias_down,
            d_gain_one,
            d_shift_one,
            d_gain_two,
            d_shift_two,
        ]
    )
    col_part = (
        lax.psum_scatter(
            grad_qkv.astype(jnp.bfloat16), "fsdp", scatter_dimension=1, tiled=True
        ).astype(jnp.float32),
        lax.psum_scatter(
            grad_out.astype(jnp.bfloat16), "fsdp", scatter_dimension=1, tiled=True
        ).astype(jnp.float32),
        lax.psum_scatter(
            grad_up.astype(jnp.bfloat16), "fsdp", scatter_dimension=1, tiled=True
        ).astype(jnp.float32),
        lax.psum_scatter(
            grad_down.astype(jnp.bfloat16), "fsdp", scatter_dimension=1, tiled=True
        ).astype(jnp.float32),
        lax.psum_scatter(
            projection_gradient.astype(jnp.bfloat16), "fsdp", scatter_dimension=0, tiled=True
        ).astype(jnp.float32),
        lax.psum_scatter(
            grad_vec.astype(jnp.bfloat16), "fsdp", scatter_dimension=0, tiled=True
        ).astype(jnp.float32),
    )
    owned = (
        *side_by_side(
            (
                col_part[0].astype(jnp.bfloat16),
                col_part[1].astype(jnp.bfloat16),
                col_part[2].astype(jnp.bfloat16),
            ),
            "dp",
            0,
            1,
        ),
        sum_at_owner(col_part[3].astype(jnp.bfloat16), "dp", 0),
        sum_at_owner(col_part[4].astype(jnp.bfloat16), "dp", 1),
        sum_at_owner(col_part[5].astype(jnp.bfloat16), "dp", 0),
    )
    owned_qkv, owned_out, owned_up, owned_down, owned_proj, owned_vec = owned
    local_squares = (
        jnp.sum(owned_qkv * owned_qkv)
        + jnp.sum(owned_out * owned_out)
        + jnp.sum(owned_up * owned_up)
        + jnp.sum(owned_down * owned_down)
        + jnp.sum(owned_proj * owned_proj)
        + jnp.sum(owned_vec * owned_vec)
    )
    all_squares = lax.psum(local_squares, ("fsdp", "dp"))
    grad_norm = jnp.sqrt(all_squares)
    scale_clip = jnp.minimum(1.0, CLIP_NORM / grad_norm)
    qkv_parts = adam_update(
        qkv_weight, qkv_moment, qkv_second, owned_qkv, scale_clip, RATE_QKV, DECAY_RATE
    )
    out_parts = adam_update(
        out_weight, out_moment, out_second, owned_out, scale_clip, RATE_OUT, DECAY_RATE
    )
    up_parts = adam_update(
        up_weight, up_moment, up_second, owned_up, scale_clip, RATE_UP, DECAY_RATE
    )
    down_parts = adam_update(
        down_projection_weight,
        down_moment,
        down_second,
        owned_down,
        scale_clip,
        RATE_DOWN,
        DECAY_RATE,
    )
    proj_parts = adam_update(
        proj_weight, proj_moment, proj_second, owned_proj, scale_clip, RATE_PROJ, DECAY_RATE
    )
    vec_parts = adam_update(
        vec_weight, vec_moment, vec_second, owned_vec, scale_clip, RATE_VEC, 0.0
    )
    return (
        output,
        grad_input,
        grad_norm,
        qkv_parts[0],
        qkv_parts[1],
        qkv_parts[2],
        qkv_parts[3],
        out_parts[0],
        out_parts[1],
        out_parts[2],
        out_parts[3],
        up_parts[0],
        up_parts[1],
        up_parts[2],
        up_parts[3],
        down_parts[0],
        down_parts[1],
        down_parts[2],
        down_parts[3],
        proj_parts[0],
        proj_parts[1],
        proj_parts[2],
        proj_parts[3],
        vec_parts[0],
        vec_parts[1],
        vec_parts[2],
        vec_parts[3],
    )


def solution(mesh):
    matrix = P("dp", "fsdp")
    tall = P("fsdp", "dp")
    every = P(("fsdp", "dp"))
    small = mesh.shape["fsdp"] == 4 and mesh.shape["dp"] == 8
    return jax.shard_map(
        on_device if small else on_any_mesh,
        mesh=mesh,
        in_specs=(every,) * 4 + (matrix,) * 12 + (tall,) * 3 + (every,) * 3,
        out_specs=(every, every, P()) + (matrix,) * 16 + (tall,) * 4 + (every,) * 4,
        check_vma=False,
    )
```

```python
import functools
import math

import jax
import jax.numpy as jnp
from jax import lax
from jax.experimental import pallas as pl
from jax.experimental.pallas import tpu as pltpu
from jax.sharding import PartitionSpec as P

HEADS = 12
STEP = 10
NORM_EPS = 1e-05
CLIP_NORM = 1.0
BETA_ONE = 0.9
BETA_TWO = 0.999
ADAM_EPS = 1e-08
DECAY_RATE = 0.01
RATE_QKV = 0.05
RATE_OUT = 0.4
RATE_UP = 0.05
RATE_DOWN = 0.05
RATE_PROJ = 0.05
RATE_VEC = 1.0

BF = jnp.bfloat16
F32 = jnp.float32
LOG2E = math.log2(math.e)
MIB = 1 << 20


def nn(a, b):
    return jnp.dot(a, b, preferred_element_type=F32)


def nt(a, b):
    return lax.dot_general(a, b, (((1,), (1,)), ((), ())), preferred_element_type=F32)


def sds(shape, dtype):
    return jax.ShapeDtypeStruct(tuple(shape), dtype)


def call(
    kernel, name, out_shape, args, scratch=(), place=None, flops=0, vmem=8, space=pltpu.VMEM
):
    many = isinstance(out_shape, (list, tuple))
    outs = list(out_shape) if many else [out_shape]
    specs = [pl.BlockSpec(memory_space=space)] * len(args)
    if place is not None:
        args = (place, *args)
        specs = [pl.BlockSpec(memory_space=pltpu.SMEM), *specs]
    moved = sum(math.prod(a.shape) * jnp.dtype(a.dtype).itemsize for a in (*args, *outs))
    result = pl.pallas_call(
        kernel,
        name=name,
        out_shape=outs,
        in_specs=specs,
        out_specs=[pl.BlockSpec(memory_space=pltpu.VMEM)] * len(outs),
        scratch_shapes=list(scratch),
        cost_estimate=pl.CostEstimate(
            flops=int(flops) // 1000, bytes_accessed=int(moved) // 1000, transcendentals=0
        ),
        compiler_params=pltpu.CompilerParams(vmem_limit_bytes=vmem * MIB),
    )(*args)
    return result if many else result[0]


def lanes(start, size):
    return pl.ds(pl.multiple_of(start, 128), size)


def lines(start, size):
    return pl.ds(pl.multiple_of(start, 16), size)


def norm_stats(summed):
    average = jnp.mean(summed, axis=-1, keepdims=True)
    centered = summed - average
    variance = jnp.mean(centered * centered, axis=-1, keepdims=True)
    inverse = lax.rsqrt(variance + NORM_EPS)
    return centered * inverse, inverse


def norm_grad(shaped, inverse, gains, grad):
    inner = grad * gains
    first = jnp.mean(inner, axis=-1, keepdims=True)
    second = jnp.mean(inner * shaped, axis=-1, keepdims=True)
    return inverse * (inner - first - shaped * second)


SHARE = (
    1.8312406690584326e-09,
    -1.3438994500794415e-07,
    3.981248882617272e-06,
    -5.530906739278176e-05,
    -3.29139111098754e-05,
    0.03633373340914607,
    0.7978847692370962,
)


def normal_share(u, square):
    x = jnp.minimum(square, 36.0)
    p = x * SHARE[0] + SHARE[1]
    for c in SHARE[2:]:
        p = p * x + c
    return jnp.tanh(p * u) * 0.5 + 0.5


def lanes_below(width):
    return lax.broadcasted_iota(jnp.int32, (1, 2 * width), 1) < width


def swap_halves(value):
    width = value.shape[1] // 2
    return jnp.concatenate([value[:, width:], value[:, :width]], axis=1)


def pack_kernel(place, *refs):
    given, (own, a_ref, b_ref, c_ref), (small, sems), held = (
        refs[:6],
        refs[6:10],
        refs[10:12],
        refs[12:],
    )
    copies = [pltpu.make_async_copy(a, b, sems.at[i]) for i, (a, b) in enumerate(zip(given, held))]
    for copy in copies:
        copy.start()
    for copy in copies:
        copy.wait()
    qkv, out, up, down, proj, vec = held
    vec = vec[...].reshape(1, vec.shape[0])
    odd = (place[0] & 1) == 1
    rows, wide = up.shape
    tile = 128
    half = tile // 2
    full = qkv.shape[1] - half
    after = full + tile
    q, o = qkv[...], out[...]

    def pick(one, two):
        return jnp.where(odd, one, two).astype(BF)

    a_ref[:rows, :full] = pick(q[:, half:], q[:, :full])
    a_ref[:rows, full : full + half] = pick(o[:, :half], q[:, full:])
    a_ref[:rows, full + half : after] = pick(q[:, :half], o[:, tile:])
    a_ref[:rows, after:] = pick(o[:, half:], o[:, :tile])
    small[...] = jnp.zeros_like(small)
    height, width = proj.shape
    for g in range(height // 8):
        small[0:8, g * width : (g + 1) * width] = proj[8 * g : 8 * g + 8, :]
    start = (height // 8) * width
    room = wide - start
    small[0:1, start:] = vec[:, :room]
    left = vec.shape[1] - room
    small[1:2, start : start + left] = vec[:, room:]
    a_ref[rows:, :] = small[...].astype(BF)
    b_ref[...] = up[...].astype(BF)
    across = down.shape[1]
    for h in range(down.shape[0] // rows):
        c_ref[:, h * across : (h + 1) * across] = down[rows * h : rows * (h + 1), :].astype(BF)
    tall = a_ref.shape[0]
    own[:tall, :] = a_ref[...]
    own[tall : tall + rows, :] = b_ref[...]
    own[tall + rows :, :] = c_ref[...]


def pack(place, *given):
    rows, wide = given[2].shape
    tall = rows + 16
    return call(
        pack_kernel,
        "pack_weights",
        [
            sds((tall + 2 * rows, wide), BF),
            sds((tall, wide), BF),
            sds((rows, wide), BF),
            sds((rows, wide), BF),
        ],
        given,
        scratch=[
            pltpu.VMEM((16, wide), F32),
            pltpu.SemaphoreType.DMA((len(given),)),
            *(pltpu.VMEM(a.shape, F32) for a in given),
        ],
        place=place,
        space=pltpu.HBM,
        vmem=60,
    )


def split_cores(place, value, rows, mine, theirs, cols):
    first = place[2] == 0
    for z in range(value.shape[0] // (2 * rows)):
        one = value[2 * z * rows : (2 * z + 1) * rows]
        two = value[(2 * z + 1) * rows : (2 * z + 2) * rows]
        mine[z * rows : (z + 1) * rows, cols] = jnp.where(first, one, two)
        theirs[z * rows : (z + 1) * rows, cols] = jnp.where(first, two, one)


def order_kernel(
    marked, rows, place, pos, x, front, rest, frontt, frontt_other, xt, xt_other, back
):
    seqs, length, _ = x.shape
    half = front.shape[1]
    col = lax.broadcasted_iota(jnp.int32, (half, length), 1)
    row = lax.broadcasted_iota(jnp.int32, (half, length), 0)
    before = (
        lax.broadcasted_iota(jnp.int32, (length, length), 0)
        < lax.broadcasted_iota(jnp.int32, (length, length), 1)
    ).astype(BF)
    for s in range(seqs):
        hot = (pos[s] == col) & (row < marked)
        free = 1.0 - jnp.sum(hot.astype(F32), axis=0, keepdims=True)
        rank = nn(jnp.broadcast_to(free, (16, length)).astype(BF), before)[0:1, :]
        target = jnp.where(free > 0.5, rank.astype(jnp.int32) + marked, -1)
        one = jnp.where(hot | (target == row), 1.0, 0.0)
        two = jnp.where(target == (row + half), 1.0, 0.0)
        values = x[s]
        head = nn(one.astype(BF), values)
        front[s] = head.astype(BF)
        rest[s] = nn(two.astype(BF), values).astype(BF)
        at = slice(s * half, (s + 1) * half)
        split_cores(place, head.T.astype(BF), rows, frontt, frontt_other, at)
        at = slice(s * length, (s + 1) * length)
        split_cores(place, values.T, rows, xt, xt_other, at)
        back[s, :, :half] = one.T.astype(BF)
        back[s, :, half:] = two.T.astype(BF)


def order_rows(place, tokens, positions, slots):
    seqs, length, width = tokens.shape
    marked = positions.shape[1]
    half = length // 2
    pos = jnp.pad(positions, ((0, 0), (0, half - marked)), constant_values=-1)[:, :, None]
    rows = sds((seqs, half, width), BF)
    front = sds((width // 2, seqs * half), BF)
    every = sds((width // 2, seqs * length), BF)
    return call(
        functools.partial(order_kernel, marked, width // (2 * slots)),
        "order_rows",
        [rows, rows, front, front, every, every, sds((seqs, length, length), BF)],
        (pos, tokens),
        place=place,
        flops=2 * seqs * length * length * width,
    )


def qkv_kernel(front, rest, x, weight, vec, proj, q_front, q_rest, kv, kvp):
    seqs, half, width = front.shape
    length = x.shape[1]
    piece = width // 2
    for j in range(4):
        cols = slice(j * piece, (j + 1) * piece)
        at = slice(width + j * piece, width + (j + 1) * piece)
        part = nn(x[...].reshape(seqs * length, width), weight[:, at]) + vec[:, at]
        part = part.astype(BF).reshape(seqs, length, piece)
        kv[:, :, cols] = part
        for s in range(seqs):
            kvp[s, :, cols] = nn(proj[...], part[s]).astype(BF)
    for j in range(2):
        cols = slice(j * piece, (j + 1) * piece)
        for given, result in ((front, q_front), (rest, q_rest)):
            part = nn(given[...].reshape(seqs * half, width), weight[:, cols]) + vec[:, cols]
            result[:, :, cols] = part.astype(BF).reshape(seqs, half, piece)


def make_qkv(front, rest, x, weight, vec, proj):
    seqs, half, width = front.shape
    length = x.shape[1]
    rows = proj.shape[0]
    return call(
        qkv_kernel,
        "make_qkv",
        [
            sds(front.shape, BF),
            sds(front.shape, BF),
            sds((seqs, length, 2 * width), BF),
            sds((seqs, rows, 2 * width), BF),
        ],
        (front, rest, x, weight, vec, proj),
        flops=2 * seqs * length * width * width * 3 + 2 * seqs * rows * length * 2 * width,
    )


def pair_of_heads(head, value):
    below = lanes_below(head)
    zero = jnp.zeros_like(value)
    return jnp.concatenate([jnp.where(below, value, zero), jnp.where(below, zero, value)], axis=0)


def attend_kernel(head, q_front, q_rest, kvp, o_front, o_rest):
    seqs, half, width = q_front.shape
    count = kvp.shape[1]
    below = lanes_below(head)
    factor = LOG2E / math.sqrt(head)
    for first in range(0, width, 2 * head):
        at = slice(first, first + 2 * head)
        for s in range(seqs):
            q = jnp.concatenate([q_front[s, :, at], q_rest[s, :, at]], axis=0)
            scores = nt(q, pair_of_heads(head, kvp[s, :, at]))
            weights, scales = [], []
            for h in range(2):
                part = scores[:, h * count : (h + 1) * count]
                e = jnp.exp2((part - jnp.max(part, axis=-1, keepdims=True)) * factor)
                scales.append(1.0 / jnp.sum(e, axis=-1, keepdims=True))
                weights.append(e.astype(BF))
            values = pair_of_heads(head, kvp[s, :, width + first : width + first + 2 * head])
            total = nn(jnp.concatenate(weights, axis=1), values)
            total = (total * jnp.where(below, scales[0], scales[1])).astype(BF)
            o_front[s, :, at] = total[:half]
            o_rest[s, :, at] = total[half:]


def attend(q_front, q_rest, kvp):
    seqs, half, width = q_front.shape
    rows = kvp.shape[1]
    head = width // HEADS
    return call(
        functools.partial(attend_kernel, head),
        "attend",
        [sds(q_front.shape, BF)] * 2,
        (q_front, q_rest, kvp),
        flops=2 * seqs * HEADS * 2 * half * rows * 2 * head * 2,
    )


def join_kernel(marks, keep, rows, place, attended, x, weight, vec, normed, low, *more):
    bias, gain, shift = (vec[:, a:b] for a, b in marks)
    step = 256
    for r in range(0, x.shape[0], step):
        at = slice(r, r + step)
        part = attended[at, :]
        summed = x[at, :].astype(F32) + nn(part, weight[...]) + bias
        shaped, _ = norm_stats(summed)
        result = shaped * gain + shift
        normed[at, :] = result
        low[at, :] = result.astype(BF)
        if keep:
            kept, lowt, lowt_other, attendedt, attendedt_other = more
            kept[at, :] = summed
            split_cores(place, result.T.astype(BF), rows, lowt, lowt_other, at)
            split_cores(place, part.T, rows, attendedt, attendedt_other, at)


def join(place, attended, x, weight, vec, marks, keep, slots):
    rows, width = x.shape
    outs = [sds((rows, width), F32), sds((rows, width), BF)]
    if keep:
        outs += [sds((rows, width), F32)] + [sds((width // 2, rows), BF)] * 4
    return call(
        functools.partial(join_kernel, marks, keep, width // (2 * slots)),
        "join_front" if keep else "join_rest",
        outs,
        (attended, x, weight, vec),
        place=place,
        flops=2 * rows * width * width,
    )


def lift_kernel(mark, keep, chosen, place, low, weight, vec, active, *more):
    rows = low.shape[0]
    piece = weight.shape[2]
    step = 128
    for n, f in enumerate(chosen):
        cols = slice(n * piece, (n + 1) * piece)
        bias = vec[:, mark + f * piece : mark + (f + 1) * piece]
        for r in range(0, rows, step):
            at = slice(r, r + step)
            u = nn(low[at, :], weight[f]) + bias
            square = u * u
            share = normal_share(u, square)
            a = (u * share).astype(BF)
            active[at, cols] = a
            if keep:
                slope, give = more
                bell = jnp.exp2(square * (-0.5 * LOG2E) - 0.5 * math.log2(2.0 * math.pi))
                slope[at, cols] = (share + u * bell).astype(BF)
                half = piece // 2
                give[at, n * half : (n + 1) * half] = jnp.where(
                    place[2] == 0, a[:, half:], a[:, :half]
                )


def lift(place, low, weight, vec, mark, keep, chosen):
    rows, width = low.shape
    piece = weight.shape[2]
    wide = len(chosen) * piece
    outs = [sds((rows, wide), BF)]
    if keep:
        outs += [sds((rows, wide), BF), sds((rows, wide // 2), BF)]
    return call(
        functools.partial(lift_kernel, mark, keep, tuple(chosen)),
        "lift_front" if keep else "lift_rest",
        outs,
        (low, weight, vec),
        place=place,
        flops=2 * rows * width * wide,
    )


def lower_kernel(marks, count, *refs):
    actives, (normed, weight, vec), refs = refs[:count], refs[count : count + 3], refs[count + 3 :]
    bias, gain, shift = (vec[:, a:b] for a, b in marks)
    half = normed.shape[0] // 2
    totals = []
    for r in (0, half):
        total = normed[r : r + half, :] + bias
        first = 0
        for active in actives:
            last = first + active.shape[1]
            total = total + nt(active[r : r + half, :], weight[:, first:last])
            first = last
        totals.append(total)
    step = 128
    for r in range(0, normed.shape[0], step):
        at = slice(r, r + step)
        summed = totals[r // half][r % half : r % half + step, :]
        shaped, inverse = norm_stats(summed)
        if len(refs) == 1:
            refs[0][at, :] = (shaped * gain + shift).astype(BF)
            continue
        dy, output, d_sum, d_low, d_lowt, sums = refs
        output[at, :] = (shaped * gain + shift).astype(BF)
        grad = dy[at, :].astype(F32)
        back = norm_grad(shaped, inverse, gain, grad)
        d_sum[at, :] = back
        d_low[at, :] = back.astype(BF)
        d_lowt[:, at] = back.T.astype(BF)
        new = [jnp.sum(v, axis=0, keepdims=True) for v in (grad * shaped, grad, back)]
        for i, v in enumerate(new):
            sums[i : i + 1, :] = v if r == 0 else sums[i : i + 1, :] + v


def lower(actives, normed, weight, vec, marks, dy=None):
    rows, width = normed.shape
    full = (rows, width)
    if dy is None:
        outs, more = [sds(full, BF)], ()
    else:
        outs = [
            sds(full, BF),
            sds(full, F32),
            sds(full, BF),
            sds((width, rows), BF),
            sds((8, width), F32),
        ]
        more = (dy,)
    return call(
        functools.partial(lower_kernel, marks, len(actives)),
        "lower_rest" if dy is None else "lower_front",
        outs,
        (*actives, normed, weight, vec, *more),
        flops=2 * rows * width * weight.shape[1],
    )


def hidden_back_kernel(d_low, weight, slope, d_hidden, sums):
    piece = d_low.shape[1]
    for f in range(weight.shape[1] // piece):
        cols = slice(f * piece, (f + 1) * piece)
        du = nn(d_low[...], weight[:, cols]) * slope[:, cols].astype(F32)
        d_hidden[:, cols] = du.astype(BF)
        sums[:, cols] = jnp.sum(du, axis=0, keepdims=True)


def hidden_back(d_low, weight, slope):
    rows, width = d_low.shape
    hidden = weight.shape[1]
    return call(
        hidden_back_kernel,
        "hidden_back",
        [sds((rows, hidden), BF), sds((1, hidden), F32)],
        (d_low, weight, slope),
        flops=2 * rows * width * hidden,
    )


def first_back_kernel(
    marks, d_hidden, up, d_sum, kept, vec, weight, up_sums, two_sums, *refs
):
    d_first, d_low, d_attended, sums = refs
    gain = vec[:, marks[0] : marks[1]]
    parts, _, piece = up.shape
    total = d_sum[...]
    for f in range(parts):
        total = total + nt(d_hidden[:, f * piece : (f + 1) * piece], up[f])
    step = 128
    for r in range(0, d_sum.shape[0], step):
        at = slice(r, r + step)
        grad = total[at, :]
        shaped, inverse = norm_stats(kept[at, :])
        back = norm_grad(shaped, inverse, gain, grad)
        d_first[at, :] = back
        d_low[at, :] = back.astype(BF)
        new = [jnp.sum(v, axis=0, keepdims=True) for v in (grad * shaped, grad, back)]
        for i, v in enumerate(new):
            sums[i : i + 1, :] = v if r == 0 else sums[i : i + 1, :] + v
    d_attended[...] = nt(d_low[...], weight[...]).astype(BF)
    sums[3:6, :] = two_sums[0:3, :]
    for f in range(parts):
        sums[6 + f : 7 + f, :] = up_sums[:, f * piece : (f + 1) * piece]
    sums[6 + parts :, :] = jnp.zeros((sums.shape[0] - 6 - parts, sums.shape[1]), F32)


def first_back(d_hidden, up, d_sum, kept, vec, weight, up_sums, two_sums, marks):
    rows, width = d_sum.shape
    parts, _, piece = up.shape
    full = (rows, width)
    return call(
        functools.partial(first_back_kernel, marks),
        "first_back",
        [sds(full, F32), sds(full, BF), sds(full, BF), sds((16, width), F32)],
        (d_hidden, up, d_sum, kept, vec, weight, up_sums, two_sums),
        flops=2 * rows * width * (parts * piece + width),
    )


def attend_back_kernel(head, s, queries, kvp, grads, result):
    _, half, width = queries.shape
    count = kvp.shape[1]
    below = lanes_below(head)
    scale = 1.0 / math.sqrt(head)
    for first in range(0, width, 2 * head):
        at = slice(first, first + 2 * head)
        q, k, g = queries[s, :, at], kvp[s, :, at], grads[s, :, at]
        v = kvp[s, :, width + first : width + first + 2 * head]
        scores = nt(pair_of_heads(head, k), q)
        d_probs = nt(pair_of_heads(head, v), g)
        probs, d_scores = [], []
        for h in range(2):
            part = scores[h * count : (h + 1) * count]
            e = jnp.exp2((part - jnp.max(part, axis=0, keepdims=True)) * (LOG2E * scale))
            p = e * (1.0 / jnp.sum(e, axis=0, keepdims=True))
            both = p * d_probs[h * count : (h + 1) * count]
            ds = (both - p * jnp.sum(both, axis=0, keepdims=True)) * scale
            probs.append(p.astype(BF))
            d_scores.append(ds.astype(BF))
        dv = nn(jnp.concatenate(probs, axis=0), g)
        dk = nn(jnp.concatenate(d_scores, axis=0), q)
        kt = k.T
        dq = jnp.concatenate([nn(kt[:head], d_scores[0]), nn(kt[head:], d_scores[1])], axis=0)
        result[:half, at] = dq.T.astype(BF)
        result[half : half + count, at] = jnp.where(below, dk[:count], dk[count:]).astype(BF)
        result[half + count :, at] = jnp.where(below, dv[:count], dv[count:]).astype(BF)


def attend_back(s, queries, kvp, grads):
    _, half, width = queries.shape
    rows = kvp.shape[1]
    head = width // HEADS
    return call(
        functools.partial(attend_back_kernel, head, s),
        "attend_back",
        sds((half + 2 * rows, width), BF),
        (queries, kvp, grads),
        flops=2 * HEADS * half * rows * 2 * head * 5,
    )


def input_back_kernel(projt, d_first, weight, back, *refs):
    grads, result = refs[:-1], refs[-1]
    _, half, width = d_first.shape
    rows = projt.shape[1]
    for s, grad in enumerate(grads):
        front = d_first[s] + nt(grad[:half, :], weight[:, :width])
        high = front.astype(BF)
        low = (front - high.astype(F32)).astype(BF)
        place = back[s, :, :half]
        total = nn(place, high) + nn(place, low)
        for j in (1, 2):
            part = nn(projt[...], grad[half + (j - 1) * rows : half + j * rows, :]).astype(BF)
            total = total + nt(part, weight[:, j * width : (j + 1) * width])
        result[s] = total.astype(BF)


def input_back(projt, d_first, weight, back, grads):
    seqs, half, width = d_first.shape
    length = back.shape[1]
    return call(
        input_back_kernel,
        "input_back",
        sds((seqs, length, width), BF),
        (projt, d_first, weight, back, *grads),
        flops=2 * seqs * length * width * (3 * width + length),
    )


def restore_kernel(front, rest, back, result):
    seqs, half, _ = front.shape
    for s in range(seqs):
        total = nn(back[s, :, :half], front[s]) + nn(back[s, :, half:], rest[s])
        result[s] = total.astype(BF)


def restore(front, rest, back):
    seqs, half, width = front.shape
    length = back.shape[1]
    return call(
        restore_kernel,
        "restore_order",
        sds((seqs, length, width), BF),
        (front, rest, back),
        flops=2 * seqs * length * length * width,
    )


def route(rel, slot, send_x, stay_x, send_y, stay_y):
    if slot < 2:
        return (send_x if rel & 1 else stay_x), rel >> 1, slot
    return (send_y if rel & 2 else stay_y), rel & 1, slot - 2


def grad_up_kernel(place, lowt, lowt_other, d_hidden, d_hidden_other, *refs):
    outs, work = refs[:4], refs[4]
    slots, rows, piece = work.shape
    for rel in range(4):
        cols = lanes((rel ^ place[0]) * piece, piece)
        part = nn(lowt[...], d_hidden[:, cols]) + nn(lowt_other[...], d_hidden_other[:, cols])
        work[...] = part.astype(BF).reshape(work.shape)
        for slot in range(slots):
            ref, i, j = route(rel, slot, *outs)
            ref[i, j] = work[(place[1] + slot) % slots]


def grad_up(place, lowt, lowt_other, d_hidden, d_hidden_other, fsdp, slots):
    width, count = lowt.shape
    rows = width // slots
    piece = d_hidden.shape[1] // fsdp
    return call(
        grad_up_kernel,
        "grad_up",
        [sds((2, 2, rows, piece), BF)] * 4,
        (lowt, lowt_other, d_hidden, d_hidden_other),
        scratch=[pltpu.VMEM((slots, rows, piece), BF)],
        place=place,
        flops=2 * width * 2 * count * piece * fsdp,
    )


def grad_down_kernel(place, d_lowt, d_lowt_other, active, active_other, *refs):
    outs, work = refs[:4], refs[4]
    _, _, rows, wide = outs[0].shape
    piece = work.shape[1]
    for slot in range(4):
        z = (place[1] + slot) % 4
        work[...] = (
            nn(d_lowt[...], active[:, lanes((2 * z + place[2]) * piece, piece)])
            + nn(d_lowt_other[...], active_other[:, lanes(z * piece, piece)])
        ).astype(BF)
        for rel in range(4):
            ref, i, j = route(rel, slot, *outs)
            for h in range(wide // piece):
                top = (rel ^ place[0]) * rows * (wide // piece) + h * rows
                ref[i, j, :, h * piece : (h + 1) * piece] = work[lines(top, rows), :]


def grad_down(place, d_lowt, d_lowt_other, active, active_other, rows, slots):
    width, count = d_lowt.shape
    hidden = active.shape[1]
    piece = hidden // (2 * slots)
    return call(
        grad_down_kernel,
        "grad_down",
        [sds((2, 2, rows, width), BF)] * 4,
        (d_lowt, d_lowt_other, active, active_other),
        scratch=[pltpu.VMEM((width, piece), BF)],
        place=place,
        flops=2 * hidden * 2 * count * width,
    )


def grad_rest_kernel(seqs, place, *refs):
    (xt, xt_o, frontt, frontt_o, attendedt, attendedt_o), refs = refs[:6], refs[6:]
    grads, refs = refs[: 2 * seqs], refs[2 * seqs :]
    (d_low, d_low_o, kv, kv_o, sums, sums_o, projt), refs = refs[:7], refs[7:]
    outs, (work_qkv, work_out, work_kv, vector, smalls, small, d_proj) = refs[:4], refs[4:]
    slots, rows, _ = work_qkv.shape
    _, _, tall, wide = outs[0].shape
    fsdp = smalls.shape[0]
    length, count = projt.shape
    width = d_low.shape[1]
    half = d_low.shape[0] // seqs
    first_sums = [None] * 3
    for n, grad in enumerate(grads):
        values = kv if n < seqs else kv_o
        s = n % seqs
        new = [jnp.sum(grad[:half, :].astype(F32), axis=0, keepdims=True)]
        for j in (0, 1):
            part = nn(projt[...], grad[half + j * count : half + (j + 1) * count, :])
            work_kv[n * length : (n + 1) * length, j * width : (j + 1) * width] = part.astype(BF)
            new.append(jnp.sum(part, axis=0, keepdims=True))
        first_sums = new if n == 0 else [a + b for a, b in zip(first_sums, new)]
        both = nt(grad[half : half + count, :], values[s, :, :width]) + nt(
            grad[half + count :, :], values[s, :, width:]
        )
        d_proj[...] = both if n == 0 else d_proj[...] + both

    def both_cores(a, a_o, b, b_o):
        total = nn(a[...], b) + nn(a_o[...], b_o)
        return total.astype(BF).reshape(slots, rows, total.shape[1])

    q_part = None
    for n, grad in enumerate(grads):
        left = frontt if n < seqs else frontt_o
        s = n % seqs
        part = nn(left[:, s * half : (s + 1) * half], grad[:half, :])
        q_part = part if q_part is None else q_part + part
    work_qkv[:, :, :width] = q_part.astype(BF).reshape(slots, rows, width)
    tokens = seqs * length
    for j in range(2):
        cols = slice(j * width, (j + 1) * width)
        work_qkv[:, :, (j + 1) * width : (j + 2) * width] = both_cores(
            xt, xt_o, work_kv[:tokens, cols], work_kv[tokens:, cols]
        )
    work_out[...] = both_cores(attendedt, attendedt_o, d_low[...], d_low_o[...])
    total = sums[...] + sums_o[...]
    at = 0
    for value in (
        *first_sums,
        total[2:3, :],
        *(total[i : i + 1, :] for i in range(6, 6 + vector.shape[1] // width - 9)),
        total[5:6, :],
        *(total[i : i + 1, :] for i in (0, 1, 3, 4)),
    ):
        vector[:, at : at + width] = value
        at += width
    entries = vector.shape[1] // (2 * fsdp * slots)
    height = count // fsdp
    across = length // (2 * slots)
    start = (height // 8) * across
    room = wide - start
    first = place[2] == 0
    small[...] = jnp.zeros_like(small)
    for f in range(fsdp):
        for z in range(slots):
            for g in range(height // 8):
                part = d_proj[
                    f * height + 8 * g : f * height + 8 * g + 8,
                    2 * z * across : 2 * (z + 1) * across,
                ]
                small[0:8, g * across : (g + 1) * across] = jnp.where(
                    first, part[:, :across], part[:, across:]
                )
            base = (f * 2 * slots + 2 * z) * entries
            own = jnp.where(
                first,
                vector[:, base : base + entries],
                vector[:, base + entries : base + 2 * entries],
            )
            small[0:1, start:] = own[:, :room]
            small[1:2, start : start + entries - room] = own[:, room:]
            smalls[f, z] = small[...].astype(BF)
    below = lanes_below(64)
    for rel in range(fsdp):
        f = rel ^ place[0]
        even = (f & 1) == 0
        for slot in range(slots):
            z = (place[1] + slot) % slots
            ref, i, j = route(rel, slot, *outs)
            put = ref.at[i, j]
            q_first = 9 * (f // 2) + 5 * (f & 1)
            o_pair = 3 * (f // 2)
            put[:rows, :512] = work_qkv[z, :, lanes(q_first * 128, 512)]
            shared = work_qkv[z, :, lanes((9 * (f // 2) + 4) * 128, 128)]
            out_shared = work_out[z, :, lanes((o_pair + 1) * 128, 128)]
            put[:rows, 512:640] = jnp.where(below == even, shared, swap_halves(out_shared))
            put[:rows, 640:] = work_out[z, :, lanes((o_pair + 2 * (f & 1)) * 128, 128)]
            put[rows:, :] = smalls[f, z]


def grad_rest(place, lefts, grads, rights, projt, entries, fsdp, slots):
    width, tokens = 2 * lefts[0].shape[0], lefts[0].shape[1]
    rows = width // (2 * slots)
    wide = 4 * width // fsdp
    return call(
        functools.partial(grad_rest_kernel, len(grads) // 2),
        "grad_rest",
        [sds((2, 2, rows + 16, wide), BF)] * 4,
        (*lefts, *grads, *rights, projt),
        scratch=[
            pltpu.VMEM((slots, rows, 3 * width), BF),
            pltpu.VMEM((slots, rows, width), BF),
            pltpu.VMEM((2 * tokens, 2 * width), BF),
            pltpu.VMEM((1, entries), F32),
            pltpu.VMEM((fsdp, slots, 16, wide), BF),
            pltpu.VMEM((16, wide), F32),
            pltpu.VMEM(projt.shape[::-1], F32),
        ],
        place=place,
        flops=width * width * 8 * tokens,
        vmem=20,
    )


def swap_core(value, name="core"):
    n = lax.axis_size("dp")
    with jax.named_scope(name):
        return lax.ppermute(value, "dp", [(i, i ^ 1) for i in range(n)])


def shift_slot(value, by, name="slot"):
    n = lax.axis_size("dp")
    with jax.named_scope(f"{name}_z{by}"):
        return lax.ppermute(value, "dp", [(i, (i + 2 * by) % n) for i in range(n)])


def swap_fsdp(value, bits, name="fsdp"):
    n = lax.axis_size("fsdp")
    with jax.named_scope(f"{name}_{' xyd'[bits]}"):
        return lax.ppermute(value, "fsdp", [(i, i ^ bits) for i in range(n)])


def tie(*values):
    return lax.optimization_barrier(values)


def segments_of(array, tall, blocks, cut, diagonal, low_at, high_at):
    found = []
    for first, back, rows in blocks:
        found += [(array, n * tall + first, n, back, 0, rows) for n in range(3)]
        low = min(max(cut - first, 0), rows)
        if low:
            found.append((diagonal, low_at + first, 3, back, 0, low))
        if low < rows:
            found.append((diagonal, high_at + first + low - cut, 3, back, low, rows - low))
    return found


def block_parts(segments, place, refs, slots):
    arrays = len(refs) // 2
    for other in (0, 1):
        for n, top, bits, back, line, rows in segments:
            z = (place[1] - back + slots) % slots
            ref = refs[other * arrays + n]
            yield ref, top, place[0] ^ bits, 2 * z + (place[2] ^ other), line, rows


def first_whole_kernel(segments, slots, fsdp, height, across, place, *refs):
    count = len(refs) - 8
    blocks = refs[:count]
    qkv, out, vec, proj, projt, halves, smalls, matrix = refs[count:]
    rows = qkv.shape[0] // (2 * slots)
    wide = smalls.shape[3]
    for ref, top, f, d, line, size in block_parts(segments, place, blocks, slots):
        body = min(line + size, rows) - line
        if body > 0:
            src = slice(top, top + body)
            dst = lines(d * rows + line, body)
            qkv[dst, lanes(128 * (9 * (f // 2) + 5 * (f & 1)), 512)] = ref[src, :512]
            halves[f, dst, :] = ref[src, 512:640]
            out[dst, lanes(128 * (3 * (f // 2) + 2 * (f & 1)), 128)] = ref[src, 640:]
        else:
            body = 0
        if body < size:
            smalls[f, d] = ref[top + body : top + size, :]
    entries = vec.shape[1] // (2 * slots * fsdp)
    start = (height // 8) * across
    room = wide - start
    below = lanes_below(64)
    for f in range(fsdp):
        for d in range(2 * slots):
            small = smalls[f, d].astype(F32)
            for g in range(height // 8):
                matrix[
                    f * height + 8 * g : f * height + 8 * g + 8, d * across : (d + 1) * across
                ] = small[0:8, g * across : (g + 1) * across]
            base = (f * 2 * slots + d) * entries
            vec[:, base : base + room] = small[0:1, start:]
            vec[:, base + room : base + entries] = small[1:2, start : start + entries - room]
    for f in range(0, fsdp, 2):
        one, two = halves[f], halves[f + 1]
        at = 128 * (9 * (f // 2) + 4)
        qkv[:, at : at + 128] = jnp.where(below, one, two)
        at = 128 * (3 * (f // 2) + 1)
        out[:, at : at + 128] = swap_halves(jnp.where(below, two, one))
    proj[...] = matrix[...].astype(BF)
    projt[...] = matrix[...].T.astype(BF)


def first_whole(place, blocks, segments, fsdp, slots, width, proj_shape, entries):
    wide = blocks[0].shape[1]
    height, across = proj_shape[0] // fsdp, proj_shape[1] // (2 * slots)
    return call(
        functools.partial(first_whole_kernel, segments, slots, fsdp, height, across),
        "whole_first",
        [
            sds((width, 3 * width), BF),
            sds((width, width), BF),
            sds((1, entries), F32),
            sds(proj_shape, BF),
            sds(proj_shape[::-1], BF),
        ],
        blocks,
        scratch=[
            pltpu.VMEM((fsdp, width, 128), BF),
            pltpu.VMEM((fsdp, 2 * slots, 16, wide), BF),
            pltpu.VMEM(proj_shape, F32),
        ],
        place=place,
    )


def up_whole_kernel(segments, rows, slots, place, *refs):
    blocks, result = refs[:-1], refs[-1]
    for ref, top, f, d, line, size in block_parts(segments, place, blocks, slots):
        result[f, lines(d * rows + line, size), :] = ref[top : top + size, :]


def up_whole(place, blocks, segments, rows, fsdp, slots):
    wide = blocks[0].shape[1]
    return call(
        functools.partial(up_whole_kernel, segments, rows, slots),
        "whole_up",
        sds((fsdp, 2 * slots * rows, wide), BF),
        blocks,
        place=place,
    )


def down_whole_kernel(segments, rows, slots, place, *refs):
    blocks, result = refs[:-1], refs[-1]
    piece = result.shape[1] // (2 * slots)
    parts = blocks[0].shape[1] // piece
    for ref, top, f, d, line, size in block_parts(segments, place, blocks, slots):
        for h in range(parts):
            dst = lines((f * parts + h) * rows + line, size)
            result[dst, lanes(d * piece, piece)] = ref[
                top : top + size, h * piece : (h + 1) * piece
            ]


def down_whole(place, blocks, segments, rows, slots, hidden, width):
    return call(
        functools.partial(down_whole_kernel, segments, rows, slots),
        "whole_down",
        sds((width, hidden), BF),
        blocks,
        place=place,
    )


def stack_kernel(ranges, *refs):
    at = 0
    for (first, last), ref in zip(ranges, refs[:-1]):
        refs[-1][at : at + last - first, :] = ref[first:last, :]
        at += last - first


def stack(*parts):
    arrays, ranges = [p[0] for p in parts], [p[1:] for p in parts]
    rows = sum(b - a for a, b in ranges)
    return call(
        functools.partial(stack_kernel, ranges),
        "stack",
        sds((rows, arrays[0].shape[1]), BF),
        arrays,
    )


def second_stage_kernel(stay_x, from_x, stay_y, from_y, over_y, over_x, kept):
    for stay, came, over, at in ((stay_x, from_x, over_y, 0), (stay_y, from_y, over_x, 1)):
        over[...] = (stay[1].astype(F32) + came[1].astype(F32)).astype(BF)
        kept[at] = (stay[0].astype(F32) + came[0].astype(F32)).astype(BF)


def second_stage(stay_x, from_x, stay_y, from_y):
    shape = stay_x.shape
    return call(
        second_stage_kernel,
        "second_stage",
        [sds(shape[1:], BF), sds(shape[1:], BF), sds(shape, BF)],
        (stay_x, from_x, stay_y, from_y),
    )


def third_stage_kernel(count, *refs):
    ins, owns, sends = refs[: 3 * count], refs[3 * count : 4 * count], refs[4 * count :]
    at = 0
    for n in range(count):
        kept, over_y, over_x = ins[3 * n : 3 * n + 3]
        rows = kept.shape[2]
        put = slice(at, at + rows)
        at += rows
        owns[n][...] = kept[0, 0].astype(F32) + over_y[0].astype(F32)
        sends[0][put, :] = (kept[0, 1].astype(F32) + over_y[1].astype(F32)).astype(BF)
        sends[1][put, :] = (kept[1, 0].astype(F32) + over_x[0].astype(F32)).astype(BF)
        sends[2][put, :] = (kept[1, 1].astype(F32) + over_x[1].astype(F32)).astype(BF)


def third_stage(*pieces):
    shapes = [p[0].shape[2:] for p in pieces]
    rows = sum(a for a, _ in shapes)
    count = len(pieces)
    got = call(
        functools.partial(third_stage_kernel, count),
        "third_stage",
        [sds(a, F32) for a in shapes] + [sds((rows, shapes[0][1]), BF)] * 3,
        [a for p in pieces for a in p],
    )
    return got[:count], got[count:]


def last_stage_kernel(count, *refs):
    owns, (one, two, three) = refs[:count], refs[count : count + 3]
    results, squares = refs[count + 3 : -1], refs[-1]
    at = 0
    sums = None
    for own, result in zip(owns, results):
        put = slice(at, at + own.shape[0])
        at += own.shape[0]
        total = (own[...] + two[put, :].astype(F32)) + (
            one[put, :].astype(F32) + three[put, :].astype(F32)
        )
        result[...] = total
        part = jnp.sum(total * total, axis=0, keepdims=True)
        sums = part if sums is None else sums + part
    squares[...] = jnp.broadcast_to(jnp.sum(sums), squares.shape)


def last_stage(owns, came):
    return call(
        functools.partial(last_stage_kernel, len(owns)),
        "last_stage",
        [sds(a.shape, F32) for a in owns] + [sds((8, 128), F32)],
        (*owns, *came),
    )


def sum_everywhere(value):
    a, b, c = (shift_slot(value, k, "norm") for k in (1, 2, 3))
    value = (value + b) + (a + c)
    value = value + swap_core(value)
    a, b, c = (swap_fsdp(value, k, "norm") for k in (1, 2, 3))
    return (value + a) + (b + c)


def adam(weight, moment, second, grad, scale_clip, rate, decay):
    clipped = grad * scale_clip
    new_moment = BETA_ONE * moment + (1.0 - BETA_ONE) * clipped
    new_second = BETA_TWO * second + (1.0 - BETA_TWO) * clipped * clipped
    moment_hat = new_moment / (1.0 - BETA_ONE**STEP)
    second_hat = new_second / (1.0 - BETA_TWO**STEP)
    new_weight = weight - rate * (moment_hat / (jnp.sqrt(second_hat) + ADAM_EPS) + decay * weight)
    return new_weight, new_moment, new_second, new_weight.astype(BF)


def update_kernel(rates, place, squares, g_first, g_up, g_down, *refs):
    ins, outs = refs[:18], refs[18:-3]
    norm_ref, outs = outs[0], outs[1:]
    vector, wide_work, thin_work = refs[-3:]
    odd = (place[0] & 1) == 1
    norm = jnp.sqrt(squares[0:1, 0:1])
    norm_ref[...] = norm
    clip = jnp.minimum(1.0, CLIP_NORM / norm)

    def put(n, place, grad):
        new = adam(*(ins[3 * n + i][place] for i in range(3)), grad, clip, *rates[n])
        for i in range(4):
            outs[4 * n + i][place] = new[i]

    rows, wide = g_up.shape
    piece = ins[0].shape[1]
    every = (slice(None), slice(None))
    wide_work[:, :64] = g_first[:rows, 576:640]
    wide_work[:, 64:] = g_first[:rows, :512]
    put(0, every, jnp.where(odd, wide_work[...], g_first[:rows, :piece]))

    def thin(full, first, second):
        thin_work[0, :, :128] = full
        thin_work[0, :, 128:] = second
        thin_work[1, :, :64] = first
        thin_work[1, :, 64:] = full
        return jnp.where(odd, thin_work[1], thin_work[0])

    put(1, every, thin(g_first[:rows, 640:], g_first[:rows, 512:576], g_first[:rows, 576:640]))
    put(2, every, g_up[...])
    across = ins[9].shape[1]
    for h in range(wide // across):
        put(
            3,
            (slice(h * rows, (h + 1) * rows), slice(None)),
            g_down[:, h * across : (h + 1) * across],
        )
    height, across = ins[12].shape
    for g in range(height // 8):
        put(
            4,
            (slice(8 * g, 8 * g + 8), slice(None)),
            g_first[rows : rows + 8, g * across : (g + 1) * across],
        )
    start = (height // 8) * across
    room = wide - start
    entries = ins[15].shape[0]
    vector[:, :room] = g_first[rows : rows + 1, start:]
    vector[:, room:] = g_first[rows + 1 : rows + 2, start : start + entries - room]
    state = (ins[15 + i][...].reshape(1, entries) for i in range(3))
    new = adam(*state, vector[...], clip, *rates[5])
    for i in range(4):
        outs[20 + i][...] = new[i].reshape(entries)


def update(place, squares, g_first, g_up, g_down, states, rates):
    outs = [sds((1, 1), F32)]
    for n in range(6):
        shape = states[3 * n].shape
        outs += [sds(shape, F32)] * 3 + [sds(shape, BF)]
    return call(
        functools.partial(update_kernel, rates),
        "update",
        outs,
        (squares, g_first, g_up, g_down, *states),
        scratch=[
            pltpu.VMEM((1, *states[15].shape), F32),
            pltpu.VMEM(states[0].shape, F32),
            pltpu.VMEM((2, *states[3].shape), F32),
        ],
        place=place,
    )


def on_device(
    tokens,
    cotangent,
    positions,
    counts,
    qkv_weight,
    qkv_moment,
    qkv_second,
    out_weight,
    out_moment,
    out_second,
    up_weight,
    up_moment,
    up_second,
    down_projection_weight,
    down_moment,
    down_second,
    proj_weight,
    proj_moment,
    proj_second,
    vec_weight,
    vec_moment,
    vec_second,
):
    fsdp, slots = lax.axis_size("fsdp"), lax.axis_size("dp") // 2
    place = jnp.stack(
        [lax.axis_index("fsdp"), lax.axis_index("dp") // 2, lax.axis_index("dp") % 2]
    ).astype(jnp.int32)
    seqs = counts.shape[0]
    rows, width = tokens.shape
    length = rows // seqs
    half = length // 2
    marked = positions.shape[1]
    hidden = down_projection_weight.shape[0] * slots * 2
    proj_shape = (proj_weight.shape[0] * fsdp, proj_weight.shape[1] * 2 * slots)
    entries = vec_weight.shape[0] * fsdp * 2 * slots
    rates = (
        (RATE_QKV, DECAY_RATE),
        (RATE_OUT, DECAY_RATE),
        (RATE_UP, DECAY_RATE),
        (RATE_DOWN, DECAY_RATE),
        (RATE_PROJ, DECAY_RATE),
        (RATE_VEC, 0.0),
    )

    own, own_first, own_up, own_down = pack(
        place,
        qkv_weight,
        out_weight,
        up_weight,
        down_projection_weight.T,
        proj_weight,
        vec_weight,
    )
    rows_first, rows_up = own_first.shape[0], own_up.shape[0]

    def across(value, name):
        return swap_fsdp(value, 1, name), swap_fsdp(value, 2, name)

    def cores(arrays, name):
        return [swap_core(a, name) for a in arrays]

    back_first = [shift_slot(own_first, k, "first") for k in (1, 2, 3)]
    own_x, own_y = across(own, "own")
    x = tokens.reshape(seqs, length, width)
    front, rest, frontt, frontt_give, xt, xt_give, back = order_rows(place, x, positions, slots)
    live = jnp.arange(marked, dtype=jnp.int32)[None, :] < counts[:, None]
    dy = jnp.pad(
        jnp.where(live[:, :, None], cotangent, jnp.zeros_like(cotangent)),
        ((0, 0), (0, half - marked), (0, 0)),
    ).reshape(seqs * half, width)
    back_first, own_x, own_y, own_up, own_down, own, frontt_give, xt_give, dy, front = tie(
        back_first, own_x, own_y, own_up, own_down, own, frontt_give, xt_give, dy, front
    )

    def all_of(*arrays):
        return stack(*((a, 0, a.shape[0]) for a in arrays))

    far_first = all_of(*back_first)
    first_x, first_y = across(far_first, "first")
    back_up = [shift_slot(own_up, k, "up") for k in (1, 2, 3)]
    near = all_of(own, own_x, own_y)
    own_x, own_y, far_first, first_x, first_y, own_down, near, back_up = tie(
        own_x, own_y, far_first, first_x, first_y, own_down, near, back_up
    )

    tall, far = own.shape[0], far_first.shape[0]
    half_own = tall // 32 * 16
    half_first = (tall + far) // 32 * 16 - half_own
    low = stack((own_x, 0, half_own), (first_x, 0, half_first))
    high = stack((own_y, half_own, tall), (first_y, half_first, far))
    diagonal = [swap_fsdp(low, 2, "diag"), swap_fsdp(high, 1, "diag")]
    back_down = [shift_slot(own_down, 1, "down"), None, shift_slot(own_down, 3, "down")]
    near_other = swap_core(near, "near_core")
    first = all_of(far_first, first_x, first_y)
    first_other = swap_core(first, "first_core")
    diagonal, first_other, near_other, back_down, own_down = tie(
        diagonal, first_other, near_other, back_down, own_down
    )
    diagonal = all_of(*diagonal)
    diagonal_other = swap_core(diagonal, "diag_core")
    high_at = half_own + half_first

    def near_segments(first, rows):
        return segments_of(0, tall, [(first, 0, rows)], half_own, 1, 0, high_at)

    far_up = all_of(*back_up)
    back_down[1] = shift_slot(own_down, 2, "down")
    up_x, up_y = across(far_up, "up")
    blocks = [(k * rows_first, k + 1, rows_first) for k in range(3)]
    qkv_full, out_full, vec, proj, projt = first_whole(
        place,
        [near, diagonal, first, near_other, diagonal_other, first_other],
        near_segments(0, rows_first)
        + segments_of(2, far, blocks, half_first, 1, half_own, high_at + tall - half_own),
        fsdp,
        slots,
        width,
        proj_shape,
        entries,
    )
    q_front, q_rest, kv, kvp = make_qkv(front, rest, x, qkv_full, vec, proj)
    up_x, up_y, q_front, back_down = tie(up_x, up_y, q_front, back_down)
    far_down = all_of(*back_down)

    far = far_up.shape[0]
    half_up = far // 32 * 16
    blocks = [(k * rows_up, k + 1, rows_up) for k in range(3)]

    def far_diagonal(from_x, from_y, name):
        return [swap_fsdp(from_x[:half_up], 2, name), swap_fsdp(from_y[half_up:], 1, name)]

    def rest_segments(first):
        return near_segments(first, rows_up) + segments_of(2, far, blocks, half_up, 3, 0, half_up)

    up_diagonal = far_diagonal(up_x, up_y, "updiag")
    down_x, down_y = across(far_down, "down")
    up = all_of(far_up, up_x, up_y)
    up_other = swap_core(up, "up_core")
    a_front, a_rest = attend(q_front, q_rest, kvp)

    m1 = 3 * width
    m2 = m1 + width
    m3 = m2 + hidden
    m4 = m3 + width
    ends = [m4 + i * width for i in range(5)]
    marks_one = ((m1, m2), (ends[0], ends[1]), (ends[1], ends[2]))
    marks_two = ((m3, m4), (ends[2], ends[3]), (ends[3], ends[4]))

    def flat(v):
        return v.reshape(seqs * half, width)

    h_front, low_front, kept, lowt, lowt_give, attendedt, attendedt_give = join(
        place, flat(a_front), flat(front), out_full, vec, marks_one, True, slots
    )
    up_diagonal, up_other, low_front, lowt_give, attendedt_give, a_rest = tie(
        up_diagonal, up_other, low_front, lowt_give, attendedt_give, a_rest
    )
    up_diagonal = all_of(*up_diagonal)
    up_diagonal_other = swap_core(up_diagonal, "updiag_core")
    up_diagonal_other, down_x, down_y = tie(up_diagonal_other, down_x, down_y)
    down_diagonal = far_diagonal(down_x, down_y, "downdiag")
    down = all_of(far_down, down_x, down_y)
    down_other = swap_core(down, "down_core")
    lowt_came, attendedt_came = cores((lowt_give, attendedt_give), "given_core")
    up_full = up_whole(
        place,
        [near, diagonal, up, up_diagonal]
        + [near_other, diagonal_other, up_other, up_diagonal_other],
        rest_segments(rows_first),
        rows_up,
        fsdp,
        slots,
    )
    act_front, slope, act_give = lift(place, low_front, up_full, vec, m2, True, range(fsdp))
    down_diagonal, down_other, act_front, act_give, lowt_came, attendedt_came = tie(
        down_diagonal, down_other, act_front, act_give, lowt_came, attendedt_came
    )
    down_diagonal = all_of(*down_diagonal)
    down_diagonal_other = swap_core(down_diagonal, "downdiag_core")
    down_diagonal, down_diagonal_other, act_give = tie(
        down_diagonal, down_diagonal_other, act_give
    )
    act_came = swap_core(act_give, "given_core")
    down_full = down_whole(
        place,
        [near, diagonal, down, down_diagonal]
        + [near_other, diagonal_other, down_other, down_diagonal_other],
        rest_segments(rows_first + rows_up),
        rows_up,
        slots,
        hidden,
        width,
    )
    out_front, d_sum, d_low, d_lowt, two_sums = lower(
        [act_front], h_front, down_full, vec, marks_two, dy
    )

    def send(parts, name):
        send_x, stay_x, send_y, stay_y = parts
        return swap_fsdp(send_x, 1, name), swap_fsdp(send_y, 2, name), stay_x, stay_y

    def add_up(from_x, from_y, stay_x, stay_y):
        return second_stage(stay_x, from_x, stay_y, from_y)

    def forward(over_y, over_x, kept, name):
        return kept, swap_fsdp(over_y, 2, name), swap_fsdp(over_x, 1, name)

    def along_z(pieces, name):
        owns, parts = third_stage(*pieces)
        return owns, [shift_slot(a, k + 1, name) for k, a in enumerate(parts)]

    d_lowt_came = swap_core(d_lowt, "d_low_core")
    h_rest, low_rest = join(
        place, flat(a_rest), flat(rest), out_full, vec, marks_one, False, slots
    )
    d_lowt_came, act_came, low_rest, frontt_give, xt_give = tie(
        d_lowt_came, act_came, low_rest, frontt_give, xt_give
    )
    parts_down = grad_down(place, d_lowt, d_lowt_came, act_front, act_came, rows_up, slots)
    parts_down, d_low = tie(parts_down, d_low)
    sent_down = send(parts_down, "gdown")
    frontt_came, xt_came = cores((frontt_give, xt_give), "given_core")
    d_hidden, up_sums = hidden_back(d_low, down_full, slope)
    d_hidden_came = swap_core(d_hidden, "d_hidden_core")
    d_first, d_first_low, d_attended, sums = first_back(
        d_hidden, up_full, d_sum, kept, vec, out_full, up_sums, two_sums, (ends[0], ends[1])
    )
    d_attended = d_attended.reshape(seqs, half, width)
    grads = [attend_back(0, q_front, kvp, d_attended)]
    grads, d_first_low, sums, sent_down, kv, frontt_came, xt_came = tie(
        grads, d_first_low, sums, sent_down, kv, frontt_came, xt_came
    )
    over_down = forward(*add_up(*sent_down), "gdown2")
    d_first_low_came = swap_core(d_first_low, "d_low_core")
    grads_came = cores(grads, "d_qkv_core")
    kv_came = swap_core(kv, "given_core")
    for s in range(1, seqs):
        grads.append(attend_back(s, q_front, kvp, d_attended))
    parts_up = grad_up(place, lowt, lowt_came, d_hidden, d_hidden_came, fsdp, slots)
    grads, d_first_low_came, sums, grads_came, kv_came, parts_up, over_down = tie(
        grads, d_first_low_came, sums, grads_came, kv_came, parts_up, over_down
    )
    sent_up = send(parts_up, "gup")
    sums_came = swap_core(sums, "d_low_core")
    grads_came = grads_came + cores(grads[1:], "d_qkv_core")
    grads_came, sums_came = tie(grads_came, sums_came)
    owns_down, (one, two, three) = third_stage(over_down)
    two = shift_slot(two, 2, "gdown3")
    parts_first = grad_rest(
        place,
        (xt, xt_came, frontt, frontt_came, attendedt, attendedt_came),
        grads + grads_came,
        (d_first_low, d_first_low_came, kv, kv_came, sums, sums_came),
        projt,
        entries,
        fsdp,
        slots,
    )
    parts_first, low_rest, sent_up, one, two, three = tie(
        parts_first, low_rest, sent_up, one, two, three
    )
    three = shift_slot(three, 3, "gdown3")
    over_up = forward(*add_up(*sent_up), "gup2")
    act_rest = lift(place, low_rest, up_full, vec, m2, False, range(fsdp // 2))
    parts_first, act_rest, over_up, one, three, grads, low_rest = tie(
        parts_first, act_rest, over_up, one, three, grads, low_rest
    )
    sent_first = send(parts_first, "gfirst")
    last_down = (owns_down, (shift_slot(one, 1, "gdown3"), two, three))
    owns_up, (one, two, three) = third_stage(over_up)
    two, three = shift_slot(two, 2, "gup3"), shift_slot(three, 3, "gup3")
    act_rest += lift(place, low_rest, up_full, vec, m2, False, range(fsdp // 2, fsdp))
    out_rest = lower(act_rest, h_rest, down_full, vec, marks_two)[0]
    output = restore(
        out_front.reshape(seqs, half, width), out_rest.reshape(seqs, half, width), back
    ).reshape(rows, width)
    sent_first, output, grads, one, two, three, last_down = tie(
        sent_first, output, grads, one, two, three, last_down
    )
    over_first = forward(*add_up(*sent_first), "gfirst2")
    last_up = (owns_up, (shift_slot(one, 1, "gup3"), two, three))
    g_down, squares_down = last_stage(*last_down)
    over_first, squares_down, last_up, grads = tie(over_first, squares_down, last_up, grads)
    last_first = along_z((over_first,), "gfirst3")
    g_up, squares_up = last_stage(*last_up)
    grad_input = input_back(
        projt, d_first.reshape(seqs, half, width), qkv_full, back, grads
    ).reshape(rows, width)
    last_first, grad_input, squares_up = tie(last_first, grad_input, squares_up)
    g_first, squares_first = last_stage(*last_first)
    squares_rest = squares_up + squares_down
    squares = sum_everywhere(squares_first + squares_rest)
    states = (
        qkv_weight,
        qkv_moment,
        qkv_second,
        out_weight,
        out_moment,
        out_second,
        up_weight,
        up_moment,
        up_second,
        down_projection_weight.T,
        down_moment.T,
        down_second.T,
        proj_weight,
        proj_moment,
        proj_second,
        vec_weight,
        vec_moment,
        vec_second,
    )
    new = update(place, squares, g_first, g_up, g_down, states, rates)
    norm, new = new[0].reshape(()), list(new[1:])
    new[12:16] = [v.T for v in new[12:16]]
    return (output, grad_input, norm, *new)


def split_up(value, dim, peers):
    dims = value.shape
    blocks = value.reshape(*dims[:dim], peers, dims[dim] // peers, *dims[dim + 1 :])
    return jnp.moveaxis(blocks, dim, 0)


def sum_at_owner(value, axis, dim):
    blocks = split_up(value, dim, lax.axis_size(axis))
    arrived = lax.all_to_all(blocks, axis, split_axis=0, concat_axis=0, tiled=True)
    return arrived.astype(jnp.float32).sum(axis=0)


def side_by_side(arrays, axis, dim, along):
    ends, at = ([], 0)
    for a in arrays[:-1]:
        at += a.shape[along]
        ends.append(at)
    both = jnp.concatenate(arrays, axis=along)
    return tuple(jnp.split(sum_at_owner(both, axis, dim), ends, axis=along))


def layer_norm(summed, gains, shifts):
    average = jnp.mean(summed, axis=-1, keepdims=True)
    centered = summed - average
    variance = jnp.mean(centered * centered, axis=-1, keepdims=True)
    return centered * lax.rsqrt(variance + NORM_EPS) * gains + shifts


def norm_back(summed, gains, shifts, grad_out):
    result, pullback = jax.vjp(layer_norm, summed, gains, shifts)
    return pullback(grad_out)


def gelu_exact(values):
    return jax.nn.gelu(values, approximate=False)


def split_vector(vec_full, model_width, hidden_width):
    mark_one = 3 * model_width
    mark_two = mark_one + model_width
    mark_three = mark_two + hidden_width
    mark_four = mark_three + model_width
    return (
        vec_full[:mark_one],
        vec_full[mark_one:mark_two],
        vec_full[mark_two:mark_three],
        vec_full[mark_three:mark_four],
        vec_full[mark_four : mark_four + model_width],
        vec_full[mark_four + model_width : mark_four + 2 * model_width],
        vec_full[mark_four + 2 * model_width : mark_four + 3 * model_width],
        vec_full[mark_four + 3 * model_width : mark_four + 4 * model_width],
    )


def adam_update(weight, moment, second, grad, scale_clip, rate, decay):
    clipped = grad * scale_clip
    new_moment = BETA_ONE * moment + (1.0 - BETA_ONE) * clipped
    new_second = BETA_TWO * second + (1.0 - BETA_TWO) * clipped * clipped
    moment_hat = new_moment / (1.0 - BETA_ONE**STEP)
    second_hat = new_second / (1.0 - BETA_TWO**STEP)
    new_weight = weight - rate * (moment_hat / (jnp.sqrt(second_hat) + ADAM_EPS) + decay * weight)
    return (new_weight, new_moment, new_second, new_weight.astype(jnp.bfloat16))


def fetch_whole(low_qkv, low_out, low_up, low_down, low_proj, low_vec):
    rows = (
        lax.all_gather(low_qkv, "dp", axis=0, tiled=True),
        lax.all_gather(low_out, "dp", axis=0, tiled=True),
        lax.all_gather(low_up, "dp", axis=0, tiled=True),
        lax.all_gather(low_down, "dp", axis=0, tiled=True),
        lax.all_gather(low_proj, "dp", axis=1, tiled=True),
        lax.all_gather(low_vec, "dp", axis=0, tiled=True),
    )
    return (
        lax.all_gather(rows[0], "fsdp", axis=1, tiled=True),
        lax.all_gather(rows[1], "fsdp", axis=1, tiled=True),
        lax.all_gather(rows[2], "fsdp", axis=1, tiled=True),
        lax.all_gather(rows[3], "fsdp", axis=1, tiled=True),
        lax.all_gather(rows[4], "fsdp", axis=0, tiled=True),
        lax.all_gather(rows[5], "fsdp", axis=0, tiled=True),
    )


def on_any_mesh(
    tokens,
    cotangent,
    positions,
    counts,
    qkv_weight,
    qkv_moment,
    qkv_second,
    out_weight,
    out_moment,
    out_second,
    up_weight,
    up_moment,
    up_second,
    down_projection_weight,
    down_moment,
    down_second,
    proj_weight,
    proj_moment,
    proj_second,
    vec_weight,
    vec_moment,
    vec_second,
):
    low_qkv = qkv_weight.astype(jnp.bfloat16)
    low_out = out_weight.astype(jnp.bfloat16)
    low_up = up_weight.astype(jnp.bfloat16)
    low_down = down_projection_weight.astype(jnp.bfloat16)
    low_proj = proj_weight.astype(jnp.bfloat16)
    low_vec = vec_weight.astype(jnp.bfloat16)
    qkv_full, out_full, up_full, down_full, projection_gathered, vec_full = fetch_whole(
        low_qkv, low_out, low_up, low_down, low_proj, low_vec
    )
    seq_count = counts.shape[0]
    row_count = tokens.shape[0]
    seq_length = row_count // seq_count
    model_width = tokens.shape[1]
    head_width = model_width // HEADS
    hidden_width = vec_full.shape[0] - 9 * model_width
    proj_rows = projection_gathered.shape[0]
    score_scale = head_width ** (-0.5)
    bias_qkv, bias_out, bias_up, bias_down, gain_one, shift_one, gain_two, shift_two = split_vector(
        vec_full.astype(jnp.float32), model_width, hidden_width
    )
    pre_qkv = jnp.dot(tokens, qkv_full, preferred_element_type=jnp.float32)
    qkv_low = (pre_qkv + bias_qkv).astype(jnp.bfloat16)
    queries = qkv_low[:, :model_width].reshape(seq_count, seq_length, HEADS, head_width)
    key_value_pair = qkv_low[:, model_width:].reshape(seq_count, seq_length, 2 * model_width)
    projected = jnp.einsum(
        "bu,vur->vbr", projection_gathered, key_value_pair, preferred_element_type=jnp.float32
    ).astype(jnp.bfloat16)
    key_heads = projected[:, :, :model_width].reshape(seq_count, proj_rows, HEADS, head_width)
    value_heads = projected[:, :, model_width:].reshape(seq_count, proj_rows, HEADS, head_width)
    scores = (
        jnp.einsum("slhe,sjhe->shlj", queries, key_heads, preferred_element_type=jnp.float32)
        * score_scale
    )
    peak = jnp.max(scores, axis=-1, keepdims=True)
    log_total = peak + jnp.log(jnp.sum(jnp.exp(scores - peak), axis=-1, keepdims=True))
    soft_low = jnp.exp(scores - log_total).astype(jnp.bfloat16)
    context = jnp.einsum(
        "shlj,sjhe->slhe", soft_low, value_heads, preferred_element_type=jnp.float32
    )
    attended = context.reshape(row_count, model_width).astype(jnp.bfloat16)
    first_sum = (
        tokens.astype(jnp.float32)
        + jnp.dot(attended, out_full, preferred_element_type=jnp.float32)
        + bias_out
    )
    normed_one = layer_norm(first_sum, gain_one, shift_one)
    normed_low = normed_one.astype(jnp.bfloat16)
    hidden_pre = jnp.dot(normed_low, up_full, preferred_element_type=jnp.float32) + bias_up
    active = gelu_exact(hidden_pre).astype(jnp.bfloat16)
    second_sum = (
        normed_one + jnp.dot(active, down_full, preferred_element_type=jnp.float32) + bias_down
    )
    output = layer_norm(second_sum, gain_two, shift_two).astype(jnp.bfloat16)
    slot_live = jnp.arange(positions.shape[1], dtype=jnp.int32)[None, :] < counts[:, None]
    one_hot_rows = (
        (positions[:, :, None] == jnp.arange(seq_length, dtype=jnp.int32)[None, None, :])
        & slot_live[:, :, None]
    ).astype(jnp.bfloat16)
    dense = jnp.einsum(
        "bej,bef->bjf", one_hot_rows, cotangent, preferred_element_type=jnp.float32
    ).reshape(row_count, model_width)
    qkv_full, out_full, up_full, down_full, projection_gathered, vec_full = fetch_whole(
        low_qkv, low_out, low_up, low_down, low_proj, low_vec
    )
    d_second, d_gain_two, d_shift_two = norm_back(second_sum, gain_two, shift_two, dense)
    d_bias_down = jnp.sum(d_second, axis=0)
    d_second_low = d_second.astype(jnp.bfloat16)
    grad_down = jnp.einsum("rf,rd->fd", active, d_second_low, preferred_element_type=jnp.float32)
    d_active = jnp.einsum("rd,fd->rf", d_second_low, down_full, preferred_element_type=jnp.float32)
    gelu_value, gelu_pull = jax.vjp(gelu_exact, hidden_pre)
    d_hidden = gelu_pull(d_active)[0]
    d_bias_up = jnp.sum(d_hidden, axis=0)
    d_hidden_low = d_hidden.astype(jnp.bfloat16)
    grad_up = jnp.einsum("rd,rf->df", normed_low, d_hidden_low, preferred_element_type=jnp.float32)
    d_normed = d_second + jnp.einsum(
        "rf,df->rd", d_hidden_low, up_full, preferred_element_type=jnp.float32
    )
    d_first, d_gain_one, d_shift_one = norm_back(first_sum, gain_one, shift_one, d_normed)
    d_bias_out = jnp.sum(d_first, axis=0)
    d_first_low = d_first.astype(jnp.bfloat16)
    grad_out = jnp.einsum("rd,re->de", attended, d_first_low, preferred_element_type=jnp.float32)
    d_attended = jnp.einsum("re,de->rd", d_first_low, out_full, preferred_element_type=jnp.float32)
    d_attended = d_attended.astype(jnp.bfloat16).reshape(seq_count, seq_length, HEADS, head_width)
    scores_again = (
        jnp.einsum("slhe,sjhe->shlj", queries, key_heads, preferred_element_type=jnp.float32)
        * score_scale
    )
    probs_again = jnp.exp(scores_again - log_total)
    probs_low = probs_again.astype(jnp.bfloat16)
    d_value_heads = jnp.einsum(
        "shlj,slhe->sjhe", probs_low, d_attended, preferred_element_type=jnp.float32
    )
    d_probs = jnp.einsum(
        "slhe,sjhe->shlj", d_attended, value_heads, preferred_element_type=jnp.float32
    )
    d_scores = probs_again * (d_probs - jnp.sum(probs_again * d_probs, axis=-1, keepdims=True))
    d_raw_low = (d_scores * score_scale).astype(jnp.bfloat16)
    d_queries = jnp.einsum(
        "shlj,sjhe->slhe", d_raw_low, key_heads, preferred_element_type=jnp.float32
    ).reshape(row_count, model_width)
    d_key_heads = jnp.einsum(
        "shlj,slhe->sjhe", d_raw_low, queries, preferred_element_type=jnp.float32
    )
    projected_gradient = jnp.concatenate(
        [
            d_key_heads.reshape(seq_count, proj_rows, model_width),
            d_value_heads.reshape(seq_count, proj_rows, model_width),
        ],
        axis=-1,
    ).astype(jnp.bfloat16)
    d_kv = jnp.einsum(
        "cq,uct->uqt", projection_gathered, projected_gradient, preferred_element_type=jnp.float32
    ).reshape(row_count, 2 * model_width)
    projection_gradient = jnp.einsum(
        "nhy,nxy->hx", projected_gradient, key_value_pair, preferred_element_type=jnp.float32
    )
    d_qkv = jnp.concatenate([d_queries, d_kv], axis=-1)
    d_bias_qkv = jnp.sum(d_qkv, axis=0)
    d_qkv_low = d_qkv.astype(jnp.bfloat16)
    grad_qkv = jnp.einsum("rd,re->de", tokens, d_qkv_low, preferred_element_type=jnp.float32)
    grad_input = (
        d_first + jnp.einsum("re,de->rd", d_qkv_low, qkv_full, preferred_element_type=jnp.float32)
    ).astype(jnp.bfloat16)
    grad_vec = jnp.concatenate(
        [
            d_bias_qkv,
            d_bias_out,
            d_bias_up,
            d_bias_down,
            d_gain_one,
            d_shift_one,
            d_gain_two,
            d_shift_two,
        ]
    )
    col_part = (
        lax.psum_scatter(
            grad_qkv.astype(jnp.bfloat16), "fsdp", scatter_dimension=1, tiled=True
        ).astype(jnp.float32),
        lax.psum_scatter(
            grad_out.astype(jnp.bfloat16), "fsdp", scatter_dimension=1, tiled=True
        ).astype(jnp.float32),
        lax.psum_scatter(
            grad_up.astype(jnp.bfloat16), "fsdp", scatter_dimension=1, tiled=True
        ).astype(jnp.float32),
        lax.psum_scatter(
            grad_down.astype(jnp.bfloat16), "fsdp", scatter_dimension=1, tiled=True
        ).astype(jnp.float32),
        lax.psum_scatter(
            projection_gradient.astype(jnp.bfloat16), "fsdp", scatter_dimension=0, tiled=True
        ).astype(jnp.float32),
        lax.psum_scatter(
            grad_vec.astype(jnp.bfloat16), "fsdp", scatter_dimension=0, tiled=True
        ).astype(jnp.float32),
    )
    owned = (
        *side_by_side(
            (
                col_part[0].astype(jnp.bfloat16),
                col_part[1].astype(jnp.bfloat16),
                col_part[2].astype(jnp.bfloat16),
            ),
            "dp",
            0,
            1,
        ),
        sum_at_owner(col_part[3].astype(jnp.bfloat16), "dp", 0),
        sum_at_owner(col_part[4].astype(jnp.bfloat16), "dp", 1),
        sum_at_owner(col_part[5].astype(jnp.bfloat16), "dp", 0),
    )
    owned_qkv, owned_out, owned_up, owned_down, owned_proj, owned_vec = owned
    local_squares = (
        jnp.sum(owned_qkv * owned_qkv)
        + jnp.sum(owned_out * owned_out)
        + jnp.sum(owned_up * owned_up)
        + jnp.sum(owned_down * owned_down)
        + jnp.sum(owned_proj * owned_proj)
        + jnp.sum(owned_vec * owned_vec)
    )
    all_squares = lax.psum(local_squares, ("fsdp", "dp"))
    grad_norm = jnp.sqrt(all_squares)
    scale_clip = jnp.minimum(1.0, CLIP_NORM / grad_norm)
    qkv_parts = adam_update(
        qkv_weight, qkv_moment, qkv_second, owned_qkv, scale_clip, RATE_QKV, DECAY_RATE
    )
    out_parts = adam_update(
        out_weight, out_moment, out_second, owned_out, scale_clip, RATE_OUT, DECAY_RATE
    )
    up_parts = adam_update(
        up_weight, up_moment, up_second, owned_up, scale_clip, RATE_UP, DECAY_RATE
    )
    down_parts = adam_update(
        down_projection_weight,
        down_moment,
        down_second,
        owned_down,
        scale_clip,
        RATE_DOWN,
        DECAY_RATE,
    )
    proj_parts = adam_update(
        proj_weight, proj_moment, proj_second, owned_proj, scale_clip, RATE_PROJ, DECAY_RATE
    )
    vec_parts = adam_update(
        vec_weight, vec_moment, vec_second, owned_vec, scale_clip, RATE_VEC, 0.0
    )
    return (
        output,
        grad_input,
        grad_norm,
        qkv_parts[0],
        qkv_parts[1],
        qkv_parts[2],
        qkv_parts[3],
        out_parts[0],
        out_parts[1],
        out_parts[2],
        out_parts[3],
        up_parts[0],
        up_parts[1],
        up_parts[2],
        up_parts[3],
        down_parts[0],
        down_parts[1],
        down_parts[2],
        down_parts[3],
        proj_parts[0],
        proj_parts[1],
        proj_parts[2],
        proj_parts[3],
        vec_parts[0],
        vec_parts[1],
        vec_parts[2],
        vec_parts[3],
    )


def solution(mesh):
    matrix = P("dp", "fsdp")
    tall = P("fsdp", "dp")
    every = P(("fsdp", "dp"))
    small = mesh.shape["fsdp"] == 4 and mesh.shape["dp"] == 8
    return jax.shard_map(
        on_device if small else on_any_mesh,
        mesh=mesh,
        in_specs=(every,) * 4 + (matrix,) * 12 + (tall,) * 3 + (every,) * 3,
        out_specs=(every, every, P()) + (matrix,) * 16 + (tall,) * 4 + (every,) * 4,
        check_vma=False,
    )
```
